32 devices in a mesh: dev: 32 (over z, y, x, core).
Axes of the slice: x: 2, y: 2, z: 4, core: 2. Of those that a mesh axis runs over, the one named last changes fastest.
Arguments:
- tokens: bfloat16 [32768, 1024], P('dev'), may hold values from -6 to 6
- segment_ids: int32 [32768], replicated, may hold values from -1 to 52, as said below
- first_gain: float32 [1024], P('dev'), may hold values from 0.5 to 1.5
- first_bias: float32 [1024], P('dev'), may hold values from -1.75 to 1.75
- qkv_weight: float32 [1024, 3072], P('dev'), may hold values from -0.1875 to 0.1875
- query_bias: float32 [1024], P('dev'), may hold values from -1.75 to 1.75
- value_bias: float32 [1024], P('dev'), may hold values from -1.75 to 1.75
- out_weight: float32 [1024, 1024], P('dev'), may hold values from -1.5 to 1.5
- out_bias: float32 [1024], P('dev'), may hold values from -1.75 to 1.75
- second_gain: float32 [1024], P('dev'), may hold values from 0.5 to 1.5
- second_bias: float32 [1024], P('dev'), may hold values from -1.75 to 1.75
- hidden_weight: float32 [1024, 4096], P('dev'), may hold values from -0.1875 to 0.1875
- hidden_bias: float32 [4096], P('dev'), may hold values from -1.75 to 1.75
- final_weight: float32 [4096, 1024], P('dev'), may hold values from -0.09375 to 0.09375
- final_bias: float32 [1024], P('dev'), may hold values from -1.75 to 1.75
- cotangent: bfloat16 [32768, 1024], P('dev'), may hold values from -6 to 6
Outputs:
- block_output: bfloat16 [32768, 1024], P('dev')
- input_grad: bfloat16 [32768, 1024], P('dev')
- first_gain_grad: float32 [1024], P('dev')
- first_bias_grad: float32 [1024], P('dev')
- qkv_weight_grad: float32 [1024, 3072], P('dev')
- query_bias_grad: float32 [1024], P('dev')
- value_bias_grad: float32 [1024], P('dev')
- out_weight_grad: float32 [1024, 1024], P('dev')
- out_bias_grad: float32 [1024], P('dev')
- second_gain_grad: float32 [1024], P('dev')
- second_bias_grad: float32 [1024], P('dev')
- hidden_weight_grad: float32 [1024, 4096], P('dev')
- hidden_bias_grad: float32 [4096], P('dev')
- final_weight_grad: float32 [4096, 1024], P('dev')
- final_bias_grad: float32 [1024], P('dev')
The draws below stay inside these ranges and needn't reach their ends.
Inputs may be any that keep to these rules, and one draw needn't show every extreme that they name: `segment_ids`: every image is a run of exactly 577 consecutive token slots, numbered 0, 1, ... in order along the slots, every number present once; all slots outside images are -1, in gaps of random length before, between and after images.
All inputs are finite; a program needn't handle non-finite values.
Results may differ from the reference program's by a relative error of at most 0.012.
The reference program's roundings to bfloat16 on the way count: a program that leaves them out, or rounds other values in their place, can miss the bound.
Values may be sent and summed in bfloat16 or wider, within the bound.
No kernel may reach another device: no remote copies, remote signals or barrier semaphores. Data moves between devices by JAX's collectives and lax.ppermute only.
A program may use at most 256 MiB of HBM per device.

```python
import math
import jax
import jax.numpy as jnp
from jax import lax

D = 1024
HEADS = 16
HEAD = 64
FF = 4096
IMG = 577
TOKENS = 32768
IMAGES = 53


def draw_segment_ids(key, part):
    key = jax.random.fold_in(key, 7)
    padding = TOKENS - IMAGES * IMG
    offsets = jax.random.randint(key, (IMAGES,), 0, padding + 1, dtype=jnp.int32)
    starts = jnp.sort(offsets) + jnp.arange(IMAGES, dtype=jnp.int32) * IMG
    places = jnp.arange(TOKENS, dtype=jnp.int32)
    owning = jnp.searchsorted(starts, places, side='right').astype(jnp.int32) - 1
    begins_at = starts[jnp.maximum(owning, 0)]
    inside = (owning >= 0) & (places < begins_at + IMG)
    return jnp.where(inside, owning, -1).astype(jnp.int32)


def shard_levels(rng, shape, pieces, least, largest):
    factor_of, own = 1.0, jax.random.fold_in(rng, 6)
    for position, parts in pieces:
        draws = jnp.exp(jax.random.uniform(jax.random.fold_in(own, position), (parts,), jnp.float32, least / len(pieces), largest / len(pieces)))
        factor_of = factor_of * jnp.repeat(draws, shape[position] // parts).reshape([-1 if axis == position else 1 for axis in range(len(shape))])
    return factor_of


def centred(own_key, dims, width, most, shards=(), kind=jnp.bfloat16):
    factor_of = shard_levels(own_key, dims, shards, -0.22, 0.18) if shards else 1.0
    result = jax.random.normal(own_key, dims, jnp.float32) * width * factor_of
    return jnp.minimum(jnp.maximum(result, -most), most).astype(kind)


def setup_inputs(seed: int = 0) -> dict:
    key_list = jax.random.split(jax.random.key(seed), 17)
    return {
        "tokens": centred(key_list[0], (TOKENS, D), 1.0, 6.0, ((0, 32),)),
        "segment_ids": draw_segment_ids(jax.random.fold_in(key_list[16], 71), 0),
        "first_gain": jnp.clip(1.0 + 0.1 * jax.random.normal(key_list[2], (D,), jnp.float32), 0.5, 1.5),
        "first_bias": centred(key_list[3], (D,), 0.3, 1.75, ((0, 32),), jnp.float32),
        "qkv_weight": centred(key_list[4], (D, 3 * D), D ** -0.5, 0.1875, ((0, 32),), jnp.float32),
        "query_bias": centred(key_list[5], (D,), 0.3, 1.75, ((0, 32),), jnp.float32),
        "value_bias": centred(key_list[6], (D,), 0.3, 1.75, ((0, 32),), jnp.float32),
        "out_weight": centred(key_list[7], (D, D), (D // 64) ** -0.5, 1.5, ((0, 32),), jnp.float32),
        "out_bias": centred(key_list[8], (D,), 0.3, 1.75, ((0, 32),), jnp.float32),
        "second_gain": jnp.clip(1.0 + 0.1 * jax.random.normal(key_list[9], (D,), jnp.float32), 0.5, 1.5),
        "second_bias": centred(key_list[10], (D,), 0.3, 1.75, ((0, 32),), jnp.float32),
        "hidden_weight": centred(key_list[11], (D, FF), D ** -0.5, 0.1875, ((0, 32),), jnp.float32),
        "hidden_bias": centred(key_list[12], (FF,), 0.3, 1.75, ((0, 32),), jnp.float32),
        "final_weight": centred(key_list[13], (FF, D), FF ** -0.5, 0.09375, ((0, 32),), jnp.float32),
        "final_bias": centred(key_list[14], (D,), 0.3, 1.75, ((0, 32),), jnp.float32),
        "cotangent": centred(key_list[15], (TOKENS, D), 1.0, 6.0, ((0, 32),)),
    }


highest = lax.Precision.HIGHEST
norm_epsilon = 1e-06

@jax.custom_vjp
def low(v):
    return lax.optimization_barrier(v.astype(jnp.bfloat16)).astype(jnp.float32)

@jax.custom_vjp
def low_back(v):
    return v

def low_keep(v):
    return (low(v), None)

def low_pass(kept, grad):
    return (grad,)

def back_keep(v):
    return (v, None)

def back_low(kept, grad):
    return (low(grad),)
low.defvjp(low_keep, low_pass)
low_back.defvjp(back_keep, back_low)

def layer_norm(values, gain, bias):
    center = values - lax.optimization_barrier(jnp.mean(values, axis=-1, keepdims=True))
    spread = lax.optimization_barrier(jnp.mean(center * center, axis=-1, keepdims=True))
    return center * lax.rsqrt(spread + norm_epsilon) * gain + bias

def attention(queries, key_rows, value_rows, segments):
    block_rows = math.gcd(TOKENS, 512)
    reach_rows = IMG - 1
    window = block_rows + 2 * reach_rows
    keys_padded = jnp.pad(key_rows, ((reach_rows, reach_rows), (0, 0), (0, 0)))
    values_padded = jnp.pad(value_rows, ((reach_rows, reach_rows), (0, 0), (0, 0)))
    segments_padded = jnp.pad(segments, (reach_rows, reach_rows), constant_values=-2)
    columns = jnp.arange(window, dtype=jnp.int32)
    diagonal = jnp.arange(block_rows, dtype=jnp.int32)[:, None] + reach_rows == columns[None, :]

    def one_block(offset):
        query_block = lax.dynamic_slice_in_dim(queries, offset, block_rows, 0)
        key_block = lax.dynamic_slice_in_dim(keys_padded, offset, window, 0)
        value_block = lax.dynamic_slice_in_dim(values_padded, offset, window, 0)
        query_ids = lax.dynamic_slice_in_dim(segments, offset, block_rows, 0)
        key_ids = lax.dynamic_slice_in_dim(segments_padded, offset, window, 0)
        allowed = (query_ids[:, None] == key_ids[None, :]) & (query_ids[:, None] >= 0) | diagonal
        scores = low_back(jnp.einsum('qhd,khd->hqk', query_block, key_block, precision=highest)) * 0.125
        scores = jnp.where(allowed[None], scores, -1e+30)
        maximum = lax.optimization_barrier(jnp.max(scores, axis=-1, keepdims=True))
        exponent = jnp.exp(scores - maximum)
        softmax_out = exponent / lax.optimization_barrier(jnp.sum(exponent, axis=-1, keepdims=True))
        return jnp.einsum('hqk,khd->qhd', low(softmax_out), value_block, precision=highest)
    offsets = jnp.arange(TOKENS // block_rows, dtype=jnp.int32) * block_rows
    blocks = lax.map(jax.checkpoint(one_block), offsets)
    return blocks.reshape(TOKENS, HEADS * HEAD)

def forward(inputs, segments, first_gain, first_bias, qkv_weight, query_bias, value_bias, out_weight, out_bias, second_gain, second_bias, hidden_weight, hidden_bias, final_weight, final_bias):
    first_gain, first_bias = (low(first_gain), low(first_bias))
    qkv_weight, query_bias, value_bias = (low(qkv_weight), low(query_bias), low(value_bias))
    out_weight, out_bias = (low(out_weight), low(out_bias))
    second_gain, second_bias = (low(second_gain), low(second_bias))
    hidden_weight, hidden_bias = (low(hidden_weight), low(hidden_bias))
    final_weight, final_bias = (low(final_weight), low(final_bias))
    normed_one = low(layer_norm(inputs, first_gain, first_bias))
    packed = jnp.dot(normed_one, qkv_weight, precision=highest)
    queries = low_back(low(packed[:, :D] + query_bias))
    key_rows = low_back(low(packed[:, D:2 * D]))
    value_rows = low_back(low(packed[:, 2 * D:] + value_bias))
    shape_heads = (TOKENS, HEADS, HEAD)
    mixed_heads = attention(queries.reshape(shape_heads), key_rows.reshape(shape_heads), value_rows.reshape(shape_heads), segments)
    mixed_heads = low_back(low(mixed_heads))
    middle = inputs + low_back(jnp.dot(mixed_heads, out_weight, precision=highest) + out_bias)
    normed_two = low(layer_norm(middle, second_gain, second_bias))
    hidden_pre = low_back(jnp.dot(normed_two, hidden_weight, precision=highest) + hidden_bias)
    activated = low(jax.nn.gelu(hidden_pre, approximate=False))
    return middle + jnp.dot(activated, final_weight, precision=highest) + final_bias

def reference(tokens, segment_ids, first_gain, first_bias, qkv_weight, query_bias, value_bias, out_weight, out_bias, second_gain, second_bias, hidden_weight, hidden_bias, final_weight, final_bias, cotangent):

    def wrapped(inputs, *weights):
        return forward(inputs, segment_ids, *weights)
    output, pullback = jax.vjp(wrapped, tokens.astype(jnp.float32), first_gain, first_bias, qkv_weight, query_bias, value_bias, out_weight, out_bias, second_gain, second_bias, hidden_weight, hidden_bias, final_weight, final_bias)
    gradients = pullback(cotangent.astype(jnp.float32))
    return (output.astype(jnp.bfloat16), gradients[0].astype(jnp.bfloat16), gradients[1], gradients[2], gradients[3], gradients[4], gradients[5], gradients[6], gradients[7], gradients[8], gradients[9], gradients[10], gradients[11], gradients[12], gradients[13])
```

```python
import functools
import math

import jax
import jax.numpy as jnp
from jax import lax
from jax.experimental import pallas as pl
from jax.experimental.pallas import tpu as pltpu
from jax.sharding import PartitionSpec as P

IMG = 577
REACH = IMG - 1
HEAD = 64
SPAN = 592
LANES = 128
QB = 256
PP = 2
PIECES = 32
VMEM = 60 * 1024 * 1024
f32 = jnp.float32
bf16 = jnp.bfloat16

norm_epsilon = 1e-06

def make_items(img_ref, items_ref, blocks, images):
    count = jnp.int32(0)
    for b in range(blocks):
        for i in range(images):
            start = img_ref[i]
            low = b * QB + REACH
            hit = (start < low + QB) & (start + IMG > low)

            @pl.when(hit)
            def _():
                items_ref[count] = b * 8 + i

            count = count + hit.astype(jnp.int32)
    return count

def item_scalars(img_ref, items_ref, n):
    code = items_ref[n]
    b = code // 8
    start = img_ref[code % 8]
    begin = pl.multiple_of((start // 16) * 16, 16)
    row = pl.multiple_of(b * QB, QB)
    return b, start, begin, row

def halves(x):
    lane = lax.broadcasted_iota(jnp.int32, x.shape, 1)
    zero = jnp.zeros_like(x)
    return jnp.concatenate([jnp.where(lane < HEAD, x, zero), jnp.where(lane >= HEAD, x, zero)], axis=0)

def key_valid(start, begin):
    r = lax.broadcasted_iota(jnp.int32, (SPAN, 1), 0) + (begin - start)
    return (r >= 0) & (r < IMG)

def query_valid(start, row):
    lane = lax.broadcasted_iota(jnp.int32, (1, 2 * QB), 1)
    pos = jnp.where(lane < QB, lane, lane - QB) + (row + REACH - start)
    return (pos >= 0) & (pos < IMG)

def pad_rows(img_ref, images, rows):
    r = lax.broadcasted_iota(jnp.int32, (rows, LANES), 0) + REACH
    inside = jnp.zeros((rows, LANES), jnp.bool_)
    for i in range(images):
        start = img_ref[i]
        inside = inside | ((r >= start) & (r < start + IMG))
    return ~inside

def fwd_kernel(blocks, images, img_ref, q_ref, k_ref, v_ref, o_ref, lse_ref, acc, items):
    rows = blocks * QB
    count = make_items(img_ref, items, blocks, images)
    acc[...] = jnp.zeros_like(acc)
    lse_ref[...] = jnp.zeros_like(lse_ref)

    def body(n, carry):
        b, start, begin, row = item_scalars(img_ref, items, n)
        valid = key_valid(start, begin)
        qm = query_valid(start, row)
        done = []
        for u in range(PP):
            cols = slice(u * LANES, (u + 1) * LANES)
            q2 = halves(q_ref[pl.ds(row, QB), cols])
            kw = k_ref[pl.ds(begin, SPAN), cols]
            vw = v_ref[pl.ds(begin, SPAN), cols]
            s = lax.dot_general(kw, q2, (((1,), (1,)), ((), ())), preferred_element_type=f32)
            s = jnp.where(valid, s, -1e30)
            m = jnp.max(s, axis=0, keepdims=True)
            e = jnp.exp(s - m)
            l = jnp.sum(e, axis=0, keepdims=True)
            p = (e * jnp.where(qm, 1.0 / l, 0.0)).astype(bf16)
            ot = lax.dot_general(vw, p, (((0,), (0,)), ((), ())), preferred_element_type=f32)
            done.append((jnp.concatenate([ot[:HEAD, :QB], ot[HEAD:, QB:]], axis=0).T, m + jnp.log(l)))
        for u in range(PP):
            cols = slice(u * LANES, (u + 1) * LANES)
            o, total = done[u]
            acc[pl.ds(row, QB), cols] += o
            old = lse_ref[u, pl.ds(b, 1), :]
            lse_ref[u, pl.ds(b, 1), :] = jnp.where(qm, total, old)
        return carry

    lax.fori_loop(0, count, body, 0)
    pad = pad_rows(img_ref, images, rows)
    for u in range(PP):
        cols = slice(u * LANES, (u + 1) * LANES)
        own = v_ref[pl.ds(REACH, rows), cols].astype(f32)
        o_ref[:, cols] = jnp.where(pad, own, acc[:, cols]).astype(bf16)

def attention_forward(img, q, k, v, first, pairs):
    rows, width = q.shape
    win = k.shape[0]
    blocks = rows // QB
    images = img.shape[0]
    spec = lambda r: pl.BlockSpec((r, PP * LANES), lambda p, *_: (0, first // PP + p))
    return pl.pallas_call(
        functools.partial(fwd_kernel, blocks, images),
        grid_spec=pltpu.PrefetchScalarGridSpec(
            num_scalar_prefetch=1,
            grid=(pairs // PP,),
            in_specs=[spec(rows), spec(win), spec(win)],
            out_specs=[
                pl.BlockSpec((rows, PP * LANES), lambda p, *_: (0, p)),
                pl.BlockSpec((PP, blocks, 2 * QB), lambda p, *_: (p, 0, 0)),
            ],
            scratch_shapes=[pltpu.VMEM((rows, PP * LANES), f32), pltpu.SMEM((blocks * images,), jnp.int32)],
        ),
        out_shape=[
            jax.ShapeDtypeStruct((rows, pairs * LANES), bf16),
            jax.ShapeDtypeStruct((pairs, blocks, 2 * QB), f32),
        ],
        compiler_params=pltpu.CompilerParams(vmem_limit_bytes=VMEM, dimension_semantics=("arbitrary",)),
        cost_estimate=pl.CostEstimate(flops=pairs * 4 * 1300 * SPAN * 256, bytes_accessed=pairs * 2 * LANES * (2 * rows + 2 * win), transcendentals=pairs * 2 * 1300 * SPAN),
        name="attention_forward",
    )(img, q, k, v)

def bwd_kernel(blocks, images, img_ref, q_ref, k_ref, v_ref, g_ref, lse_ref,
               dq_ref, dk_ref, dv_ref, left_ref, right_ref, dq_acc, dk_acc, dv_acc, items):
    rows = blocks * QB
    count = make_items(img_ref, items, blocks, images)
    dq_acc[...] = jnp.zeros_like(dq_acc)
    dk_acc[...] = jnp.zeros_like(dk_acc)
    dv_acc[...] = jnp.zeros_like(dv_acc)

    def body(n, carry):
        b, start, begin, row = item_scalars(img_ref, items, n)
        valid = key_valid(start, begin)
        qm = query_valid(start, row)
        done = []
        for u in range(PP):
            cols = slice(u * LANES, (u + 1) * LANES)
            q2 = halves(q_ref[pl.ds(row, QB), cols])
            g2 = halves(g_ref[pl.ds(row, QB), cols])
            kw = k_ref[pl.ds(begin, SPAN), cols]
            vw = v_ref[pl.ds(begin, SPAN), cols]
            lse = jnp.where(qm, lse_ref[u, pl.ds(b, 1), :], 1e30)
            s = lax.dot_general(kw, q2, (((1,), (1,)), ((), ())), preferred_element_type=f32)
            dp = lax.dot_general(vw, g2, (((1,), (1,)), ((), ())), preferred_element_type=f32)
            p = jnp.exp(jnp.where(valid, s, -1e30) - lse)
            inner = jnp.sum(p * dp, axis=0, keepdims=True)
            ds = (p * (dp - inner)).astype(bf16)
            dv = jnp.dot(p.astype(bf16), g2, preferred_element_type=f32)
            dk = jnp.dot(ds, q2, preferred_element_type=f32)
            dqt = lax.dot_general(kw, ds, (((0,), (0,)), ((), ())), preferred_element_type=f32)
            done.append((dv, dk, jnp.concatenate([dqt[:HEAD, :QB], dqt[HEAD:, QB:]], axis=0).T))
        for u in range(PP):
            cols = slice(u * LANES, (u + 1) * LANES)
            dv, dk, dq = done[u]
            dv_acc[pl.ds(begin, SPAN), cols] += dv
            dk_acc[pl.ds(begin, SPAN), cols] += dk
            dq_acc[pl.ds(row, QB), cols] += dq
        return carry

    lax.fori_loop(0, count, body, 0)
    pad = pad_rows(img_ref, images, rows)
    dq_ref[...] = (dq_acc[...] * 0.125).astype(bf16)
    dk_ref[...] = dk_acc[pl.ds(REACH, rows), :]
    for u in range(PP):
        cols = slice(u * LANES, (u + 1) * LANES)
        dv_ref[:, cols] = dv_acc[pl.ds(REACH, rows), cols] + jnp.where(pad, g_ref[:, cols].astype(f32), 0.0)
    left_ref[0] = dk_acc[pl.ds(0, REACH), :].astype(bf16)
    left_ref[1] = dv_acc[pl.ds(0, REACH), :].astype(bf16)
    right_ref[0] = dk_acc[pl.ds(REACH + rows, REACH), :].astype(bf16)
    right_ref[1] = dv_acc[pl.ds(REACH + rows, REACH), :].astype(bf16)

def attention_backward(img, q, k, v, g, lse, first, pairs):
    rows, width = q.shape
    win = k.shape[0]
    blocks = rows // QB
    images = img.shape[0]
    C = PP * LANES
    spec = lambda r: pl.BlockSpec((r, C), lambda p, *_: (0, first // PP + p))
    out = lambda r: pl.BlockSpec((r, C), lambda p, *_: (0, p))
    edge = pl.BlockSpec((2, REACH, C), lambda p, *_: (0, 0, p))
    sds = jax.ShapeDtypeStruct
    cols = pairs * LANES
    return pl.pallas_call(
        functools.partial(bwd_kernel, blocks, images),
        grid_spec=pltpu.PrefetchScalarGridSpec(
            num_scalar_prefetch=1,
            grid=(pairs // PP,),
            in_specs=[spec(rows), spec(win), spec(win), spec(rows),
                      pl.BlockSpec((PP, blocks, 2 * QB), lambda p, *_: (first // PP + p, 0, 0))],
            out_specs=[out(rows), out(rows), out(rows), edge, edge],
            scratch_shapes=[pltpu.VMEM((rows, C), f32), pltpu.VMEM((win, C), f32), pltpu.VMEM((win, C), f32),
                            pltpu.SMEM((blocks * images,), jnp.int32)],
        ),
        out_shape=[sds((rows, cols), bf16), sds((rows, cols), f32), sds((rows, cols), f32),
                   sds((2, REACH, cols), bf16), sds((2, REACH, cols), bf16)],
        compiler_params=pltpu.CompilerParams(vmem_limit_bytes=VMEM, dimension_semantics=("arbitrary",)),
        cost_estimate=pl.CostEstimate(flops=pairs * 10 * 1300 * SPAN * 256, bytes_accessed=pairs * 2 * LANES * (8 * rows + 4 * win), transcendentals=pairs * 2 * 1300 * SPAN),
        name="attention_backward",
    )(img, q, k, v, g, lse)

def bit_orders(count):
    bits = [1 << i for i in range(count.bit_length() - 1)]
    return (bits[0], bits[2], bits[1], *reversed(bits[3:])), (bits[0], bits[1], bits[2], *reversed(bits[3:]))


def exchange(x, bit, count):
    return lax.ppermute(x, "dev", [(i, i ^ bit) for i in range(count)])


def owners(order, me):
    table = []
    for place in range(PIECES):
        offset = 0
        for i, bit in enumerate(order):
            if (place >> (len(order) - 1 - i)) & 1:
                offset |= bit
        table.append(offset)
    return jnp.array(table, jnp.int32) ^ me


def gather_pieces(shard, order, count):
    held = shard[None]
    for bit in reversed(order[1:]):
        held = jnp.concatenate([held, exchange(held, bit, count)], axis=0)
    return held, exchange(held, order[0], count)


def place_kernel(rows, table, near, far, out, sems):
    half = PIECES // 2
    copies = []
    for place in range(PIECES):
        source = near if place < half else far
        target = out.at[pl.ds(pl.multiple_of(table[place] * rows, 16), rows), :]
        copies.append(pltpu.make_async_copy(source.at[place % half], target, sems.at[place]))
    for copy in copies:
        copy.start()
    for copy in copies:
        copy.wait()


def place(near, far, table):
    _, rows, cols = near.shape
    return pl.pallas_call(
        functools.partial(place_kernel, rows),
        in_specs=[pl.BlockSpec(memory_space=pltpu.SMEM), pl.BlockSpec(memory_space=pl.ANY), pl.BlockSpec(memory_space=pl.ANY)],
        out_specs=pl.BlockSpec(memory_space=pl.ANY),
        out_shape=jax.ShapeDtypeStruct((PIECES * rows, cols), near.dtype),
        scratch_shapes=[pltpu.SemaphoreType.DMA((PIECES,))],
        name="place_pieces",
    )(table, near, far)


def spread_kernel(rows, table, whole, near, far, sems):
    half = PIECES // 2
    copies = []
    for place in range(PIECES):
        target = near if place < half else far
        source = whole.at[pl.ds(pl.multiple_of(table[place] * rows, 16), rows), :]
        copies.append(pltpu.make_async_copy(source, target.at[place % half], sems.at[place]))
    for copy in copies:
        copy.start()
    for copy in copies:
        copy.wait()


def spread(whole, table):
    rows, cols = whole.shape[0] // PIECES, whole.shape[1]
    piece = jax.ShapeDtypeStruct((PIECES // 2, rows, cols), whole.dtype)
    return pl.pallas_call(
        functools.partial(spread_kernel, rows),
        in_specs=[pl.BlockSpec(memory_space=pltpu.SMEM), pl.BlockSpec(memory_space=pl.ANY)],
        out_specs=[pl.BlockSpec(memory_space=pl.ANY)] * 2,
        out_shape=[piece, piece],
        scratch_shapes=[pltpu.SemaphoreType.DMA((PIECES,))],
        name="spread_pieces",
    )(table, whole)


def scatter_pieces(near, far, order, count):
    for step, bit in enumerate(order):
        arrived = exchange(far, bit, count)
        total = lambda a, b: a.astype(f32) + b.astype(f32)
        half = near.shape[0] // 2
        if step + 1 == len(order):
            return total(near, arrived)[0]
        near, far = (
            total(near[:half], arrived[:half]).astype(bf16),
            total(near[half:], arrived[half:]).astype(bf16),
        )


def all_sum(x, count):
    for bit in bit_orders(count)[0]:
        x = x + exchange(x, bit, count)
    return x


def gather_weight(parts, count, me):
    if count != PIECES:
        return [lax.all_gather(part, "dev", axis=0, tiled=True) for part in parts]
    orders = bit_orders(count)
    wholes = []
    for number, part in enumerate(parts):
        order = orders[number % 2]
        near, far = gather_pieces(part, order, count)
        wholes.append(place(near, far, owners(order, me)))
    return wholes


def scatter_weight(parts, count, me):
    if count != PIECES:
        return [lax.psum_scatter(part.astype(f32), "dev", scatter_dimension=0, tiled=True) for part in parts]
    orders = bit_orders(count)
    shards = []
    for number, part in enumerate(parts):
        order = orders[number % 2]
        near, far = spread(part.astype(bf16), owners(order, me))
        shards.append(scatter_pieces(near, far, order, count))
    return shards


def layer_norm(values, gain, bias):
    center = values - jnp.mean(values, axis=-1, keepdims=True)
    spread_of = jnp.mean(center * center, axis=-1, keepdims=True)
    return center * lax.rsqrt(spread_of + norm_epsilon) * gain + bias


def exact_gelu(values):
    return jax.nn.gelu(values, approximate=False)


def image_starts(segment_ids, me, rows):
    padded = jnp.pad(segment_ids, (REACH, REACH), constant_values=-2)
    window = lax.dynamic_slice_in_dim(padded, me * rows, rows + 2 * REACH, 0)
    own = window[REACH : REACH + rows]
    far = jnp.int32(1 << 20)
    first = jnp.min(jnp.where(own >= 0, own, far))
    places = jnp.arange(rows + 2 * REACH, dtype=jnp.int32)
    images = (rows - 2) // IMG + 2
    starts = []
    for i in range(images):
        start = jnp.min(jnp.where(window == first + i, places, far))
        starts.append(jnp.where(start == far, -far, start))
    return jnp.stack(starts)


def per_device(
    tokens,
    segment_ids,
    first_gain,
    first_bias,
    qkv_weight,
    query_bias,
    value_bias,
    out_weight,
    out_bias,
    second_gain,
    second_bias,
    hidden_weight,
    hidden_bias,
    final_weight,
    final_bias,
    cotangent,
):
    count = lax.axis_size("dev")
    me = lax.axis_index("dev")
    rows, width = tokens.shape
    hidden_width = hidden_weight.shape[1]
    pairs = width // LANES
    part = width // count
    img = image_starts(segment_ids, me, rows)
    to_right = [(i, i + 1) for i in range(count - 1)]
    to_left = [(i + 1, i) for i in range(count - 1)]
    window = jnp.concatenate(
        [lax.ppermute(tokens[rows - REACH :], "dev", to_right), tokens, lax.ppermute(tokens[:REACH], "dev", to_left)], axis=0
    )

    vectors = [first_gain, first_bias, query_bias, value_bias, out_bias, second_gain, second_bias, final_bias]
    small = jnp.concatenate([jnp.stack(vectors, axis=1), hidden_bias.reshape(part, -1)], axis=1).astype(bf16)
    small = jnp.pad(small, ((0, 0), (0, LANES - small.shape[1])))
    qkv_low = qkv_weight.astype(bf16)
    split = 2 * width
    part_one, part_two = gather_weight(
        [qkv_low[:, :split], jnp.concatenate([qkv_low[:, split:], out_weight.astype(bf16), small], axis=1)], count, me
    )
    feed = jnp.concatenate([hidden_weight.astype(bf16), final_weight.astype(bf16).reshape(4, part, width).transpose(1, 0, 2).reshape(part, 4 * width)], axis=1)
    feed = lax.all_gather(feed, "dev", axis=0, tiled=True)
    weight_hidden = feed[:, :hidden_width]
    weight_final = feed[:, hidden_width:].reshape(count, part, 4, width).transpose(0, 2, 1, 3).reshape(hidden_width, width)
    weight_value = part_two[:, :width]
    weight_out = part_two[:, width : 2 * width]
    vectors = part_two[:, 2 * width :].astype(f32)
    gain_one, bias_one, bias_query, bias_value, bias_out, gain_two, bias_two, bias_final = [vectors[:, i] for i in range(8)]
    bias_hidden = vectors[:, 8:12].reshape(hidden_width)

    normed = layer_norm(window.astype(f32), gain_one, bias_one).astype(bf16)
    normed_one = normed[REACH : REACH + rows]
    inputs = tokens.astype(f32)
    queries = (jnp.dot(normed_one, part_one[:, :width], preferred_element_type=f32) + bias_query).astype(bf16)
    queries = queries * jnp.asarray(HEAD**-0.5, bf16)
    key_rows = jnp.dot(normed, part_one[:, width:], preferred_element_type=f32).astype(bf16)
    value_rows = (jnp.dot(normed, weight_value, preferred_element_type=f32) + bias_value).astype(bf16)

    mixed_low, totals = attention_forward(img, queries, key_rows, value_rows, 0, pairs)
    middle = inputs + (jnp.dot(mixed_low, weight_out, preferred_element_type=f32) + bias_out)
    normed_two = layer_norm(middle, gain_two, bias_two).astype(bf16)
    hidden_pre = jnp.dot(normed_two, weight_hidden, preferred_element_type=f32) + bias_hidden
    activated = exact_gelu(hidden_pre).astype(bf16)
    result = (middle + jnp.dot(activated, weight_final, preferred_element_type=f32) + bias_final).astype(bf16)

    grad_output = cotangent.astype(f32)
    final_weight_grad = jnp.einsum("tf,td->fd", activated, cotangent, preferred_element_type=f32)
    final_bias_grad = jnp.sum(grad_output, axis=0)
    grad_activated = jnp.einsum("td,fd->tf", cotangent, weight_final, preferred_element_type=f32)
    gelu_pull = jax.vjp(exact_gelu, hidden_pre)[1]
    grad_pre = gelu_pull(grad_activated)[0].astype(bf16)
    hidden_bias_grad = jnp.sum(grad_pre, axis=0, dtype=f32)
    hidden_weight_grad = jnp.einsum("tc,tf->cf", normed_two, grad_pre, preferred_element_type=f32)
    grad_normed_two = jnp.einsum("tf,cf->tc", grad_pre, weight_hidden, preferred_element_type=f32)
    norm_pull = jax.vjp(layer_norm, middle, gain_two, bias_two)[1]
    grad_from_norm, second_gain_grad, second_bias_grad = norm_pull(grad_normed_two)
    grad_middle = grad_output + grad_from_norm
    grad_branch = grad_middle.astype(bf16)
    out_bias_grad = jnp.sum(grad_branch, axis=0, dtype=f32)
    out_weight_grad = jnp.einsum("tc,td->cd", mixed_low, grad_branch, preferred_element_type=f32)
    grad_mixed = jnp.einsum("td,cd->tc", grad_branch, weight_out, preferred_element_type=f32).astype(bf16)
    final_shard, hidden_shard, out_shard = scatter_weight([final_weight_grad, hidden_weight_grad, out_weight_grad], count, me)

    groups = 2
    step = pairs // groups
    cols = step * LANES
    query_parts, key_parts, value_parts = [], [], []
    for group in range(groups):
        dq, dk, dv, left, right = attention_backward(
            img, queries, key_rows, value_rows, grad_mixed, totals, group * step, step
        )
        from_left = lax.ppermute(right, "dev", to_right).astype(f32)
        from_right = lax.ppermute(left, "dev", to_left).astype(f32)
        rest = ((0, rows - REACH), (0, 0))
        back = ((rows - REACH, 0), (0, 0))
        key_parts.append((dk + jnp.pad(from_left[0], rest) + jnp.pad(from_right[0], back)).astype(bf16))
        value_parts.append((dv + jnp.pad(from_left[1], rest) + jnp.pad(from_right[1], back)).astype(bf16))
        query_parts.append(dq)
    grad_queries, grad_keys, grad_values = [jnp.concatenate(p, axis=1) for p in (query_parts, key_parts, value_parts)]
    grad_qk = jnp.concatenate([grad_queries, grad_keys], axis=1)
    qk_weight_grad = jnp.einsum("tc,tq->cq", normed_one, grad_qk, preferred_element_type=f32)
    value_weight_grad = jnp.einsum("tc,tq->cq", normed_one, grad_values, preferred_element_type=f32)
    query_bias_grad = jnp.sum(grad_queries, axis=0, dtype=f32)
    value_bias_grad = jnp.sum(grad_values, axis=0, dtype=f32)
    qk_shard, value_shard = scatter_weight([qk_weight_grad, value_weight_grad], count, me)
    grad_normed_one = jnp.einsum("tq,cq->tc", grad_qk, part_one, preferred_element_type=f32) + jnp.einsum(
        "tq,cq->tc", grad_values, weight_value, preferred_element_type=f32
    )
    first_pull = jax.vjp(layer_norm, inputs, gain_one, bias_one)[1]
    grad_from_first, first_gain_grad, first_bias_grad = first_pull(grad_normed_one)
    input_grad = (grad_middle + grad_from_first).astype(bf16)

    sums = [first_gain_grad, first_bias_grad, query_bias_grad, value_bias_grad, out_bias_grad, second_gain_grad, second_bias_grad, final_bias_grad]
    sums = jnp.concatenate([jnp.stack(sums), hidden_bias_grad.reshape(-1, width)], axis=0)
    sums = all_sum(sums, count)
    own = lax.dynamic_slice_in_dim(sums[:8], me * part, part, 1)
    own_hidden = lax.dynamic_slice_in_dim(sums[8:].reshape(-1), me * hidden_bias.shape[0], hidden_bias.shape[0], 0)
    return (
        result,
        input_grad,
        own[0],
        own[1],
        jnp.concatenate([qk_shard, value_shard], axis=1),
        own[2],
        own[3],
        out_shard,
        own[4],
        own[5],
        own[6],
        hidden_shard,
        own_hidden,
        final_shard,
        own[7],
    )


def solution(mesh):
    split = P("dev", None)
    line = P("dev")
    return jax.shard_map(
        per_device,
        mesh=mesh,
        in_specs=(split, P(), line, line, split, line, line, split, line, line, line, split, line, split, line, split),
        out_specs=(split, split, line, line, split, line, line, split, line, line, line, split, line, split, line),
        check_vma=False,
    )
```

```python
import functools
import math

import jax
import jax.numpy as jnp
from jax import lax
from jax.experimental import pallas as pl
from jax.experimental.pallas import tpu as pltpu
from jax.sharding import PartitionSpec as P

IMG = 577
REACH = IMG - 1
HEAD = 64
SPAN = 592
LANES = 128
QB = 256
PP = 2
PIECES = 32
VMEM = 60 * 1024 * 1024
f32 = jnp.float32
bf16 = jnp.bfloat16

norm_epsilon = 1e-06

def make_items(img_ref, items_ref, blocks, images):
    count = jnp.int32(0)
    for b in range(blocks):
        for i in range(images):
            start = img_ref[i]
            low = b * QB + REACH
            hit = (start < low + QB) & (start + IMG > low)

            @pl.when(hit)
            def _():
                items_ref[count] = b * 8 + i

            count = count + hit.astype(jnp.int32)
    return count

def item_scalars(img_ref, items_ref, n):
    code = items_ref[n]
    b = code // 8
    start = img_ref[code % 8]
    begin = pl.multiple_of((start // 16) * 16, 16)
    row = pl.multiple_of(b * QB, QB)
    return b, start, begin, row

def halves(x):
    lane = lax.broadcasted_iota(jnp.int32, x.shape, 1)
    zero = jnp.zeros_like(x)
    return jnp.concatenate([jnp.where(lane < HEAD, x, zero), jnp.where(lane >= HEAD, x, zero)], axis=0)

def key_valid(start, begin):
    r = lax.broadcasted_iota(jnp.int32, (SPAN, 1), 0) + (begin - start)
    return (r >= 0) & (r < IMG)

def query_valid(start, row):
    lane = lax.broadcasted_iota(jnp.int32, (1, 2 * QB), 1)
    pos = jnp.where(lane < QB, lane, lane - QB) + (row + REACH - start)
    return (pos >= 0) & (pos < IMG)

def pad_rows(img_ref, images, rows):
    r = lax.broadcasted_iota(jnp.int32, (rows, LANES), 0) + REACH
    inside = jnp.zeros((rows, LANES), jnp.bool_)
    for i in range(images):
        start = img_ref[i]
        inside = inside | ((r >= start) & (r < start + IMG))
    return ~inside

def fwd_kernel(blocks, images, img_ref, q_ref, k_ref, v_ref, o_ref, lse_ref, acc, items):
    rows = blocks * QB
    count = make_items(img_ref, items, blocks, images)
    acc[...] = jnp.zeros_like(acc)
    lse_ref[...] = jnp.zeros_like(lse_ref)

    def body(n, carry):
        b, start, begin, row = item_scalars(img_ref, items, n)
        valid = key_valid(start, begin)
        qm = query_valid(start, row)
        done = []
        for u in range(PP):
            cols = slice(u * LANES, (u + 1) * LANES)
            q2 = halves(q_ref[pl.ds(row, QB), cols])
            kw = k_ref[pl.ds(begin, SPAN), cols]
            vw = v_ref[pl.ds(begin, SPAN), cols]
            s = lax.dot_general(kw, q2, (((1,), (1,)), ((), ())), preferred_element_type=f32)
            s = jnp.where(valid, s, -1e30)
            m = jnp.max(s, axis=0, keepdims=True)
            e = jnp.exp(s - m)
            l = jnp.sum(e, axis=0, keepdims=True)
            p = (e * jnp.where(qm, 1.0 / l, 0.0)).astype(bf16)
            ot = lax.dot_general(vw, p, (((0,), (0,)), ((), ())), preferred_element_type=f32)
            done.append((jnp.concatenate([ot[:HEAD, :QB], ot[HEAD:, QB:]], axis=0).T, m + jnp.log(l)))
        for u in range(PP):
            cols = slice(u * LANES, (u + 1) * LANES)
            o, total = done[u]
            acc[pl.ds(row, QB), cols] += o
            old = lse_ref[u, pl.ds(b, 1), :]
            lse_ref[u, pl.ds(b, 1), :] = jnp.where(qm, total, old)
        return carry

    lax.fori_loop(0, count, body, 0)
    pad = pad_rows(img_ref, images, rows)
    for u in range(PP):
        cols = slice(u * LANES, (u + 1) * LANES)
        own = v_ref[pl.ds(REACH, rows), cols].astype(f32)
        o_ref[:, cols] = jnp.where(pad, own, acc[:, cols]).astype(bf16)

def attention_forward(img, q, k, v, first, pairs):
    rows, width = q.shape
    win = k.shape[0]
    blocks = rows // QB
    images = img.shape[0]
    spec = lambda r: pl.BlockSpec((r, PP * LANES), lambda p, *_: (0, first // PP + p))
    return pl.pallas_call(
        functools.partial(fwd_kernel, blocks, images),
        grid_spec=pltpu.PrefetchScalarGridSpec(
            num_scalar_prefetch=1,
            grid=(pairs // PP,),
            in_specs=[spec(rows), spec(win), spec(win)],
            out_specs=[
                pl.BlockSpec((rows, PP * LANES), lambda p, *_: (0, p)),
                pl.BlockSpec((PP, blocks, 2 * QB), lambda p, *_: (p, 0, 0)),
            ],
            scratch_shapes=[pltpu.VMEM((rows, PP * LANES), f32), pltpu.SMEM((blocks * images,), jnp.int32)],
        ),
        out_shape=[
            jax.ShapeDtypeStruct((rows, pairs * LANES), bf16),
            jax.ShapeDtypeStruct((pairs, blocks, 2 * QB), f32),
        ],
        compiler_params=pltpu.CompilerParams(vmem_limit_bytes=VMEM, dimension_semantics=("arbitrary",)),
        cost_estimate=pl.CostEstimate(flops=pairs * 4 * 1300 * SPAN * 256, bytes_accessed=pairs * 2 * LANES * (2 * rows + 2 * win), transcendentals=pairs * 2 * 1300 * SPAN),
        name="attention_forward",
    )(img, q, k, v)

def bwd_kernel(blocks, images, img_ref, q_ref, k_ref, v_ref, g_ref, lse_ref,
               dq_ref, dk_ref, dv_ref, left_ref, right_ref, dq_acc, dk_acc, dv_acc, items):
    rows = blocks * QB
    count = make_items(img_ref, items, blocks, images)
    dq_acc[...] = jnp.zeros_like(dq_acc)
    dk_acc[...] = jnp.zeros_like(dk_acc)
    dv_acc[...] = jnp.zeros_like(dv_acc)

    def body(n, carry):
        b, start, begin, row = item_scalars(img_ref, items, n)
        valid = key_valid(start, begin)
        qm = query_valid(start, row)
        done = []
        for u in range(PP):
            cols = slice(u * LANES, (u + 1) * LANES)
            q2 = halves(q_ref[pl.ds(row, QB), cols])
            g2 = halves(g_ref[pl.ds(row, QB), cols])
            kw = k_ref[pl.ds(begin, SPAN), cols]
            vw = v_ref[pl.ds(begin, SPAN), cols]
            lse = jnp.where(qm, lse_ref[u, pl.ds(b, 1), :], 1e30)
            s = lax.dot_general(kw, q2, (((1,), (1,)), ((), ())), preferred_element_type=f32)
            dp = lax.dot_general(vw, g2, (((1,), (1,)), ((), ())), preferred_element_type=f32)
            p = jnp.exp(jnp.where(valid, s, -1e30) - lse)
            inner = jnp.sum(p * dp, axis=0, keepdims=True)
            ds = (p * (dp - inner)).astype(bf16)
            dv = jnp.dot(p.astype(bf16), g2, preferred_element_type=f32)
            dk = jnp.dot(ds, q2, preferred_element_type=f32)
            dqt = lax.dot_general(kw, ds, (((0,), (0,)), ((), ())), preferred_element_type=f32)
            done.append((dv, dk, jnp.concatenate([dqt[:HEAD, :QB], dqt[HEAD:, QB:]], axis=0).T))
        for u in range(PP):
            cols = slice(u * LANES, (u + 1) * LANES)
            dv, dk, dq = done[u]
            dv_acc[pl.ds(begin, SPAN), cols] += dv
            dk_acc[pl.ds(begin, SPAN), cols] += dk
            dq_acc[pl.ds(row, QB), cols] += dq
        return carry

    lax.fori_loop(0, count, body, 0)
    pad = pad_rows(img_ref, images, rows)
    dq_ref[...] = (dq_acc[...] * 0.125).astype(bf16)
    dk_ref[...] = dk_acc[pl.ds(REACH, rows), :]
    for u in range(PP):
        cols = slice(u * LANES, (u + 1) * LANES)
        dv_ref[:, cols] = dv_acc[pl.ds(REACH, rows), cols] + jnp.where(pad, g_ref[:, cols].astype(f32), 0.0)
    left_ref[0] = dk_acc[pl.ds(0, REACH), :].astype(bf16)
    left_ref[1] = dv_acc[pl.ds(0, REACH), :].astype(bf16)
    right_ref[0] = dk_acc[pl.ds(REACH + rows, REACH), :].astype(bf16)
    right_ref[1] = dv_acc[pl.ds(REACH + rows, REACH), :].astype(bf16)

def attention_backward(img, q, k, v, g, lse, first, pairs):
    rows, width = q.shape
    win = k.shape[0]
    blocks = rows // QB
    images = img.shape[0]
    C = PP * LANES
    spec = lambda r: pl.BlockSpec((r, C), lambda p, *_: (0, first // PP + p))
    out = lambda r: pl.BlockSpec((r, C), lambda p, *_: (0, p))
    edge = pl.BlockSpec((2, REACH, C), lambda p, *_: (0, 0, p))
    sds = jax.ShapeDtypeStruct
    cols = pairs * LANES
    return pl.pallas_call(
        functools.partial(bwd_kernel, blocks, images),
        grid_spec=pltpu.PrefetchScalarGridSpec(
            num_scalar_prefetch=1,
            grid=(pairs // PP,),
            in_specs=[spec(rows), spec(win), spec(win), spec(rows),
                      pl.BlockSpec((PP, blocks, 2 * QB), lambda p, *_: (first // PP + p, 0, 0))],
            out_specs=[out(rows), out(rows), out(rows), edge, edge],
            scratch_shapes=[pltpu.VMEM((rows, C), f32), pltpu.VMEM((win, C), f32), pltpu.VMEM((win, C), f32),
                            pltpu.SMEM((blocks * images,), jnp.int32)],
        ),
        out_shape=[sds((rows, cols), bf16), sds((rows, cols), f32), sds((rows, cols), f32),
                   sds((2, REACH, cols), bf16), sds((2, REACH, cols), bf16)],
        compiler_params=pltpu.CompilerParams(vmem_limit_bytes=VMEM, dimension_semantics=("arbitrary",)),
        cost_estimate=pl.CostEstimate(flops=pairs * 10 * 1300 * SPAN * 256, bytes_accessed=pairs * 2 * LANES * (8 * rows + 4 * win), transcendentals=pairs * 2 * 1300 * SPAN),
        name="attention_backward",
    )(img, q, k, v, g, lse)


FT = 512
ROWS = 256


def contract(a, b, dims):
    return lax.dot_general(a, b, (dims, ((), ())), preferred_element_type=f32)


def feed_kernel(
    tiles, places, table, home, normed, cot, middle, bias_final, wide, tall, bias_hidden,
    result, grad_normed, bias_grad, hidden_near, hidden_far, final_near, final_far,
    total, normed_t, final, active, grad_pre, hidden_grad, final_grad, sems,
):
    step = pl.program_id(0)
    slot = lax.rem(step, 2)
    rows, width = normed.shape
    devices = tall.shape[0] // 32
    depth = FT // devices
    half = places // 2

    @pl.when(step == 0)
    def _():
        total[...] = middle[...] + bias_final[...]
        grad_normed[...] = jnp.zeros_like(grad_normed)
        normed_t[...] = normed[...].T

    for d in range(devices):
        for i in range(4):
            final[d * depth + i * 32 : d * depth + (i + 1) * 32, :] = tall[d * 32 : (d + 1) * 32, i * width : (i + 1) * width]
    for r in range(0, rows, ROWS):
        cut = slice(r, r + ROWS)
        pre = contract(normed[cut, :], wide[...], ((1,), (0,))) + bias_hidden[...]
        grad = contract(cot[cut, :], final[...], ((1,), (1,)))
        phi = 0.5 + 0.5 * lax.erf(pre * (0.5**0.5))
        slope = phi + pre * jnp.exp(pre * pre * -0.5) * ((0.5 / math.pi) ** 0.5)
        active[cut, :] = (pre * phi).astype(bf16)
        grad_pre[cut, :] = (grad * slope).astype(bf16)
        total[cut, :] += contract(active[cut, :], final[...], ((1,), (0,)))
        grad_normed[cut, :] += contract(grad_pre[cut, :], wide[...], ((1,), (1,)))
    bias_grad[...] = jnp.sum(grad_pre[...].astype(f32), axis=0, keepdims=True)

    hidden_grad[...] = contract(normed_t[...], grad_pre[...], ((1,), (0,)))
    piece = width // places
    for place in range(places):
        rows_of = hidden_grad[pl.ds(pl.multiple_of(table[place] * piece, piece), piece), :].astype(bf16)
        if place < half:
            hidden_near[place] = rows_of
        else:
            hidden_far[place - half] = rows_of

    def copy_out(slot, d, target):
        return pltpu.make_async_copy(final_grad.at[slot, d], target, sems.at[slot, d])

    @pl.when(step >= 2)
    def _():
        for d in range(devices):
            copy_out(slot, d, final_near.at[0]).wait()

    final_grad[slot] = contract(active[...], cot[...], ((0,), (0,))).astype(bf16).reshape(devices, depth, width)
    for d in range(devices):
        at = home[step * devices + d]

        @pl.when(at < half)
        def _():
            copy_out(slot, d, final_near.at[at]).start()

        @pl.when(at >= half)
        def _():
            copy_out(slot, d, final_far.at[at - half]).start()

    @pl.when(step == tiles - 1)
    def _():
        result[...] = total[...].astype(bf16)
        for d in range(devices):
            copy_out(1 - slot, d, final_near.at[0]).wait()
            copy_out(slot, d, final_near.at[0]).wait()


def feed_forward(normed, cot, middle, bias_final, feed, bias_hidden, table, home):
    rows, width = normed.shape
    hidden_width = bias_hidden.shape[1]
    tiles = hidden_width // FT
    places = PIECES
    whole = lambda *shape: pl.BlockSpec(shape, lambda t, *_: (0,) * len(shape), pipeline_mode=pl.Buffered(1))
    sds = jax.ShapeDtypeStruct
    final_rows = hidden_width // places
    devices = FT // final_rows
    edge = pl.BlockSpec((places // 2, width // places, FT), lambda t, *_: (0, 0, t))
    anywhere = pl.BlockSpec(memory_space=pl.ANY)
    flops = 12 * rows * width * hidden_width
    return pl.pallas_call(
        functools.partial(feed_kernel, tiles, places),
        grid_spec=pltpu.PrefetchScalarGridSpec(
            num_scalar_prefetch=2,
            grid=(tiles,),
            in_specs=[
                whole(rows, width), whole(rows, width), whole(rows, width), whole(1, width),
                pl.BlockSpec((width, FT), lambda t, *_: (0, t)),
                pl.BlockSpec((devices * 32, 4 * width), lambda t, *_: (t, 1)),
                pl.BlockSpec((1, FT), lambda t, *_: (0, t)),
            ],
            out_specs=[
                whole(rows, width), whole(rows, width), pl.BlockSpec((1, FT), lambda t, *_: (0, t)),
                edge, edge, anywhere, anywhere,
            ],
            scratch_shapes=[
                pltpu.VMEM((rows, width), f32), pltpu.VMEM((width, rows), bf16), pltpu.VMEM((FT, width), bf16),
                pltpu.VMEM((rows, FT), bf16), pltpu.VMEM((rows, FT), bf16), pltpu.VMEM((width, FT), f32),
                pltpu.VMEM((2, devices, final_rows, width), bf16), pltpu.SemaphoreType.DMA((2, devices)),
            ],
        ),
        out_shape=[
            sds((rows, width), bf16), sds((rows, width), f32), sds((1, hidden_width), f32),
            sds((places // 2, width // places, hidden_width), bf16), sds((places // 2, width // places, hidden_width), bf16),
            sds((places // 2, final_rows, width), bf16), sds((places // 2, final_rows, width), bf16),
        ],
        compiler_params=pltpu.CompilerParams(vmem_limit_bytes=VMEM, dimension_semantics=("arbitrary",)),
        cost_estimate=pl.CostEstimate(flops=flops, bytes_accessed=60 * 1024 * 1024, transcendentals=2 * rows * hidden_width),
        name="feed_forward",
    )(table, home, normed, cot, middle, bias_final, feed, feed, bias_hidden)


def bit_orders(count):
    bits = [1 << i for i in range(count.bit_length() - 1)]
    return (bits[0], bits[2], bits[1], *bits[3:]), (bits[0], bits[1], bits[2], *bits[3:])


def exchange(x, bit, count):
    return lax.ppermute(x, "dev", [(i, i ^ bit) for i in range(count)])


def owners(order, me):
    table = []
    for place in range(PIECES):
        offset = 0
        for i, bit in enumerate(order):
            if (place >> (len(order) - 1 - i)) & 1:
                offset |= bit
        table.append(offset)
    return jnp.array(table, jnp.int32) ^ me


def gather_pieces(shard, order, count):
    held = shard[None]
    for bit in reversed(order[1:]):
        held = jnp.concatenate([held, exchange(held, bit, count)], axis=0)
    return held, exchange(held, order[0], count)


def place_kernel(table, near, far, out):
    half, rows, _ = near.shape
    for place in range(2 * half):
        piece = near[place] if place < half else far[place - half]
        out[pl.ds(pl.multiple_of(table[place] * rows, rows), rows), :] = piece


def place(near, far, table):
    half, rows, cols = near.shape
    step = max(c for c in range(LANES, 1024, LANES) if cols % c == 0)
    return pl.pallas_call(
        place_kernel,
        grid_spec=pltpu.PrefetchScalarGridSpec(
            num_scalar_prefetch=1,
            grid=(cols // step,),
            in_specs=[pl.BlockSpec((half, rows, step), lambda c, *_: (0, 0, c))] * 2,
            out_specs=pl.BlockSpec((2 * half * rows, step), lambda c, *_: (0, c)),
        ),
        out_shape=jax.ShapeDtypeStruct((2 * half * rows, cols), near.dtype),
        compiler_params=pltpu.CompilerParams(vmem_limit_bytes=VMEM, dimension_semantics=("arbitrary",)),
        cost_estimate=pl.CostEstimate(flops=0, bytes_accessed=8 * half * rows * cols, transcendentals=0),
        name="place_pieces",
    )(table, near, far)


def spread_kernel(table, whole, near, far):
    half, rows, _ = near.shape
    for place in range(2 * half):
        piece = whole[pl.ds(pl.multiple_of(table[place] * rows, rows), rows), :]
        if place < half:
            near[place] = piece
        else:
            far[place - half] = piece


def spread(whole, table):
    total, cols = whole.shape
    half, rows = PIECES // 2, total // PIECES
    step = max(c for c in range(LANES, 1024, LANES) if cols % c == 0)
    piece = jax.ShapeDtypeStruct((half, rows, cols), whole.dtype)
    return pl.pallas_call(
        spread_kernel,
        grid_spec=pltpu.PrefetchScalarGridSpec(
            num_scalar_prefetch=1,
            grid=(cols // step,),
            in_specs=[pl.BlockSpec((total, step), lambda c, *_: (0, c))],
            out_specs=[pl.BlockSpec((half, rows, step), lambda c, *_: (0, 0, c))] * 2,
        ),
        out_shape=[piece, piece],
        compiler_params=pltpu.CompilerParams(vmem_limit_bytes=VMEM, dimension_semantics=("arbitrary",)),
        cost_estimate=pl.CostEstimate(flops=0, bytes_accessed=4 * total * cols, transcendentals=0),
        name="spread_pieces",
    )(table, whole)


def add_low(a, b):
    return (a.astype(f32) + b.astype(f32)).astype(bf16)


def scatter_step(near, far, bit, count):
    arrived = exchange(far, bit, count)
    half = near.shape[0] // 2
    if half == 0:
        return near[0].astype(f32) + arrived[0].astype(f32), None
    return add_low(near[:half], arrived[:half]), add_low(near[half:], arrived[half:])


def scatter_steps(near, far, order, count):
    for bit in order:
        near, far = scatter_step(near, far, bit, count)
    return near


def all_sum(x, count):
    for bit in bit_orders(count)[0]:
        x = x + exchange(x, bit, count)
    return x


def gather_weight(parts, count, me):
    if count != PIECES:
        return [lax.all_gather(part, "dev", axis=0, tiled=True) for part in parts]
    orders = bit_orders(count)
    wholes = []
    for number, part in enumerate(parts):
        order = orders[number % 2]
        near, far = gather_pieces(part, order, count)
        wholes.append(place(near, far, owners(order, me)))
    return wholes


def scatter_whole(near, far, count):
    whole = jnp.concatenate([near, far], axis=0).reshape(-1, near.shape[2])
    return lax.psum_scatter(whole.astype(f32), "dev", scatter_dimension=0, tiled=True)


def layer_norm(values, gain, bias):
    center = values - jnp.mean(values, axis=-1, keepdims=True)
    spread_of = jnp.mean(center * center, axis=-1, keepdims=True)
    return center * lax.rsqrt(spread_of + norm_epsilon) * gain + bias


def image_starts(segment_ids, me, rows):
    padded = jnp.pad(segment_ids, (REACH, REACH), constant_values=-2)
    window = lax.dynamic_slice_in_dim(padded, me * rows, rows + 2 * REACH, 0)
    own = window[REACH : REACH + rows]
    far = jnp.int32(1 << 20)
    first = jnp.min(jnp.where(own >= 0, own, far))
    places = jnp.arange(rows + 2 * REACH, dtype=jnp.int32)
    images = (rows - 2) // IMG + 2
    starts = []
    for i in range(images):
        start = jnp.min(jnp.where(window == first + i, places, far))
        starts.append(jnp.where(start == far, -far, start))
    return jnp.stack(starts)


def per_device(
    tokens,
    segment_ids,
    first_gain,
    first_bias,
    qkv_weight,
    query_bias,
    value_bias,
    out_weight,
    out_bias,
    second_gain,
    second_bias,
    hidden_weight,
    hidden_bias,
    final_weight,
    final_bias,
    cotangent,
):
    count = lax.axis_size("dev")
    me = lax.axis_index("dev")
    direct = count == PIECES
    rows, width = tokens.shape
    hidden_width = hidden_weight.shape[1]
    pairs = width // LANES
    part = width // count
    order_one, order_two = bit_orders(PIECES)
    table_one = owners(order_one, me if direct else 0)
    table_two = owners(order_two, me if direct else 0)
    home_two = jnp.argsort(table_two).astype(jnp.int32)
    img = image_starts(segment_ids, me, rows)
    to_right = [(i, i + 1) for i in range(count - 1)]
    to_left = [(i + 1, i) for i in range(count - 1)]
    window = jnp.concatenate(
        [lax.ppermute(tokens[rows - REACH :], "dev", to_right), tokens, lax.ppermute(tokens[:REACH], "dev", to_left)], axis=0
    )

    vectors = [first_gain, first_bias, query_bias, value_bias, out_bias, second_gain, second_bias, final_bias]
    small = jnp.concatenate([jnp.stack(vectors, axis=1), hidden_bias.reshape(part, -1)], axis=1).astype(bf16)
    small = jnp.pad(small, ((0, 0), (0, 2 * LANES - small.shape[1])))
    qkv_low = qkv_weight.astype(bf16)
    split = 2 * width
    part_one, part_two = gather_weight(
        [qkv_low[:, :split], jnp.concatenate([qkv_low[:, split:], out_weight.astype(bf16), small], axis=1)], count, me
    )
    final_low = final_weight.astype(bf16)
    if direct:
        feed = jnp.concatenate([hidden_weight.astype(bf16)] + [final_low[32 * i : 32 * (i + 1)] for i in range(4)], axis=1)
        feed = lax.all_gather(feed, "dev", axis=0, tiled=True)
    else:
        hidden_low = lax.all_gather(hidden_weight.astype(bf16), "dev", axis=0, tiled=True)
        final_low = lax.all_gather(final_low, "dev", axis=0, tiled=True)
        final_low = final_low.reshape(PIECES, 4, 32, width).transpose(0, 2, 1, 3).reshape(width, 4 * width)
        feed = jnp.concatenate([hidden_low, final_low], axis=1)
    weight_value = part_two[:, :width]
    weight_out = part_two[:, width : 2 * width]
    vectors = part_two[:, 2 * width :].astype(f32)
    gain_one, bias_one, bias_query, bias_value, bias_out, gain_two, bias_two, bias_final = [vectors[:, i] for i in range(8)]
    bias_hidden = vectors[:, 8 : 8 + hidden_width // width].reshape(1, hidden_width)

    normed = layer_norm(window.astype(f32), gain_one, bias_one).astype(bf16)
    normed_one = normed[REACH : REACH + rows]
    inputs = tokens.astype(f32)
    queries = (jnp.dot(normed_one, part_one[:, :width], preferred_element_type=f32) + bias_query).astype(bf16)
    queries = queries * jnp.asarray(HEAD**-0.5, bf16)
    key_rows = jnp.dot(normed, part_one[:, width:], preferred_element_type=f32).astype(bf16)
    value_rows = (jnp.dot(normed, weight_value, preferred_element_type=f32) + bias_value).astype(bf16)

    mixed_low, totals = attention_forward(img, queries, key_rows, value_rows, 0, pairs)
    middle = inputs + (jnp.dot(mixed_low, weight_out, preferred_element_type=f32) + bias_out)
    normed_two = layer_norm(middle, gain_two, bias_two).astype(bf16)
    grad_output = cotangent.astype(f32)
    final_bias_grad = jnp.sum(grad_output, axis=0)
    result, grad_normed_two, hidden_bias_grad, hidden_near, hidden_far, final_near, final_far = feed_forward(
        normed_two, cotangent, middle, bias_final[None], feed, bias_hidden, table_one, home_two
    )

    norm_pull = jax.vjp(layer_norm, middle, gain_two, bias_two)[1]
    grad_from_norm, second_gain_grad, second_bias_grad = norm_pull(grad_normed_two)
    grad_middle = grad_output + grad_from_norm
    grad_branch = grad_middle.astype(bf16)
    out_bias_grad = jnp.sum(grad_branch, axis=0, dtype=f32)
    grad_mixed = jnp.einsum("td,cd->tc", grad_branch, weight_out, preferred_element_type=f32).astype(bf16)
    if direct:
        hidden_near, hidden_far = scatter_step(hidden_near, hidden_far, order_one[0], count)
        final_near, final_far = scatter_step(final_near, final_far, order_two[0], count)
        grad_mixed, hidden_near, hidden_far, final_near, final_far = lax.optimization_barrier(
            (grad_mixed, hidden_near, hidden_far, final_near, final_far)
        )
    else:
        hidden_shard = scatter_whole(hidden_near, hidden_far, count)
        final_shard = scatter_whole(final_near, final_far, count)

    groups = 2
    step = pairs // groups
    cols = step * LANES
    query_parts, key_parts, value_parts, shards = [], [], [], []
    for group in range(groups):
        dq, dk, dv, left, right = attention_backward(
            img, queries, key_rows, value_rows, grad_mixed, totals, group * step, step
        )
        if direct and group == groups - 1:
            hidden_near, hidden_far = scatter_step(hidden_near, hidden_far, order_one[1], count)
            final_near, final_far = scatter_step(final_near, final_far, order_two[1], count)
            dq, hidden_near, hidden_far, final_near, final_far = lax.optimization_barrier(
                (dq, hidden_near, hidden_far, final_near, final_far)
            )
            hidden_shard = scatter_steps(hidden_near, hidden_far, order_one[2:], count)
            final_shard = scatter_steps(final_near, final_far, order_two[2:], count)
        from_left = lax.ppermute(right, "dev", to_right).astype(f32)
        from_right = lax.ppermute(left, "dev", to_left).astype(f32)
        rest = ((0, rows - REACH), (0, 0))
        back = ((rows - REACH, 0), (0, 0))
        query_parts.append(dq)
        key_parts.append((dk + jnp.pad(from_left[0], rest) + jnp.pad(from_right[0], back)).astype(bf16))
        value_parts.append((dv + jnp.pad(from_left[1], rest) + jnp.pad(from_right[1], back)).astype(bf16))
        packed = jnp.concatenate([query_parts[-1], key_parts[-1], value_parts[-1]], axis=1)
        share = jnp.einsum("tc,tq->cq", normed_one, packed, preferred_element_type=f32).astype(bf16)
        pieces = [share[:, : share.shape[1] // 2], share[:, share.shape[1] // 2 :]]
        if group == 0:
            pieces = [share, jnp.einsum("tc,td->cd", mixed_low, grad_branch, preferred_element_type=f32).astype(bf16)]
        for piece, order, table in zip(pieces, (order_one, order_two), (table_one, table_two)):
            near, far = spread(piece, table)
            shards.append(scatter_steps(near, far, order, count) if direct else scatter_whole(near, far, count))
    grad_queries, grad_keys, grad_values = [jnp.concatenate(p, axis=1) for p in (query_parts, key_parts, value_parts)]
    out_shard = shards[1]
    halves_of = [shards[0], jnp.concatenate(shards[2:], axis=1)]
    qkv_shard = jnp.concatenate([h[:, i * cols : (i + 1) * cols] for i in range(3) for h in halves_of], axis=1)
    query_bias_grad = jnp.sum(grad_queries, axis=0, dtype=f32)
    value_bias_grad = jnp.sum(grad_values, axis=0, dtype=f32)
    grad_normed_one = jnp.einsum(
        "tq,cq->tc", jnp.concatenate([grad_queries, grad_keys], axis=1), part_one, preferred_element_type=f32
    ) + jnp.einsum("tq,cq->tc", grad_values, weight_value, preferred_element_type=f32)
    first_pull = jax.vjp(layer_norm, inputs, gain_one, bias_one)[1]
    grad_from_first, first_gain_grad, first_bias_grad = first_pull(grad_normed_one)
    input_grad = (grad_middle + grad_from_first).astype(bf16)

    sums = [first_gain_grad, first_bias_grad, query_bias_grad, value_bias_grad, out_bias_grad, second_gain_grad, second_bias_grad, final_bias_grad]
    sums = jnp.concatenate([jnp.stack(sums), hidden_bias_grad.reshape(-1, width)], axis=0)
    sums = all_sum(sums, count)
    own = lax.dynamic_slice_in_dim(sums[:8], me * part, part, 1)
    own_hidden = lax.dynamic_slice_in_dim(sums[8:].reshape(-1), me * hidden_bias.shape[0], hidden_bias.shape[0], 0)
    return (
        result,
        input_grad,
        own[0],
        own[1],
        qkv_shard,
        own[2],
        own[3],
        out_shard,
        own[4],
        own[5],
        own[6],
        hidden_shard,
        own_hidden,
        final_shard,
        own[7],
    )


def solution(mesh):
    split = P("dev", None)
    line = P("dev")
    return jax.shard_map(
        per_device,
        mesh=mesh,
        in_specs=(split, P(), line, line, split, line, line, split, line, line, line, split, line, split, line, split),
        out_specs=(split, split, line, line, split, line, line, split, line, line, line, split, line, split, line),
        check_vma=False,
    )
```

```python
import functools
import math

import jax
import jax.numpy as jnp
from jax import lax
from jax.experimental import pallas as pl
from jax.experimental.pallas import tpu as pltpu
from jax.sharding import PartitionSpec as P

IMG = 577
REACH = IMG - 1
HEAD = 64
SPAN = 592
LANES = 128
QB = 256
PP = 2
PIECES = 32
PACE = 1.0e5
FEED_AFTER = 2
GROUPS = 2
VMEM = 60 * 1024 * 1024
f32 = jnp.float32
bf16 = jnp.bfloat16

norm_epsilon = 1e-06


def spent(us):
    return pl.CostEstimate(flops=0, bytes_accessed=int(us * PACE), transcendentals=0)


def make_items(img_ref, items_ref, blocks, images):
    count = jnp.int32(0)
    for b in range(blocks):
        for i in range(images):
            start = img_ref[i]
            low = b * QB + REACH
            hit = (start < low + QB) & (start + IMG > low)

            @pl.when(hit)
            def _():
                items_ref[count] = b * 8 + i

            count = count + hit.astype(jnp.int32)
    return count

def item_scalars(img_ref, items_ref, n):
    code = items_ref[n]
    b = code // 8
    start = img_ref[code % 8]
    begin = pl.multiple_of((start // 16) * 16, 16)
    row = pl.multiple_of(b * QB, QB)
    return b, start, begin, row

def halves(x):
    lane = lax.broadcasted_iota(jnp.int32, x.shape, 1)
    zero = jnp.zeros_like(x)
    return jnp.concatenate([jnp.where(lane < HEAD, x, zero), jnp.where(lane >= HEAD, x, zero)], axis=0)

def key_valid(start, begin):
    r = lax.broadcasted_iota(jnp.int32, (SPAN, 1), 0) + (begin - start)
    return (r >= 0) & (r < IMG)

def query_valid(start, row):
    lane = lax.broadcasted_iota(jnp.int32, (1, 2 * QB), 1)
    pos = jnp.where(lane < QB, lane, lane - QB) + (row + REACH - start)
    return (pos >= 0) & (pos < IMG)

def pad_rows(img_ref, images, rows):
    r = lax.broadcasted_iota(jnp.int32, (rows, LANES), 0) + REACH
    inside = jnp.zeros((rows, LANES), jnp.bool_)
    for i in range(images):
        start = img_ref[i]
        inside = inside | ((r >= start) & (r < start + IMG))
    return ~inside

def fwd_kernel(blocks, images, img_ref, q_ref, k_ref, v_ref, o_ref, lse_ref, acc, items):
    rows = blocks * QB
    count = make_items(img_ref, items, blocks, images)
    acc[...] = jnp.zeros_like(acc)
    lse_ref[...] = jnp.zeros_like(lse_ref)

    def body(n, carry):
        b, start, begin, row = item_scalars(img_ref, items, n)
        valid = key_valid(start, begin)
        qm = query_valid(start, row)
        done = []
        for u in range(PP):
            cols = slice(u * LANES, (u + 1) * LANES)
            q2 = halves(q_ref[pl.ds(pl.multiple_of(row + REACH, 16), QB), cols])
            kw = k_ref[pl.ds(begin, SPAN), cols]
            vw = v_ref[pl.ds(begin, SPAN), cols]
            s = lax.dot_general(kw, q2, (((1,), (1,)), ((), ())), preferred_element_type=f32)
            s = jnp.where(valid, s, -1e30)
            m = jnp.max(s, axis=0, keepdims=True)
            e = jnp.exp(s - m)
            l = jnp.sum(e, axis=0, keepdims=True)
            p = (e * jnp.where(qm, 1.0 / l, 0.0)).astype(bf16)
            ot = lax.dot_general(vw, p, (((0,), (0,)), ((), ())), preferred_element_type=f32)
            done.append((jnp.concatenate([ot[:HEAD, :QB], ot[HEAD:, QB:]], axis=0).T, m + jnp.log(l)))
        for u in range(PP):
            cols = slice(u * LANES, (u + 1) * LANES)
            o, total = done[u]
            acc[pl.ds(row, QB), cols] += o
            old = lse_ref[u, pl.ds(b, 1), :]
            lse_ref[u, pl.ds(b, 1), :] = jnp.where(qm, total, old)
        return carry

    lax.fori_loop(0, count, body, 0)
    pad = pad_rows(img_ref, images, rows)
    for u in range(PP):
        cols = slice(u * LANES, (u + 1) * LANES)
        own = v_ref[pl.ds(REACH, rows), cols].astype(f32)
        o_ref[:, cols] = jnp.where(pad, own, acc[:, cols]).astype(bf16)

def attention_forward(img, q, k, v, first, pairs):
    win = k.shape[0]
    rows = win - 2 * REACH
    blocks = rows // QB
    images = img.shape[0]
    spec = lambda r: pl.BlockSpec((r, PP * LANES), lambda p, *_: (0, first // PP + p))
    return pl.pallas_call(
        functools.partial(fwd_kernel, blocks, images),
        grid_spec=pltpu.PrefetchScalarGridSpec(
            num_scalar_prefetch=1,
            grid=(pairs // PP,),
            in_specs=[spec(win), spec(win), spec(win)],
            out_specs=[
                pl.BlockSpec((rows, PP * LANES), lambda p, *_: (0, p)),
                pl.BlockSpec((PP, blocks, 2 * QB), lambda p, *_: (p, 0, 0)),
            ],
            scratch_shapes=[pltpu.VMEM((rows, PP * LANES), f32), pltpu.SMEM((blocks * images,), jnp.int32)],
        ),
        out_shape=[
            jax.ShapeDtypeStruct((rows, pairs * LANES), bf16),
            jax.ShapeDtypeStruct((pairs, blocks, 2 * QB), f32),
        ],
        compiler_params=pltpu.CompilerParams(vmem_limit_bytes=VMEM, dimension_semantics=("arbitrary",)),
        cost_estimate=spent(5 * pairs),
        name="attention_forward",
    )(img, q, k, v)

def bwd_kernel(blocks, images, img_ref, q_ref, k_ref, v_ref, g_ref, lse_ref,
               dq_ref, dk_ref, dv_ref, left_ref, right_ref, dq_acc, dk_acc, dv_acc, items):
    rows = blocks * QB
    count = make_items(img_ref, items, blocks, images)
    dq_acc[...] = jnp.zeros_like(dq_acc)
    dk_acc[...] = jnp.zeros_like(dk_acc)
    dv_acc[...] = jnp.zeros_like(dv_acc)

    def body(n, carry):
        b, start, begin, row = item_scalars(img_ref, items, n)
        valid = key_valid(start, begin)
        qm = query_valid(start, row)
        done = []
        for u in range(PP):
            cols = slice(u * LANES, (u + 1) * LANES)
            q2 = halves(q_ref[pl.ds(pl.multiple_of(row + REACH, 16), QB), cols])
            g2 = halves(g_ref[pl.ds(row, QB), cols])
            kw = k_ref[pl.ds(begin, SPAN), cols]
            vw = v_ref[pl.ds(begin, SPAN), cols]
            lse = jnp.where(qm, lse_ref[u, pl.ds(b, 1), :], 1e30)
            s = lax.dot_general(kw, q2, (((1,), (1,)), ((), ())), preferred_element_type=f32)
            dp = lax.dot_general(vw, g2, (((1,), (1,)), ((), ())), preferred_element_type=f32)
            p = jnp.exp(jnp.where(valid, s, -1e30) - lse)
            inner = jnp.sum(p * dp, axis=0, keepdims=True)
            ds = (p * (dp - inner)).astype(bf16)
            dv = jnp.dot(p.astype(bf16), g2, preferred_element_type=f32)
            dk = jnp.dot(ds, q2, preferred_element_type=f32)
            dqt = lax.dot_general(kw, ds, (((0,), (0,)), ((), ())), preferred_element_type=f32)
            done.append((dv, dk, jnp.concatenate([dqt[:HEAD, :QB], dqt[HEAD:, QB:]], axis=0).T))
        for u in range(PP):
            cols = slice(u * LANES, (u + 1) * LANES)
            dv, dk, dq = done[u]
            dv_acc[pl.ds(begin, SPAN), cols] += dv
            dk_acc[pl.ds(begin, SPAN), cols] += dk
            dq_acc[pl.ds(row, QB), cols] += dq
        return carry

    lax.fori_loop(0, count, body, 0)
    pad = pad_rows(img_ref, images, rows)
    dq_ref[...] = (dq_acc[...] * 0.125).astype(bf16)
    dk_ref[...] = dk_acc[pl.ds(REACH, rows), :]
    for u in range(PP):
        cols = slice(u * LANES, (u + 1) * LANES)
        dv_ref[:, cols] = dv_acc[pl.ds(REACH, rows), cols] + jnp.where(pad, g_ref[:, cols].astype(f32), 0.0)
    left_ref[0] = dk_acc[pl.ds(0, REACH), :].astype(bf16)
    left_ref[1] = dv_acc[pl.ds(0, REACH), :].astype(bf16)
    right_ref[0] = dk_acc[pl.ds(REACH + rows, REACH), :].astype(bf16)
    right_ref[1] = dv_acc[pl.ds(REACH + rows, REACH), :].astype(bf16)

def attention_backward(img, q, k, v, g, lse, first, pairs):
    win = k.shape[0]
    rows = win - 2 * REACH
    blocks = rows // QB
    images = img.shape[0]
    C = PP * LANES
    spec = lambda r: pl.BlockSpec((r, C), lambda p, *_: (0, first // PP + p))
    out = lambda r: pl.BlockSpec((r, C), lambda p, *_: (0, p))
    edge = pl.BlockSpec((2, REACH, C), lambda p, *_: (0, 0, p))
    sds = jax.ShapeDtypeStruct
    cols = pairs * LANES
    return pl.pallas_call(
        functools.partial(bwd_kernel, blocks, images),
        grid_spec=pltpu.PrefetchScalarGridSpec(
            num_scalar_prefetch=1,
            grid=(pairs // PP,),
            in_specs=[spec(win), spec(win), spec(win), spec(rows),
                      pl.BlockSpec((PP, blocks, 2 * QB), lambda p, *_: (first // PP + p, 0, 0))],
            out_specs=[out(rows), out(rows), out(rows), edge, edge],
            scratch_shapes=[pltpu.VMEM((rows, C), f32), pltpu.VMEM((win, C), f32), pltpu.VMEM((win, C), f32),
                            pltpu.SMEM((blocks * images,), jnp.int32)],
        ),
        out_shape=[sds((rows, cols), bf16), sds((rows, cols), f32), sds((rows, cols), f32),
                   sds((2, REACH, cols), bf16), sds((2, REACH, cols), bf16)],
        compiler_params=pltpu.CompilerParams(vmem_limit_bytes=VMEM, dimension_semantics=("arbitrary",)),
        cost_estimate=spent(6.5 * pairs),
        name="attention_backward",
    )(img, q, k, v, g, lse)


FT = 512
ROWS = 256


def contract(a, b, dims):
    return lax.dot_general(a, b, (dims, ((), ())), preferred_element_type=f32)


def feed_kernel(
    table, home, normed, cot, middle, bias_final, wide, tall, bias_hidden,
    result, grad_normed, bias_grad, hidden_near, hidden_far, final_near, final_far,
    total, normed_t, final, active, grad_pre, hidden_grad, final_grad, sems,
):
    step = pl.program_id(0)
    tiles = pl.num_programs(0)
    slot = lax.rem(step, 2)
    rows, width = normed.shape
    half, piece, _ = hidden_near.shape
    devices = tall.shape[0] // 32
    depth = FT // devices

    @pl.when(step == 0)
    def _():
        total[...] = middle[...] + bias_final[...]
        grad_normed[...] = jnp.zeros_like(grad_normed)
        normed_t[...] = normed[...].T

    for d in range(devices):
        for i in range(4):
            final[d * depth + i * 32 : d * depth + (i + 1) * 32, :] = tall[d * 32 : (d + 1) * 32, i * width : (i + 1) * width]
    for r in range(0, rows, ROWS):
        cut = slice(r, r + ROWS)
        pre = contract(normed[cut, :], wide[...], ((1,), (0,))) + bias_hidden[...]
        grad = contract(cot[cut, :], final[...], ((1,), (1,)))
        phi = 0.5 + 0.5 * lax.erf(pre * (0.5**0.5))
        slope = phi + pre * jnp.exp(pre * pre * -0.5) * ((0.5 / math.pi) ** 0.5)
        active[cut, :] = (pre * phi).astype(bf16)
        grad_pre[cut, :] = (grad * slope).astype(bf16)
        total[cut, :] += contract(active[cut, :], final[...], ((1,), (0,)))
        grad_normed[cut, :] += contract(grad_pre[cut, :], wide[...], ((1,), (1,)))
    bias_grad[...] = jnp.sum(grad_pre[...].astype(f32), axis=0, keepdims=True)
    hidden_grad[...] = contract(normed_t[...], grad_pre[...], ((1,), (0,)))
    for place in range(2 * half):
        rows_of = hidden_grad[pl.ds(pl.multiple_of(table[place] * piece, piece), piece), :].astype(bf16)
        if place < half:
            hidden_near[place] = rows_of
        else:
            hidden_far[place - half] = rows_of

    def copy_out(slot, d, target):
        return pltpu.make_async_copy(final_grad.at[slot, d], target, sems.at[slot, d])

    def wait_out(slot):
        for d in range(devices):
            copy_out(slot, d, final_near.at[0]).wait()

    @pl.when(step >= 2)
    def _():
        wait_out(slot)

    final_grad[slot] = contract(active[...], cot[...], ((0,), (0,))).astype(bf16).reshape(devices, depth, width)
    for d in range(devices):
        at = home[step * devices + d]

        @pl.when(at < half)
        def _():
            copy_out(slot, d, final_near.at[at]).start()

        @pl.when(at >= half)
        def _():
            copy_out(slot, d, final_far.at[at - half]).start()

    @pl.when(step == tiles - 1)
    def _():
        result[...] = total[...].astype(bf16)
        wait_out(1 - slot)
        wait_out(slot)


def feed_forward(normed, cot, middle, bias_final, feed, bias_hidden, table, home):
    rows, width = normed.shape
    units = bias_hidden.shape[1]
    whole = lambda *shape: pl.BlockSpec(shape, lambda t, *_: (0,) * len(shape), pipeline_mode=pl.Buffered(1))
    sds = jax.ShapeDtypeStruct
    depth = units // PIECES
    devices = FT // depth
    line = pl.BlockSpec((1, FT), lambda t, *_: (0, t))
    square = whole(rows, width)
    wide_piece = sds((PIECES // 2, width // PIECES, units), bf16)
    tall_piece = sds((PIECES // 2, depth, width), bf16)
    edge = pl.BlockSpec((PIECES // 2, width // PIECES, FT), lambda t, *_: (0, 0, t))
    return pl.pallas_call(
        feed_kernel,
        grid_spec=pltpu.PrefetchScalarGridSpec(
            num_scalar_prefetch=2,
            grid=(units // FT,),
            in_specs=[
                square, square, square, whole(1, width),
                pl.BlockSpec((width, FT), lambda t, *_: (0, t)),
                pl.BlockSpec((devices * 32, 4 * width), lambda t, *_: (t, 1)),
                line,
            ],
            out_specs=[square, square, line, edge, edge] + [pl.BlockSpec(memory_space=pl.ANY)] * 2,
            scratch_shapes=[
                pltpu.VMEM((rows, width), f32), pltpu.VMEM((width, rows), bf16), pltpu.VMEM((FT, width), bf16),
                pltpu.VMEM((rows, FT), bf16), pltpu.VMEM((rows, FT), bf16), pltpu.VMEM((width, FT), f32),
                pltpu.VMEM((2, devices, depth, width), bf16), pltpu.SemaphoreType.DMA((2, devices)),
            ],
        ),
        out_shape=[
            sds((rows, width), bf16), sds((rows, width), f32), sds((1, units), f32),
            wide_piece, wide_piece, tall_piece, tall_piece,
        ],
        compiler_params=pltpu.CompilerParams(vmem_limit_bytes=VMEM, dimension_semantics=("arbitrary",)),
        cost_estimate=spent(70),
        name="feed_forward",
    )(table, home, normed, cot, middle, bias_final, feed, feed, bias_hidden)


def project_kernel(
    table_one, table_two, x, one_near, one_far, two_near, two_far,
    q_out, k_out, v_out, normed_out, weight, weight_out, vectors, small,
):
    half, piece, split = one_near.shape
    width = x.shape[1]
    wide = weight.shape[1]

    @pl.when(pl.program_id(0) == 0)
    def _():
        for place in range(2 * half):
            a, b, at = (one_near, two_near, place) if place < half else (one_far, two_far, place - half)
            rows = pl.ds(pl.multiple_of(table_one[place] * piece, piece), piece)
            weight[rows, :split] = a[at]
            rows = pl.ds(pl.multiple_of(table_two[place] * piece, piece), piece)
            weight[rows, split:] = b[at, :, : wide - split]
            weight_out[rows, :] = b[at, :, wide - split : wide - split + width]
            small[rows, :] = b[at, :, wide - split + width : wide - split + width + LANES].astype(f32)
        vectors[...] = small[...].T[: vectors.shape[0]]

    values = x[...].astype(f32)
    center = values - jnp.mean(values, axis=-1, keepdims=True)
    spread_of = jnp.mean(center * center, axis=-1, keepdims=True)
    normed = (center * lax.rsqrt(spread_of + norm_epsilon) * vectors[0:1, :] + vectors[1:2, :]).astype(bf16)
    normed_out[...] = normed
    cols = width // GROUPS
    for group in range(GROUPS):
        out = slice(group * cols, (group + 1) * cols)
        begin = 3 * group * cols
        product = [
            jnp.dot(normed, weight[:, begin + i * cols : begin + (i + 1) * cols], preferred_element_type=f32) for i in range(3)
        ]
        q_out[:, out] = (product[0] + vectors[2:3, out]).astype(bf16) * jnp.asarray(HEAD**-0.5, bf16)
        k_out[:, out] = product[1].astype(bf16)
        v_out[:, out] = (product[2] + vectors[3:4, out]).astype(bf16)


def project(window, one, two, tables):
    rows, width = window.shape
    half, piece, split = one[0].shape
    block = rows // 4
    whole = lambda *shape: pl.BlockSpec(shape, lambda t, *_: (0,) * len(shape), pipeline_mode=pl.Buffered(1))
    strip = pl.BlockSpec((block, width), lambda t, *_: (t, 0))
    sds = jax.ShapeDtypeStruct
    return pl.pallas_call(
        project_kernel,
        grid_spec=pltpu.PrefetchScalarGridSpec(
            num_scalar_prefetch=2,
            grid=(4,),
            in_specs=[strip] + [whole(half, piece, split)] * 2 + [whole(*two[0].shape)] * 2,
            out_specs=[strip] * 4 + [whole(width, 3 * width), whole(width, width), whole(16, width)],
            scratch_shapes=[pltpu.VMEM((width, LANES), f32)],
        ),
        out_shape=[sds((rows, width), bf16)] * 4 + [sds((width, 3 * width), bf16), sds((width, width), bf16), sds((16, width), f32)],
        compiler_params=pltpu.CompilerParams(vmem_limit_bytes=VMEM, dimension_semantics=("arbitrary",)),
        cost_estimate=spent(24),
        name="project",
    )(*tables, window, *one, *two)


CW = 256


def share_kernel(
    extra, table_one, table_two, normed, dq, dk, dv, left, right, *refs,
):
    mixed, branch = refs[:2] if extra else (None, None)
    packed, sums, near_one, far_one, near_two, far_two, normed_t, mixed_t, x = refs[2 if extra else 0 :]
    step = pl.program_id(0)
    steps = pl.num_programs(0)
    rows = dq.shape[0]
    half, piece, _ = near_one.shape
    per = dq.shape[1] // CW if dq.shape[1] > CW else None

    @pl.when(step == 0)
    def _():
        normed_t[...] = normed[pl.ds(REACH, rows), :].T

    def halo(own, number):
        x[...] = own[...].astype(bf16)
        edge = rows - REACH
        x[:edge, :] = (own[:edge, :] + left[number, :edge, :].astype(f32)).astype(bf16)
        x[edge:REACH, :] = (own[edge:REACH, :] + left[number, edge:, :].astype(f32) + right[number, : REACH - edge, :].astype(f32)).astype(bf16)
        x[REACH:, :] = (own[REACH:, :] + right[number, REACH - edge :, :].astype(f32)).astype(bf16)

    @pl.when(step < 2)
    def _():
        x[...] = dq[...]

    @pl.when((step >= 2) & (step < 4))
    def _():
        halo(dk, 0)

    @pl.when((step >= 4) & (step < 6))
    def _():
        halo(dv, 1)

    if extra:
        @pl.when(step == 6)
        def _():
            normed_t[...] = mixed[...].T

        @pl.when(step >= 6)
        def _():
            x[...] = branch[...]

    @pl.when(step < 6)
    def _():
        packed[...] = x[...]

    sums[...] = jnp.sum(x[...].astype(f32), axis=0, keepdims=True)
    mixed_t[...] = jnp.dot(normed_t[...], x[...], preferred_element_type=f32)

    def put(table, near, far):
        for place in range(2 * half):
            rows_of = mixed_t[pl.ds(pl.multiple_of(table[place] * piece, piece), piece), :].astype(bf16)
            if place < half:
                near[place] = rows_of
            else:
                far[place - half] = rows_of

    @pl.when(step < steps // 2)
    def _():
        put(table_one, near_one, far_one)

    @pl.when(step >= steps // 2)
    def _():
        put(table_two, near_two, far_two)


def weight_share(normed, dq, dk, dv, left, right, tables, extra=()):
    rows, cols = dq.shape
    win, width = normed.shape
    steps = 6 + (4 if extra else 0)
    whole = lambda *shape: pl.BlockSpec(shape, lambda t, *_: (0,) * len(shape), pipeline_mode=pl.Buffered(1))
    clip = lambda t, low, top: jnp.minimum(jnp.maximum(t - low, 0), top)
    tall = lambda low, top: pl.BlockSpec((rows, CW), lambda t, *_: (0, clip(t, low, top)))
    edge = pl.BlockSpec((2, REACH, CW), lambda t, *_: (0, 0, jnp.where(t < 4, clip(t, 2, 1), clip(t, 4, 1))))
    piece = lambda low, top: pl.BlockSpec((PIECES // 2, width // PIECES, CW), lambda t, *_: (0, 0, clip(t, low, top)))
    sds = jax.ShapeDtypeStruct
    hold = steps // 2
    pieces = sds((PIECES // 2, width // PIECES, hold * CW), bf16)
    return pl.pallas_call(
        functools.partial(share_kernel, bool(extra)),
        grid_spec=pltpu.PrefetchScalarGridSpec(
            num_scalar_prefetch=2,
            grid=(steps,),
            in_specs=[whole(win, width), tall(0, 1), tall(2, 1), tall(4, 1), edge, edge]
            + ([whole(rows, width), tall(6, 3)] if extra else []),
            out_specs=[tall(0, 5), pl.BlockSpec((1, CW), lambda t, *_: (0, t))]
            + [piece(0, hold - 1)] * 2 + [piece(hold, hold - 1)] * 2,
            scratch_shapes=[pltpu.VMEM((width, rows), bf16), pltpu.VMEM((width, CW), f32), pltpu.VMEM((rows, CW), bf16)],
        ),
        out_shape=[sds((rows, 6 * CW), bf16), sds((1, steps * CW), f32), pieces, pieces, pieces, pieces],
        compiler_params=pltpu.CompilerParams(vmem_limit_bytes=VMEM, dimension_semantics=("arbitrary",)),
        cost_estimate=spent(10 if extra else 7),
        name="weight_share",
    )(*tables, normed, dq, dk, dv, left, right, *extra)


def norm_backward(values, gain, grad):
    center = values - jnp.mean(values, axis=-1, keepdims=True)
    scale = lax.rsqrt(jnp.mean(center * center, axis=-1, keepdims=True) + norm_epsilon)
    unit = center * scale
    scaled = grad * gain
    moved = scaled - jnp.mean(scaled, axis=-1, keepdims=True) - unit * jnp.mean(scaled * unit, axis=-1, keepdims=True)
    column = lambda x: jnp.sum(x, axis=0, keepdims=True)
    return scale * moved, column(grad * unit), column(grad)


def branch_kernel(grad, middle, cot, weight_out, vectors, total, branch, mixed, sums):
    @pl.when(pl.program_id(0) == 0)
    def _():
        sums[...] = jnp.zeros_like(sums)

    up = cot[...].astype(f32)
    moved, gain_sum, bias_sum = norm_backward(middle[...], vectors[5:6, :], grad[...])
    total[...] = up + moved
    branch[...] = total[...].astype(bf16)
    mixed[...] = contract(branch[...], weight_out[...], ((1,), (1,))).astype(bf16)
    sums[0:1, :] += gain_sum
    sums[1:2, :] += bias_sum
    sums[2:3, :] += jnp.sum(up, axis=0, keepdims=True)


def input_kernel(one, two, weight, tokens, middle_grad, vectors, out, sums):
    @pl.when(pl.program_id(0) == 0)
    def _():
        sums[...] = jnp.zeros_like(sums)

    cols = one.shape[1]
    grad = contract(one[...], weight[:, :cols], ((1,), (1,))) + contract(two[...], weight[:, cols:], ((1,), (1,)))
    moved, gain_sum, bias_sum = norm_backward(tokens[...].astype(f32), vectors[0:1, :], grad)
    out[...] = (middle_grad[...] + moved).astype(bf16)
    sums[0:1, :] += gain_sum
    sums[1:2, :] += bias_sum


def row_blocks(kernel, name, blocked, whole, outs, us):
    rows, width = blocked[0].shape[0], outs[0][0]
    block = rows // 4
    strip = lambda cols: pl.BlockSpec((block, cols), lambda t: (t, 0))
    fixed = lambda *shape: pl.BlockSpec(shape, lambda t: (0,) * len(shape), pipeline_mode=pl.Buffered(1))
    return pl.pallas_call(
        kernel,
        grid=(4,),
        in_specs=[strip(a.shape[1]) for a in blocked] + [fixed(*a.shape) for a in whole],
        out_specs=[strip(cols) for cols, _ in outs] + [fixed(8, width)],
        out_shape=[jax.ShapeDtypeStruct((rows, cols), kind) for cols, kind in outs] + [jax.ShapeDtypeStruct((8, width), f32)],
        compiler_params=pltpu.CompilerParams(vmem_limit_bytes=VMEM, dimension_semantics=("arbitrary",)),
        cost_estimate=spent(us),
        name=name,
    )(*blocked, *whole)


def branch_gradient(grad, middle, cot, weight_out, vectors):
    width = middle.shape[1]
    outs = [(width, f32), (width, bf16), (width, bf16)]
    return row_blocks(branch_kernel, "branch_gradient", [grad, middle, cot], [weight_out, vectors], outs, 10)


def input_gradient(one, two, tokens, middle_grad, weight, vectors):
    def kernel(one, two, tokens, middle_grad, weight, vectors, out, sums):
        input_kernel(one, two, weight, tokens, middle_grad, vectors, out, sums)

    return row_blocks(kernel, "input_gradient", [one, two, tokens, middle_grad], [weight, vectors], [(tokens.shape[1], bf16)], 12)


def bit_orders(count):
    bits = [1 << i for i in range(count.bit_length() - 1)]
    return (bits[0], bits[2], bits[1], *bits[3:]), (bits[0], bits[1], bits[2], *bits[3:])


def exchange(x, bit, count):
    return lax.ppermute(x, "dev", [(i, i ^ bit) for i in range(count)])


def owners(order, me):
    table = []
    for place in range(PIECES):
        offset = 0
        for i, bit in enumerate(order):
            if (place >> (len(order) - 1 - i)) & 1:
                offset |= bit
        table.append(offset)
    return jnp.array(table, jnp.int32) ^ me


def gather_step(held, order, step, count):
    bit = order[len(order) - 1 - step]
    arrived = exchange(held, bit, count)
    return (held, arrived) if bit == order[0] else jnp.concatenate([held, arrived], axis=0)


def add_low(a, b):
    return (a.astype(f32) + b.astype(f32)).astype(bf16)


def near_whole(near, arrived):
    return add_low(near, arrived)


def add_halves(near, arrived):
    half = near.shape[0] // 2
    return add_low(near[:half], arrived[:half]), add_low(near[half:], arrived[half:])


near_halves = near_whole


def line_swap(held, order, count):
    near, middle, far = order[3], order[4], order[3] | order[4]
    return held[0], (exchange(held[2], near, count), exchange(held[1], middle, count), exchange(held[3], far, count))


def line_sum(own, parts):
    one, two, three = [p.astype(f32) for p in parts]
    return (own.astype(f32) + one) + (two + three)


def plane_swap(held, order, count):
    quarter = held.shape[0] // 4
    cut = lambda i: held[i * quarter : (i + 1) * quarter]
    bits = order[2], order[1], order[1] | order[2]
    return cut(0), [exchange(cut(i + 1), bit, count) for i, bit in enumerate(bits)]


def plane_sum(own, parts):
    one, two, three = [p.astype(f32) for p in parts]
    return ((own.astype(f32) + one) + (two + three)).astype(bf16)


def scatter_whole(near, far, count):
    whole = jnp.concatenate([near, far], axis=0).reshape(-1, near.shape[2])
    return lax.psum_scatter(whole.astype(f32), "dev", scatter_dimension=0, tiled=True)


def layer_norm(values, gain, bias):
    center = values - jnp.mean(values, axis=-1, keepdims=True)
    spread_of = jnp.mean(center * center, axis=-1, keepdims=True)
    return center * lax.rsqrt(spread_of + norm_epsilon) * gain + bias


def exact_gelu(values):
    return jax.nn.gelu(values, approximate=False)


def image_starts(segment_ids, me, rows):
    padded = jnp.pad(segment_ids, (REACH, REACH), constant_values=-2)
    window = lax.dynamic_slice_in_dim(padded, me * rows, rows + 2 * REACH, 0)
    own = window[REACH : REACH + rows]
    far = jnp.int32(1 << 20)
    first = jnp.min(jnp.where(own >= 0, own, far))
    places = jnp.arange(rows + 2 * REACH, dtype=jnp.int32)
    images = (rows - 2) // IMG + 2
    starts = []
    for i in range(images):
        start = jnp.min(jnp.where(window == first + i, places, far))
        starts.append(jnp.where(start == far, -far, start))
    return jnp.stack(starts)


def per_device(
    tokens,
    segment_ids,
    first_gain,
    first_bias,
    qkv_weight,
    query_bias,
    value_bias,
    out_weight,
    out_bias,
    second_gain,
    second_bias,
    hidden_weight,
    hidden_bias,
    final_weight,
    final_bias,
    cotangent,
):
    count = lax.axis_size("dev")
    me = lax.axis_index("dev")
    direct = count == PIECES
    rows, width = tokens.shape
    hidden_width = hidden_weight.shape[1]
    pairs = width // LANES
    part = width // count
    half = PIECES // 2
    unit = hidden_width // PIECES
    orders = bit_orders(PIECES)
    tables = [owners(order, me if direct else 0) for order in orders]
    homes = [jnp.argsort(table).astype(jnp.int32) for table in tables]
    sync = lax.optimization_barrier
    img = image_starts(segment_ids, me, rows)
    to_right = [(i, i + 1) for i in range(count - 1)]
    to_left = [(i + 1, i) for i in range(count - 1)]
    send = lambda left, right: (lax.ppermute(right, "dev", to_right), lax.ppermute(left, "dev", to_left))

    vectors = [first_gain, first_bias, query_bias, value_bias, out_bias, second_gain, second_bias, final_bias]
    small = jnp.concatenate([jnp.stack(vectors, axis=1), hidden_bias.reshape(part, -1)], axis=1).astype(bf16)
    small = jnp.pad(small, ((0, 0), (0, 2 * LANES - small.shape[1])))
    cols = width // GROUPS
    qkv_low = qkv_weight.astype(bf16)
    qkv_low = jnp.concatenate(
        [qkv_low[:, i * width + g * cols : i * width + (g + 1) * cols] for g in range(GROUPS) for i in range(3)], axis=1
    )
    split = 2 * width
    early = [qkv_low[:, :split], jnp.concatenate([qkv_low[:, split:], out_weight.astype(bf16), small], axis=1)]
    hidden_low = hidden_weight.astype(bf16)
    final_low = final_weight.astype(bf16)
    if direct:
        feed = jnp.concatenate([hidden_low] + [final_low[32 * i : 32 * (i + 1)] for i in range(4)], axis=1)
        held = [p[None] for p in early]
        halo = send(tokens[:REACH], tokens[rows - REACH :])
        lines = [[exchange(h, o[3], count), exchange(h, o[4], count), exchange(h, o[3] | o[4], count)] for h, o in zip(held, orders)]
        lines, held, halo = sync((lines, held, halo))
        held = [jnp.concatenate([h, line[1], line[0], line[2]], axis=0) for h, line in zip(held, lines)]
        held = [gather_step(h, o, 2, count) for h, o in zip(held, orders)]
        if FEED_AFTER == 2:
            held, feed = sync((held, feed))
        held = [gather_step(h, o, 3, count) for h, o in zip(held, orders)]
        if FEED_AFTER == 3:
            held, feed = sync((held, feed))
        held = [gather_step(h, o, 4, count) for h, o in zip(held, orders)]
        feed = lax.all_gather(feed, "dev", axis=0, tiled=True)
        one, two = held
    else:
        one, two = [jnp.split(lax.all_gather(p, "dev", axis=0, tiled=True).reshape(PIECES, width // PIECES, -1), 2) for p in early]
        hidden_low = lax.all_gather(hidden_low, "dev", axis=0, tiled=True)
        final_low = lax.all_gather(final_low, "dev", axis=0, tiled=True)
        final_low = final_low.reshape(PIECES, 4, 32, width).transpose(0, 2, 1, 3).reshape(width, 4 * width)
        feed = jnp.concatenate([hidden_low, final_low], axis=1)
        halo = send(tokens[:REACH], tokens[rows - REACH :])
    window = jnp.concatenate([halo[0], tokens, halo[1]], axis=0)
    inputs = tokens.astype(f32)
    queries, key_rows, value_rows, normed, weight_qkv, weight_out, vectors = project(window, one, two, tables)
    gain_one, bias_one, bias_query, bias_value, bias_out, gain_two, bias_two, bias_final = [vectors[i] for i in range(8)]
    bias_hidden = vectors[8 : 8 + hidden_width // width].T.reshape(1, hidden_width)
    mixed_low, totals = attention_forward(img, queries, key_rows, value_rows, 0, pairs)
    middle = inputs + (jnp.dot(mixed_low, weight_out, preferred_element_type=f32) + bias_out)
    normed_two = layer_norm(middle, gain_two, bias_two).astype(bf16)
    result, grad_normed_two, hidden_bias_grad, *grads = feed_forward(
        normed_two, cotangent, middle, bias_final[None], feed, bias_hidden, tables[0], homes[1]
    )
    grads = [grads[:2], grads[2:]]
    swap = lambda state, step: [exchange(far, o[step], count) for (_, far), o in zip(state, orders)]
    take = lambda state, arrived: [add_halves(near, a) for (near, _), a in zip(state, arrived)]
    step = pairs // GROUPS
    if direct:
        moving = swap(grads, 0)
    middle_grad, grad_branch, grad_mixed, sums_mid = branch_gradient(grad_normed_two, middle, cotangent, weight_out, vectors)
    if direct:
        grads, moving, grad_mixed = sync((grads, moving, grad_mixed))
        grads = take(grads, moving)
        grads, grad_mixed = sync((grads, grad_mixed))
        moving = swap(grads, 1)
    first = attention_backward(img, queries, key_rows, value_rows, grad_mixed, totals, 0, step)
    if direct:
        grad_mixed, first = sync((grad_mixed, first))
    halo = send(*first[3:])
    second = attention_backward(img, queries, key_rows, value_rows, grad_mixed, totals, step, step)
    if direct:
        moving, first, second, halo, normed, grad_branch = sync((moving, first, second, halo, normed, grad_branch))
        grads = take(grads, moving)
        grads, first, second, halo, normed, grad_branch = sync((grads, first, second, halo, normed, grad_branch))
        moving = swap(grads, 2)
    next_halo = send(*second[3:])
    packed_one, sums_one, *share_one = weight_share(normed, *first[:3], *halo, tables, (mixed_low, grad_branch))
    share_one = [share_one[:2], share_one[2:]]
    if direct:
        moving, grads, second, next_halo, normed, share_one = sync((moving, grads, second, next_halo, normed, share_one))
        lines = [line_swap(near_halves(near, a), order, count) for (near, _), a, order in zip(grads, moving, orders)]
        moving = swap(share_one, 0)
    packed_two, sums_two, *share_two = weight_share(normed, *second[:3], *next_halo, tables)
    share_two = [share_two[:2], share_two[2:]]
    if direct:
        moving, share_one, share_two, packed_one, packed_two = sync((moving, share_one, share_two, packed_one, packed_two))
        planes = [plane_swap(near_whole(near, a), order, count) for (near, _), a, order in zip(share_one, moving, orders)]
        moving = swap(share_two, 0)
    input_grad, sums_first = input_gradient(packed_one, packed_two, tokens, middle_grad, weight_qkv, vectors)
    pick = lambda i: jnp.concatenate([s[:, i * cols : (i + 1) * cols] for s in (sums_one, sums_two)], axis=1)
    sums = jnp.concatenate(
        [sums_first[:2], pick(0), pick(2), sums_one[:, 3 * cols :], sums_mid[:3], hidden_bias_grad.reshape(-1, width)], axis=0
    )
    if direct:
        lines, planes, share_two, moving, input_grad, sums = sync((lines, planes, share_two, moving, input_grad, sums))
        hidden_shard, final_shard = [line_sum(*line) for line in lines]
        lines = [line_swap(plane_sum(*plane), order, count) for plane, order in zip(planes, orders)]
        planes = [plane_swap(near_whole(near, a), order, count) for (near, _), a, order in zip(share_two, moving, orders)]
        parts = [exchange(sums, bit, count) for bit in range(1, 8)]
        lines, planes, sums, parts, hidden_shard, final_shard = sync((lines, planes, sums, parts, hidden_shard, final_shard))
        shards_one = jnp.concatenate([line_sum(*line) for line in lines], axis=1)
        lines = [line_swap(plane_sum(*plane), order, count) for plane, order in zip(planes, orders)]
        sums = functools.reduce(lambda a, b: a + b, parts, sums)
        parts = [exchange(sums, bit, count) for bit in (8, 16, 24)]
        shards_two = jnp.concatenate([line_sum(*line) for line in lines], axis=1)
        sums = sums + parts[0] + (parts[1] + parts[2])
    else:
        sums = lax.psum(sums, "dev")
        shards_one = jnp.concatenate([scatter_whole(*s, count) for s in share_one], axis=1)
        shards_two = jnp.concatenate([scatter_whole(*s, count) for s in share_two], axis=1)
        hidden_shard, final_shard = [scatter_whole(*s, count) for s in grads]
    out_shard = shards_one[:, 3 * cols :]
    qkv_shard = jnp.concatenate([h[:, i * cols : (i + 1) * cols] for i in range(3) for h in (shards_one, shards_two)], axis=1)
    own = lax.dynamic_slice_in_dim(sums[:8], me * part, part, 1)
    own_hidden = lax.dynamic_slice_in_dim(sums[8:].reshape(-1), me * hidden_bias.shape[0], hidden_bias.shape[0], 0)
    return (
        result,
        input_grad,
        own[0],
        own[1],
        qkv_shard,
        own[2],
        own[3],
        out_shard,
        own[4],
        own[5],
        own[6],
        hidden_shard,
        own_hidden,
        final_shard,
        own[7],
    )


def solution(mesh):
    split = P("dev", None)
    line = P("dev")
    return jax.shard_map(
        per_device,
        mesh=mesh,
        in_specs=(split, P(), line, line, split, line, line, split, line, line, line, split, line, split, line, split),
        out_specs=(split, split, line, line, split, line, line, split, line, line, line, split, line, split, line),
        check_vma=False,
    )
```

```python
import functools
import math

import jax
import jax.numpy as jnp
from jax import lax
from jax.experimental import pallas as pl
from jax.experimental.pallas import tpu as pltpu
from jax.sharding import PartitionSpec as P

IMG = 577
REACH = IMG - 1
HEAD = 64
SPAN = 592
LANES = 128
PP = 2
PIECES = 32
PACE = 1.0e5
FEED_AFTER = 2
GROUPS = 2
VMEM = 60 * 1024 * 1024
f32 = jnp.float32
bf16 = jnp.bfloat16

norm_epsilon = 1e-06


def spent(us):
    return pl.CostEstimate(flops=0, bytes_accessed=int(us * PACE), transcendentals=0)


FP = 4
SLOTS = 8
CHUNKS = (384, 256, 128)


def make_items(img_ref, lists, counts, rows, images):
    for kind in range(len(CHUNKS)):
        counts[kind] = 0

    def add(kind, first, begin, end, start):
        size = CHUNKS[kind]
        n = counts[kind]
        base = (kind * SLOTS + n) * 4
        lists[base] = jnp.minimum(first, rows - size)
        lists[base + 1] = jnp.maximum(first, begin)
        lists[base + 2] = jnp.minimum(first + size, end)
        lists[base + 3] = start
        counts[kind] = n + 1

    for i in range(images):
        start = img_ref[i]
        begin = jnp.maximum(start - REACH, 0)
        end = jnp.minimum(start - REACH + IMG, rows)
        low = (begin // 16) * 16
        left = jnp.where(end > begin, end - low, 0)

        @pl.when(left > 512)
        def _():
            add(0, low, begin, end, start)
            add(1, low + 384, begin, end, start)

        @pl.when((left > 384) & (left <= 512))
        def _():
            add(1, low, begin, end, start)
            add(1, low + 256, begin, end, start)

        @pl.when((left > 256) & (left <= 384))
        def _():
            add(0, low, begin, end, start)

        @pl.when((left > 128) & (left <= 256))
        def _():
            add(1, low, begin, end, start)

        @pl.when((left > 0) & (left <= 128))
        def _():
            add(2, low, begin, end, start)


def item_scalars(lists, kind, n):
    base = (kind * SLOTS + n) * 4
    start = lists[base + 3]
    begin = pl.multiple_of((start // 16) * 16, 16)
    return pl.multiple_of(lists[base], 16), lists[base + 1], lists[base + 2], start, begin


def halves(x):
    lane = lax.broadcasted_iota(jnp.int32, x.shape, 1)
    zero = jnp.zeros_like(x)
    return jnp.concatenate([jnp.where(lane < HEAD, x, zero), jnp.where(lane >= HEAD, x, zero)], axis=0)


def mask_keys(scores, start, begin):
    def masked(low, top):
        r = lax.broadcasted_iota(jnp.int32, (top - low, 1), 0) + (low + begin - start)
        return jnp.where((r >= 0) & (r < IMG), scores[low:top], -1e30)

    return jnp.concatenate([masked(0, 16), scores[16 : SPAN - 16], masked(SPAN - 16, SPAN)], axis=0)


def query_valid(size, row, low, top):
    lane = lax.broadcasted_iota(jnp.int32, (1, 2 * size), 1)
    pos = jnp.where(lane < size, lane, lane - size) + row
    return (pos >= low) & (pos < top)


def pad_rows(img_ref, images, rows):
    r = lax.broadcasted_iota(jnp.int32, (rows, LANES), 0) + REACH
    inside = jnp.zeros((rows, LANES), jnp.bool_)
    for i in range(images):
        start = img_ref[i]
        inside = inside | ((r >= start) & (r < start + IMG))
    return ~inside


def fwd_kernel(images, img_ref, q_ref, k_ref, v_ref, o_ref, lse_ref, acc, lists, counts):
    rows = acc.shape[0]
    make_items(img_ref, lists, counts, rows, images)
    acc[...] = jnp.zeros_like(acc)

    def body(kind, size, n, carry):
        row, low, top, start, begin = item_scalars(lists, kind, n)
        qm = query_valid(size, row, low, top)
        done = []
        for u in range(FP):
            cols = slice(u * LANES, (u + 1) * LANES)
            q2 = halves(q_ref[pl.ds(pl.multiple_of(row + REACH, 16), size), cols])
            kw = k_ref[pl.ds(begin, SPAN), cols]
            vw = v_ref[pl.ds(begin, SPAN), cols]
            s = lax.dot_general(kw, q2, (((1,), (1,)), ((), ())), preferred_element_type=f32)
            s = mask_keys(s, start, begin)
            m = jnp.max(s, axis=0, keepdims=True)
            e = jnp.exp(s - m)
            l = jnp.sum(e, axis=0, keepdims=True)
            ot = lax.dot_general(vw, e.astype(bf16), (((0,), (0,)), ((), ())), preferred_element_type=f32)
            ot = ot * jnp.where(qm, 1.0 / l, 0.0)
            done.append((jnp.concatenate([ot[:HEAD, :size], ot[HEAD:, size:]], axis=0).T, m + jnp.log(l)))
        for u in range(FP):
            cols = slice(u * LANES, (u + 1) * LANES)
            acc[pl.ds(row, size), cols] += done[u][0]
            lse_ref[u, pl.ds(kind * SLOTS + n, 1), : 2 * size] = done[u][1]
        return carry

    for kind, size in enumerate(CHUNKS):
        lax.fori_loop(0, counts[kind], functools.partial(body, kind, size), 0)
    pad = pad_rows(img_ref, images, rows)
    for u in range(FP):
        cols = slice(u * LANES, (u + 1) * LANES)
        own = v_ref[pl.ds(REACH, rows), cols].astype(f32)
        o_ref[:, cols] = jnp.where(pad, own, acc[:, cols]).astype(bf16)


def attention_forward(img, q, k, v, first, pairs):
    win = k.shape[0]
    rows = win - 2 * REACH
    images = img.shape[0]
    spec = lambda r: pl.BlockSpec((r, FP * LANES), lambda p, *_: (0, first // FP + p))
    return pl.pallas_call(
        functools.partial(fwd_kernel, images),
        grid_spec=pltpu.PrefetchScalarGridSpec(
            num_scalar_prefetch=1,
            grid=(pairs // FP,),
            in_specs=[spec(win), spec(win), spec(win)],
            out_specs=[
                pl.BlockSpec((rows, FP * LANES), lambda p, *_: (0, p)),
                pl.BlockSpec((FP, 3 * SLOTS, 2 * CHUNKS[0]), lambda p, *_: (p, 0, 0)),
            ],
            scratch_shapes=[
                pltpu.VMEM((rows, FP * LANES), f32), pltpu.SMEM((3 * SLOTS * 4,), jnp.int32), pltpu.SMEM((3,), jnp.int32)
            ],
        ),
        out_shape=[
            jax.ShapeDtypeStruct((rows, pairs * LANES), bf16),
            jax.ShapeDtypeStruct((pairs, 3 * SLOTS, 2 * CHUNKS[0]), f32),
        ],
        compiler_params=pltpu.CompilerParams(vmem_limit_bytes=VMEM, dimension_semantics=("arbitrary",)),
        cost_estimate=spent(5 * pairs),
        name="attention_forward",
    )(img, q, k, v)


def bwd_kernel(images, img_ref, q_ref, k_ref, v_ref, g_ref, lse_ref,
               dq_ref, dk_ref, dv_ref, left_ref, right_ref, dq_acc, dk_acc, dv_acc, lists, counts):
    rows = dq_acc.shape[0]
    make_items(img_ref, lists, counts, rows, images)
    dq_acc[...] = jnp.zeros_like(dq_acc)
    dk_acc[...] = jnp.zeros_like(dk_acc)
    dv_acc[...] = jnp.zeros_like(dv_acc)

    def body(kind, size, n, carry):
        row, low, top, start, begin = item_scalars(lists, kind, n)
        qm = query_valid(size, row, low, top)
        done = []
        for u in range(PP):
            cols = slice(u * LANES, (u + 1) * LANES)
            q2 = halves(q_ref[pl.ds(pl.multiple_of(row + REACH, 16), size), cols])
            g2 = halves(g_ref[pl.ds(row, size), cols])
            kw = k_ref[pl.ds(begin, SPAN), cols]
            vw = v_ref[pl.ds(begin, SPAN), cols]
            lse = jnp.where(qm, lse_ref[u, pl.ds(kind * SLOTS + n, 1), : 2 * size], 1e30)
            s = lax.dot_general(kw, q2, (((1,), (1,)), ((), ())), preferred_element_type=f32)
            dp = lax.dot_general(vw, g2, (((1,), (1,)), ((), ())), preferred_element_type=f32)
            p = jnp.exp(mask_keys(s, start, begin) - lse)
            inner = jnp.sum(p * dp, axis=0, keepdims=True)
            ds = (p * (dp - inner)).astype(bf16)
            dv = jnp.dot(p.astype(bf16), g2, preferred_element_type=f32)
            dk = jnp.dot(ds, q2, preferred_element_type=f32)
            dqt = lax.dot_general(kw, ds, (((0,), (0,)), ((), ())), preferred_element_type=f32)
            done.append((dv, dk, jnp.concatenate([dqt[:HEAD, :size], dqt[HEAD:, size:]], axis=0).T))
        for u in range(PP):
            cols = slice(u * LANES, (u + 1) * LANES)
            dv, dk, dq = done[u]
            dv_acc[pl.ds(begin, SPAN), cols] += dv
            dk_acc[pl.ds(begin, SPAN), cols] += dk
            dq_acc[pl.ds(row, size), cols] += dq
        return carry

    for kind, size in enumerate(CHUNKS):
        lax.fori_loop(0, counts[kind], functools.partial(body, kind, size), 0)
    pad = pad_rows(img_ref, images, rows)
    dq_ref[...] = (dq_acc[...] * 0.125).astype(bf16)
    dk_ref[...] = dk_acc[pl.ds(REACH, rows), :]
    for u in range(PP):
        cols = slice(u * LANES, (u + 1) * LANES)
        dv_ref[:, cols] = dv_acc[pl.ds(REACH, rows), cols] + jnp.where(pad, g_ref[:, cols].astype(f32), 0.0)
    left_ref[0] = dk_acc[pl.ds(0, REACH), :].astype(bf16)
    left_ref[1] = dv_acc[pl.ds(0, REACH), :].astype(bf16)
    right_ref[0] = dk_acc[pl.ds(REACH + rows, REACH), :].astype(bf16)
    right_ref[1] = dv_acc[pl.ds(REACH + rows, REACH), :].astype(bf16)


def attention_backward(img, q, k, v, g, lse, first, pairs):
    win = k.shape[0]
    rows = win - 2 * REACH
    images = img.shape[0]
    C = PP * LANES
    spec = lambda r: pl.BlockSpec((r, C), lambda p, *_: (0, first // PP + p))
    out = lambda r: pl.BlockSpec((r, C), lambda p, *_: (0, p))
    edge = pl.BlockSpec((2, REACH, C), lambda p, *_: (0, 0, p))
    sds = jax.ShapeDtypeStruct
    cols = pairs * LANES
    return pl.pallas_call(
        functools.partial(bwd_kernel, images),
        grid_spec=pltpu.PrefetchScalarGridSpec(
            num_scalar_prefetch=1,
            grid=(pairs // PP,),
            in_specs=[spec(win), spec(win), spec(win), spec(rows),
                      pl.BlockSpec((PP, 3 * SLOTS, 2 * CHUNKS[0]), lambda p, *_: (first // PP + p, 0, 0))],
            out_specs=[out(rows), out(rows), out(rows), edge, edge],
            scratch_shapes=[pltpu.VMEM((rows, C), f32), pltpu.VMEM((win, C), f32), pltpu.VMEM((win, C), f32),
                            pltpu.SMEM((3 * SLOTS * 4,), jnp.int32), pltpu.SMEM((3,), jnp.int32)],
        ),
        out_shape=[sds((rows, cols), bf16), sds((rows, cols), f32), sds((rows, cols), f32),
                   sds((2, REACH, cols), bf16), sds((2, REACH, cols), bf16)],
        compiler_params=pltpu.CompilerParams(vmem_limit_bytes=VMEM, dimension_semantics=("arbitrary",)),
        cost_estimate=spent(6.5 * pairs),
        name="attention_backward",
    )(img, q, k, v, g, lse)


FT = 512
ROWS = 1024


def contract(a, b, dims):
    return lax.dot_general(a, b, (dims, ((), ())), preferred_element_type=f32)


def feed_kernel(
    table, home, normed, cot, middle, bias_final, wide, tall, bias_hidden,
    result, grad_normed, bias_grad, hidden_near, hidden_far, final_near, final_far,
    total, normed_t, final, active, grad_pre, hidden_grad, final_grad, sems,
):
    step = pl.program_id(0)
    tiles = pl.num_programs(0)
    slot = lax.rem(step, 2)
    rows, width = normed.shape
    half, _, piece, _ = hidden_near.shape
    devices = tall.shape[0] // 32
    depth = FT // devices

    @pl.when(step == 0)
    def _():
        total[...] = middle[...] + bias_final[...]
        grad_normed[...] = jnp.zeros_like(grad_normed)
        normed_t[...] = normed[...].T

    for d in range(devices):
        for i in range(4):
            final[d * depth + i * 32 : d * depth + (i + 1) * 32, :] = tall[d * 32 : (d + 1) * 32, i * width : (i + 1) * width]
    for r in range(0, rows, ROWS):
        cut = slice(r, r + ROWS)
        pre = contract(normed[cut, :], wide[...], ((1,), (0,))) + bias_hidden[...]
        grad = contract(cot[cut, :], final[...], ((1,), (1,)))
        phi = 0.5 + 0.5 * lax.erf(pre * (0.5**0.5))
        slope = phi + pre * jnp.exp(pre * pre * -0.5) * ((0.5 / math.pi) ** 0.5)
        active[cut, :] = (pre * phi).astype(bf16)
        grad_pre[cut, :] = (grad * slope).astype(bf16)
        total[cut, :] += contract(active[cut, :], final[...], ((1,), (0,)))
        grad_normed[cut, :] += contract(grad_pre[cut, :], wide[...], ((1,), (1,)))
    bias_grad[...] = jnp.sum(grad_pre[...].astype(f32), axis=0, keepdims=True)
    hidden_grad[...] = contract(normed_t[...], grad_pre[...], ((1,), (0,)))
    for place in range(2 * half):
        rows_of = hidden_grad[pl.ds(pl.multiple_of(table[place] * piece, piece), piece), :].astype(bf16)
        if place < half:
            hidden_near[place, 0] = rows_of
        else:
            hidden_far[place - half, 0] = rows_of

    def copy_out(slot, d, target):
        return pltpu.make_async_copy(final_grad.at[slot, d], target, sems.at[slot, d])

    def wait_out(slot):
        for d in range(devices):
            copy_out(slot, d, final_near.at[0]).wait()

    @pl.when(step >= 2)
    def _():
        wait_out(slot)

    final_grad[slot] = contract(active[...], cot[...], ((0,), (0,))).astype(bf16).reshape(devices, depth, width)
    for d in range(devices):
        at = home[step * devices + d]

        @pl.when(at < half)
        def _():
            copy_out(slot, d, final_near.at[at]).start()

        @pl.when(at >= half)
        def _():
            copy_out(slot, d, final_far.at[at - half]).start()

    @pl.when(step == tiles - 1)
    def _():
        result[...] = total[...].astype(bf16)
        wait_out(1 - slot)
        wait_out(slot)


def feed_forward(normed, cot, middle, bias_final, feed, bias_hidden, table, home):
    rows, width = normed.shape
    units = bias_hidden.shape[1]
    whole = lambda *shape: pl.BlockSpec(shape, lambda t, *_: (0,) * len(shape), pipeline_mode=pl.Buffered(1))
    sds = jax.ShapeDtypeStruct
    depth = units // PIECES
    devices = FT // depth
    line = pl.BlockSpec((1, FT), lambda t, *_: (0, t))
    square = whole(rows, width)
    wide_piece = sds((PIECES // 2, units // width, width // PIECES, width), bf16)
    tall_piece = sds((PIECES // 2, depth, width), bf16)
    blocks = width // FT
    edge = pl.BlockSpec((PIECES // 2, 1, width // PIECES, FT), lambda t, *_: (0, t // blocks, 0, t % blocks))
    return pl.pallas_call(
        feed_kernel,
        grid_spec=pltpu.PrefetchScalarGridSpec(
            num_scalar_prefetch=2,
            grid=(units // FT,),
            in_specs=[
                square, square, square, whole(1, width),
                pl.BlockSpec((width, FT), lambda t, *_: (0, t)),
                pl.BlockSpec((devices * 32, 4 * width), lambda t, *_: (t, 1)),
                line,
            ],
            out_specs=[square, square, line, edge, edge] + [pl.BlockSpec(memory_space=pl.ANY)] * 2,
            scratch_shapes=[
                pltpu.VMEM((rows, width), f32), pltpu.VMEM((width, rows), bf16), pltpu.VMEM((FT, width), bf16),
                pltpu.VMEM((rows, FT), bf16), pltpu.VMEM((rows, FT), bf16), pltpu.VMEM((width, FT), f32),
                pltpu.VMEM((2, devices, depth, width), bf16), pltpu.SemaphoreType.DMA((2, devices)),
            ],
        ),
        out_shape=[
            sds((rows, width), bf16), sds((rows, width), f32), sds((1, units), f32),
            wide_piece, wide_piece, tall_piece, tall_piece,
        ],
        compiler_params=pltpu.CompilerParams(vmem_limit_bytes=VMEM, dimension_semantics=("arbitrary",)),
        cost_estimate=spent(70),
        name="feed_forward",
    )(table, home, normed, cot, middle, bias_final, feed, feed, bias_hidden)


def project_kernel(
    table_one, table_two, x, one_near, one_far, two_near, two_far,
    q_out, k_out, v_out, normed_out, weight, weight_out, vectors, small,
):
    half, piece, split = one_near.shape
    width = x.shape[1]
    wide = weight.shape[1]

    @pl.when(pl.program_id(0) == 0)
    def _():
        for place in range(2 * half):
            a, b, at = (one_near, two_near, place) if place < half else (one_far, two_far, place - half)
            rows = pl.ds(pl.multiple_of(table_one[place] * piece, piece), piece)
            weight[rows, :split] = a[at]
            rows = pl.ds(pl.multiple_of(table_two[place] * piece, piece), piece)
            weight[rows, split:] = b[at, :, : wide - split]
            weight_out[rows, :] = b[at, :, wide - split : wide - split + width]
            small[rows, :] = b[at, :, wide - split + width : wide - split + width + LANES].astype(f32)
        vectors[...] = small[...].T[: vectors.shape[0]]

    values = x[...].astype(f32)
    center = values - jnp.mean(values, axis=-1, keepdims=True)
    spread_of = jnp.mean(center * center, axis=-1, keepdims=True)
    normed = (center * lax.rsqrt(spread_of + norm_epsilon) * vectors[0:1, :] + vectors[1:2, :]).astype(bf16)
    normed_out[...] = normed
    cols = width // GROUPS
    needs_queries = (pl.program_id(0) == 1) | (pl.program_id(0) == 2)
    for group in range(GROUPS):
        out = slice(group * cols, (group + 1) * cols)
        begin = 3 * group * cols
        keys = jnp.dot(normed, weight[:, begin + cols : begin + 2 * cols], preferred_element_type=f32)
        values = jnp.dot(normed, weight[:, begin + 2 * cols : begin + 3 * cols], preferred_element_type=f32)
        k_out[:, out] = keys.astype(bf16)
        v_out[:, out] = (values + vectors[3:4, out]).astype(bf16)

        @pl.when(needs_queries)
        def _():
            queries = jnp.dot(normed, weight[:, begin : begin + cols], preferred_element_type=f32)
            q_out[:, out] = (queries + vectors[2:3, out]).astype(bf16) * jnp.asarray(HEAD**-0.5, bf16)


def project(window, one, two, tables):
    rows, width = window.shape
    half, piece, split = one[0].shape
    block = rows // 4
    whole = lambda *shape: pl.BlockSpec(shape, lambda t, *_: (0,) * len(shape), pipeline_mode=pl.Buffered(1))
    strip = pl.BlockSpec((block, width), lambda t, *_: (t, 0))
    sds = jax.ShapeDtypeStruct
    return pl.pallas_call(
        project_kernel,
        grid_spec=pltpu.PrefetchScalarGridSpec(
            num_scalar_prefetch=2,
            grid=(4,),
            in_specs=[strip] + [whole(half, piece, split)] * 2 + [whole(*two[0].shape)] * 2,
            out_specs=[strip] * 4 + [whole(width, 3 * width), whole(width, width), whole(16, width)],
            scratch_shapes=[pltpu.VMEM((width, LANES), f32)],
        ),
        out_shape=[sds((rows, width), bf16)] * 4 + [sds((width, 3 * width), bf16), sds((width, width), bf16), sds((16, width), f32)],
        compiler_params=pltpu.CompilerParams(vmem_limit_bytes=VMEM, dimension_semantics=("arbitrary",)),
        cost_estimate=spent(24),
        name="project",
    )(*tables, window, *one, *two)


CW = 256


def share_kernel(
    extra, table, normed, dq, dk, dv, left, right, *refs,
):
    mixed, branch = refs[:2] if extra else (None, None)
    packed, sums, near, far, normed_t, product, x = refs[2 if extra else 0 :]
    step = pl.program_id(0)
    rows = dq.shape[0]
    half, piece, _ = near.shape

    @pl.when(step == 0)
    def _():
        normed_t[...] = normed[pl.ds(REACH, rows), :].T

    def halo(own, number):
        x[...] = own[...].astype(bf16)
        edge = rows - REACH
        x[:edge, :] = (own[:edge, :] + left[number, :edge, :].astype(f32)).astype(bf16)
        x[edge:REACH, :] = (own[edge:REACH, :] + left[number, edge:, :].astype(f32) + right[number, : REACH - edge, :].astype(f32)).astype(bf16)
        x[REACH:, :] = (own[REACH:, :] + right[number, REACH - edge :, :].astype(f32)).astype(bf16)

    @pl.when(step < 2)
    def _():
        x[...] = dq[...]

    @pl.when((step >= 2) & (step < 4))
    def _():
        halo(dk, 0)

    @pl.when((step >= 4) & (step < 6))
    def _():
        halo(dv, 1)

    if extra:
        @pl.when(step == 6)
        def _():
            normed_t[...] = mixed[...].T

        @pl.when(step >= 6)
        def _():
            x[...] = branch[...]

    @pl.when(step < 6)
    def _():
        packed[...] = x[...]

    sums[...] = jnp.sum(x[...].astype(f32), axis=0, keepdims=True)
    product[...] = jnp.dot(normed_t[...], x[...], preferred_element_type=f32)
    for place in range(2 * half):
        rows_of = product[pl.ds(pl.multiple_of(table[place] * piece, piece), piece), :].astype(bf16)
        if place < half:
            near[place] = rows_of
        else:
            far[place - half] = rows_of


def weight_share(normed, dq, dk, dv, left, right, table, extra=()):
    rows, cols = dq.shape
    win, width = normed.shape
    steps = 6 + (4 if extra else 0)
    whole = lambda *shape: pl.BlockSpec(shape, lambda t, *_: (0,) * len(shape), pipeline_mode=pl.Buffered(1))
    clip = lambda t, low, top: jnp.minimum(jnp.maximum(t - low, 0), top)
    tall = lambda low, top: pl.BlockSpec((rows, CW), lambda t, *_: (0, clip(t, low, top)))
    edge = pl.BlockSpec((2, REACH, CW), lambda t, *_: (0, 0, jnp.where(t < 4, clip(t, 2, 1), clip(t, 4, 1))))
    piece = pl.BlockSpec((PIECES // 2, width // PIECES, CW), lambda t, *_: (0, 0, t))
    sds = jax.ShapeDtypeStruct
    pieces = sds((PIECES // 2, width // PIECES, steps * CW), bf16)
    return pl.pallas_call(
        functools.partial(share_kernel, bool(extra)),
        grid_spec=pltpu.PrefetchScalarGridSpec(
            num_scalar_prefetch=1,
            grid=(steps,),
            in_specs=[whole(win, width), tall(0, 1), tall(2, 1), tall(4, 1), edge, edge]
            + ([whole(rows, width), tall(6, 3)] if extra else []),
            out_specs=[tall(0, 5), pl.BlockSpec((1, CW), lambda t, *_: (0, t))]
            + [piece] * 2,
            scratch_shapes=[pltpu.VMEM((width, rows), bf16), pltpu.VMEM((width, CW), f32), pltpu.VMEM((rows, CW), bf16)],
        ),
        out_shape=[sds((rows, 6 * CW), bf16), sds((1, steps * CW), f32), pieces, pieces],
        compiler_params=pltpu.CompilerParams(vmem_limit_bytes=VMEM, dimension_semantics=("arbitrary",)),
        cost_estimate=spent(10 if extra else 7),
        name="weight_share",
    )(table, normed, dq, dk, dv, left, right, *extra)


def norm_backward(values, gain, grad):
    center = values - jnp.mean(values, axis=-1, keepdims=True)
    scale = lax.rsqrt(jnp.mean(center * center, axis=-1, keepdims=True) + norm_epsilon)
    unit = center * scale
    scaled = grad * gain
    moved = scaled - jnp.mean(scaled, axis=-1, keepdims=True) - unit * jnp.mean(scaled * unit, axis=-1, keepdims=True)
    column = lambda x: jnp.sum(x, axis=0, keepdims=True)
    return scale * moved, column(grad * unit), column(grad)


def branch_kernel(grad, middle, cot, weight_out, vectors, total, branch, mixed, sums):
    @pl.when(pl.program_id(0) == 0)
    def _():
        sums[...] = jnp.zeros_like(sums)

    up = cot[...].astype(f32)
    moved, gain_sum, bias_sum = norm_backward(middle[...], vectors[5:6, :], grad[...])
    total[...] = up + moved
    branch[...] = total[...].astype(bf16)
    mixed[...] = contract(branch[...], weight_out[...], ((1,), (1,))).astype(bf16)
    sums[0:1, :] += gain_sum
    sums[1:2, :] += bias_sum
    sums[2:3, :] += jnp.sum(up, axis=0, keepdims=True)


def input_kernel(one, two, weight, tokens, middle_grad, vectors, out, sums):
    @pl.when(pl.program_id(0) == 0)
    def _():
        sums[...] = jnp.zeros_like(sums)

    cols = one.shape[1]
    grad = contract(one[...], weight[:, :cols], ((1,), (1,))) + contract(two[...], weight[:, cols:], ((1,), (1,)))
    moved, gain_sum, bias_sum = norm_backward(tokens[...].astype(f32), vectors[0:1, :], grad)
    out[...] = (middle_grad[...] + moved).astype(bf16)
    sums[0:1, :] += gain_sum
    sums[1:2, :] += bias_sum


def row_blocks(kernel, name, blocked, whole, outs, us):
    rows, width = blocked[0].shape[0], outs[0][0]
    block = rows // 4
    strip = lambda cols: pl.BlockSpec((block, cols), lambda t: (t, 0))
    fixed = lambda *shape: pl.BlockSpec(shape, lambda t: (0,) * len(shape), pipeline_mode=pl.Buffered(1))
    return pl.pallas_call(
        kernel,
        grid=(4,),
        in_specs=[strip(a.shape[1]) for a in blocked] + [fixed(*a.shape) for a in whole],
        out_specs=[strip(cols) for cols, _ in outs] + [fixed(8, width)],
        out_shape=[jax.ShapeDtypeStruct((rows, cols), kind) for cols, kind in outs] + [jax.ShapeDtypeStruct((8, width), f32)],
        compiler_params=pltpu.CompilerParams(vmem_limit_bytes=VMEM, dimension_semantics=("arbitrary",)),
        cost_estimate=spent(us),
        name=name,
    )(*blocked, *whole)


def branch_gradient(grad, middle, cot, weight_out, vectors):
    width = middle.shape[1]
    outs = [(width, f32), (width, bf16), (width, bf16)]
    return row_blocks(branch_kernel, "branch_gradient", [grad, middle, cot], [weight_out, vectors], outs, 10)


def input_gradient(one, two, tokens, middle_grad, weight, vectors):
    def kernel(one, two, tokens, middle_grad, weight, vectors, out, sums):
        input_kernel(one, two, weight, tokens, middle_grad, vectors, out, sums)

    return row_blocks(kernel, "input_gradient", [one, two, tokens, middle_grad], [weight, vectors], [(tokens.shape[1], bf16)], 12)


def bit_orders(count):
    bits = [1 << i for i in range(count.bit_length() - 1)]
    return (bits[0], bits[2], bits[1], *bits[3:]), (bits[0], bits[1], bits[2], *bits[3:])


def exchange(x, bit, count):
    return lax.ppermute(x, "dev", [(i, i ^ bit) for i in range(count)])


def owners(order, me):
    table = []
    for place in range(PIECES):
        offset = 0
        for i, bit in enumerate(order):
            if (place >> (len(order) - 1 - i)) & 1:
                offset |= bit
        table.append(offset)
    return jnp.array(table, jnp.int32) ^ me


def places(order, me):
    offset = jnp.arange(PIECES, dtype=jnp.int32) ^ me
    return sum(jnp.where(offset & bit != 0, 1 << (len(order) - 1 - i), 0) for i, bit in enumerate(order)).astype(jnp.int32)


def gather_step(held, order, step, count):
    bit = order[len(order) - 1 - step]
    arrived = exchange(held, bit, count)
    return (held, arrived) if bit == order[0] else jnp.concatenate([held, arrived], axis=0)


def total(parts, kind=bf16):
    return functools.reduce(lambda a, b: a + b, [p.astype(f32) for p in parts]).astype(kind)


def straight(parts, bits, count):
    size = parts[0].shape[0] // (len(bits) + 1)
    return [exchange(total([p[(i + 1) * size : (i + 2) * size] for p in parts]), bit, count) for i, bit in enumerate(bits)]


def scatter_whole(near, far, count):
    whole = jnp.concatenate([near, far], axis=0).reshape(-1, near.shape[2])
    return lax.psum_scatter(whole.astype(f32), "dev", scatter_dimension=0, tiled=True)


def layer_norm(values, gain, bias):
    center = values - jnp.mean(values, axis=-1, keepdims=True)
    spread_of = jnp.mean(center * center, axis=-1, keepdims=True)
    return center * lax.rsqrt(spread_of + norm_epsilon) * gain + bias


def exact_gelu(values):
    return jax.nn.gelu(values, approximate=False)


def image_starts(segment_ids, me, rows):
    padded = jnp.pad(segment_ids, (REACH, REACH), constant_values=-2)
    window = lax.dynamic_slice_in_dim(padded, me * rows, rows + 2 * REACH, 0)
    own = window[REACH : REACH + rows]
    far = jnp.int32(1 << 20)
    first = jnp.min(jnp.where(own >= 0, own, far))
    places = jnp.arange(rows + 2 * REACH, dtype=jnp.int32)
    images = (rows - 2) // IMG + 2
    starts = []
    for i in range(images):
        start = jnp.min(jnp.where(window == first + i, places, far))
        starts.append(jnp.where(start == far, -far, start))
    return jnp.stack(starts)


def per_device(
    tokens,
    segment_ids,
    first_gain,
    first_bias,
    qkv_weight,
    query_bias,
    value_bias,
    out_weight,
    out_bias,
    second_gain,
    second_bias,
    hidden_weight,
    hidden_bias,
    final_weight,
    final_bias,
    cotangent,
):
    count = lax.axis_size("dev")
    me = lax.axis_index("dev")
    direct = count == PIECES
    rows, width = tokens.shape
    hidden_width = hidden_weight.shape[1]
    pairs = width // LANES
    part = width // count
    part_rows = width // PIECES
    half = PIECES // 2
    unit = hidden_width // PIECES
    orders = bit_orders(PIECES)
    tables = [owners(order, me if direct else 0) for order in orders]
    home = places(orders[1], me if direct else 0)
    sync = lax.optimization_barrier
    img = image_starts(segment_ids, me, rows)
    to_right = [(i, i + 1) for i in range(count - 1)]
    to_left = [(i + 1, i) for i in range(count - 1)]
    send = lambda left, right: (lax.ppermute(right, "dev", to_right), lax.ppermute(left, "dev", to_left))

    vectors = [first_gain, first_bias, query_bias, value_bias, out_bias, second_gain, second_bias, final_bias]
    small = sync(jnp.concatenate([jnp.stack(vectors, axis=1), hidden_bias.reshape(part, -1)], axis=1)).astype(bf16)
    small = jnp.pad(small, ((0, 0), (0, LANES - small.shape[1])))
    cols = width // GROUPS
    qkv_low = qkv_weight.astype(bf16)
    qkv_low = jnp.concatenate(
        [qkv_low[:, i * width + g * cols : i * width + (g + 1) * cols] for g in range(GROUPS) for i in range(3)], axis=1
    )
    split = 2 * width
    early = jnp.concatenate([qkv_low, out_weight.astype(bf16), small], axis=1)
    hidden_low = hidden_weight.astype(bf16)
    final_low = final_weight.astype(bf16)
    if direct:
        feed = jnp.concatenate([hidden_low] + [final_low[32 * i : 32 * (i + 1)] for i in range(4)], axis=1)
        halo = send(tokens[:REACH], tokens[rows - REACH :])
        line = [exchange(early[None], bit, count) for bit in (orders[0][4], orders[0][3], orders[0][3] | orders[0][4])]
        line, halo, feed = sync((line, halo, feed)) if FEED_AFTER == 1 else (*sync((line, halo)), feed)
        held = [jnp.concatenate([p[..., cut] for p in (early[None], *line)], axis=0) for cut in (slice(0, split), slice(split, None))]
        held = [gather_step(h, o, 2, count) for h, o in zip(held, orders)]
        if FEED_AFTER == 2:
            held, feed = sync((held, feed))
        held = [gather_step(h, o, 3, count) for h, o in zip(held, orders)]
        if FEED_AFTER == 3:
            held, feed = sync((held, feed))
        held = [gather_step(h, o, 4, count) for h, o in zip(held, orders)]
        feed = lax.all_gather(feed, "dev", axis=0, tiled=True)
        one, two = held
    else:
        early = lax.all_gather(early, "dev", axis=0, tiled=True).reshape(PIECES, width // PIECES, -1)
        one, two = [jnp.split(p, 2) for p in (early[..., :split], early[..., split:])]
        hidden_low = lax.all_gather(hidden_low, "dev", axis=0, tiled=True)
        final_low = lax.all_gather(final_low, "dev", axis=0, tiled=True)
        final_low = final_low.reshape(PIECES, 4, 32, width).transpose(0, 2, 1, 3).reshape(width, 4 * width)
        feed = jnp.concatenate([hidden_low, final_low], axis=1)
        halo = send(tokens[:REACH], tokens[rows - REACH :])
    window = jnp.concatenate([halo[0], tokens, halo[1]], axis=0)
    inputs = tokens.astype(f32)
    queries, key_rows, value_rows, normed, weight_qkv, weight_out, vectors = project(window, one, two, tables)
    gain_one, bias_one, bias_query, bias_value, bias_out, gain_two, bias_two, bias_final = [vectors[i] for i in range(8)]
    bias_hidden = vectors[8 : 8 + hidden_width // width].T.reshape(1, hidden_width)
    mixed_low, totals = attention_forward(img, queries, key_rows, value_rows, 0, pairs)
    middle = inputs + (jnp.dot(mixed_low, weight_out, preferred_element_type=f32) + bias_out)
    normed_two = layer_norm(middle, gain_two, bias_two).astype(bf16)
    result, grad_normed_two, hidden_bias_grad, *grads = feed_forward(
        normed_two, cotangent, middle, bias_final[None], feed, bias_hidden, tables[0], home
    )
    grads = [[g.reshape(g.shape[0], -1, part_rows, width) for g in grads[i : i + 2]] for i in (0, 2)]
    step = pairs // GROUPS
    if direct:
        got = [[near, exchange(far, order[0], count)] for (near, far), order in zip(grads, orders)]
    middle_grad, grad_branch, grad_mixed, sums_mid = branch_gradient(grad_normed_two, middle, cotangent, weight_out, vectors)
    if direct:
        got, grad_mixed = sync((got, grad_mixed))
        away = [total([p[8:] for p in parts]) for parts in got]
        away, grad_mixed = sync((away, grad_mixed))
        moving = [exchange(a, order[1], count) for a, order in zip(away, orders)]
    first = attention_backward(img, queries, key_rows, value_rows, grad_mixed, totals, 0, step)
    if direct:
        grad_mixed, first = sync((grad_mixed, first))
    halo = send(*first[3:])
    second = attention_backward(img, queries, key_rows, value_rows, grad_mixed, totals, step, step)
    if direct:
        moving, first, second, halo, normed, grad_branch = sync((moving, first, second, halo, normed, grad_branch))
        got = [parts + [m] for parts, m in zip(got, moving)]
        away = [total([p[4:8] for p in parts]) for parts in got]
        away, first, second, halo, normed, grad_branch = sync((away, first, second, halo, normed, grad_branch))
        moving = [exchange(a, order[2], count) for a, order in zip(away, orders)]
    next_halo = send(*second[3:])
    packed_one, sums_one, *share_one = weight_share(normed, *first[:3], *halo, tables[0], (mixed_low, grad_branch))
    if direct:
        moving, second, next_halo, normed, share_one = sync((moving, second, next_halo, normed, share_one))
        got = [parts + [m] for parts, m in zip(got, moving)]
        away = jnp.concatenate([total([p[2:4] for p in parts]) for parts in got], axis=0)
        away, second, next_halo, normed, share_one = sync((away, second, next_halo, normed, share_one))
        lined = exchange(away, orders[0][3], count)
        share_one = [share_one[0], exchange(share_one[1], orders[0][0], count)]
    packed_two, sums_two, *share_two = weight_share(normed, *second[:3], *next_halo, tables[0])
    plane = (orders[0][2], orders[0][1], orders[0][1] | orders[0][2])
    line = (orders[0][4], orders[0][3], orders[0][3] | orders[0][4])
    if direct:
        share_one, share_two, packed_one, packed_two = sync((share_one, share_two, packed_one, packed_two))
        plane_one = straight(share_one, plane, count)
        share_two = [share_two[0], exchange(share_two[1], orders[0][0], count)]
    input_grad, sums_first = input_gradient(packed_one, packed_two, tokens, middle_grad, weight_qkv, vectors)
    pick = lambda i: jnp.concatenate([s[:, i * cols : (i + 1) * cols] for s in (sums_one, sums_two)], axis=1)
    sums = jnp.concatenate([sums_first[:2], pick(0), pick(2), sums_one[:, 3 * cols :], sums_mid[:3]], axis=0)
    sums = jnp.concatenate(
        [sums.reshape(8, count, part).transpose(1, 0, 2).reshape(count, 8 * part), hidden_bias_grad.reshape(count, -1)], axis=1
    )
    if direct:
        lined, plane_one, share_one, share_two, input_grad, sums = sync((lined, plane_one, share_one, share_two, input_grad, sums))
        got = [parts + [lined[2 * i : 2 * i + 2]] for i, parts in enumerate(got)]
        ended = exchange(jnp.concatenate([total([p[1:2] for p in parts]) for parts in got], axis=0), orders[0][4], count)
        plane_two = straight(share_two, plane, count)
        share_one = [p[:4] for p in share_one] + plane_one
        lined = exchange(total([p[2:4] for p in share_one]), orders[0][3], count)
        sums = lax.all_to_all(sums, "dev", 0, 0, tiled=True)
        lined, plane_two, share_two, sums, ended = sync((lined, plane_two, share_two, sums, ended))
        share_one = [p[:2] for p in share_one] + [lined]
        share_two = [p[:4] for p in share_two] + plane_two
        last_one = exchange(total([p[1:2] for p in share_one]), orders[0][4], count)
        last_two = straight(share_two, line, count)
        finals = [total([p[0] for p in parts] + [ended[i]], f32) for i, parts in enumerate(got)]
        hidden_shard = finals[0].transpose(1, 0, 2).reshape(part, hidden_width)
        final_shard = finals[1].reshape(-1, width)
        shards_one = total([p[0] for p in share_one] + [last_one[0]], f32)
        shards_two = total([p[0] for p in share_two] + [p[0] for p in last_two], f32)
    else:
        sums = lax.all_to_all(sums, "dev", 0, 0, tiled=True)
        shards_one, shards_two = scatter_whole(*share_one, count), scatter_whole(*share_two, count)
        finals = [jnp.concatenate(g, axis=0) for g in grads]
        finals[0] = finals[0].transpose(0, 2, 1, 3).reshape(width, hidden_width)
        finals[1] = finals[1].reshape(hidden_width, width)
        hidden_shard, final_shard = [lax.psum_scatter(p.astype(f32), "dev", scatter_dimension=0, tiled=True) for p in finals]
    sums = jnp.sum(sums, axis=0)
    own = [sums[i * part : (i + 1) * part] for i in range(8)]
    own_hidden = sums[8 * part :]
    out_shard = shards_one[:, 3 * cols :]
    qkv_shard = jnp.concatenate([h[:, i * cols : (i + 1) * cols] for i in range(3) for h in (shards_one, shards_two)], axis=1)
    return (
        result,
        input_grad,
        own[0],
        own[1],
        qkv_shard,
        own[2],
        own[3],
        out_shard,
        own[4],
        own[5],
        own[6],
        hidden_shard,
        own_hidden,
        final_shard,
        own[7],
    )


def solution(mesh):
    split = P("dev", None)
    line = P("dev")
    return jax.shard_map(
        per_device,
        mesh=mesh,
        in_specs=(split, P(), line, line, split, line, line, split, line, line, line, split, line, split, line, split),
        out_specs=(split, split, line, line, split, line, line, split, line, line, line, split, line, split, line),
        check_vma=False,
    )
```

```python
import functools
import math

import jax
import jax.numpy as jnp
from jax import lax
from jax.experimental import pallas as pl
from jax.experimental.pallas import tpu as pltpu
from jax.sharding import PartitionSpec as P

IMG = 577
REACH = IMG - 1
HEAD = 64
SPAN = 592
LANES = 128
PP = 2
PIECES = 32
PACE = 1.0e5
FEED_AFTER = 2
GROUPS = 2
VMEM = 60 * 1024 * 1024
f32 = jnp.float32
bf16 = jnp.bfloat16

norm_epsilon = 1e-06


def spent(us):
    return pl.CostEstimate(flops=0, bytes_accessed=int(us * PACE), transcendentals=0)


FP = 4
SLOTS = 8
CHUNKS = (384, 256, 128)


def make_items(img_ref, lists, counts, rows, images):
    for kind in range(len(CHUNKS)):
        counts[kind] = 0

    def add(kind, first, begin, end, start):
        size = CHUNKS[kind]
        n = counts[kind]
        base = (kind * SLOTS + n) * 4
        lists[base] = jnp.minimum(first, rows - size)
        lists[base + 1] = jnp.maximum(first, begin)
        lists[base + 2] = jnp.minimum(first + size, end)
        lists[base + 3] = start
        counts[kind] = n + 1

    for i in range(images):
        start = img_ref[i]
        begin = jnp.maximum(start - REACH, 0)
        end = jnp.minimum(start - REACH + IMG, rows)
        low = (begin // 16) * 16
        left = jnp.where(end > begin, end - low, 0)

        @pl.when(left > 512)
        def _():
            add(0, low, begin, end, start)
            add(1, low + 384, begin, end, start)

        @pl.when((left > 384) & (left <= 512))
        def _():
            add(1, low, begin, end, start)
            add(1, low + 256, begin, end, start)

        @pl.when((left > 256) & (left <= 384))
        def _():
            add(0, low, begin, end, start)

        @pl.when((left > 128) & (left <= 256))
        def _():
            add(1, low, begin, end, start)

        @pl.when((left > 0) & (left <= 128))
        def _():
            add(2, low, begin, end, start)


def item_scalars(lists, kind, n):
    base = (kind * SLOTS + n) * 4
    start = lists[base + 3]
    begin = pl.multiple_of((start // 16) * 16, 16)
    return pl.multiple_of(lists[base], 16), lists[base + 1], lists[base + 2], start, begin


def halves(x):
    lane = lax.broadcasted_iota(jnp.int32, x.shape, 1)
    zero = jnp.zeros_like(x)
    return jnp.concatenate([jnp.where(lane < HEAD, x, zero), jnp.where(lane >= HEAD, x, zero)], axis=0)


def mask_keys(scores, start, begin):
    def masked(low, top):
        r = lax.broadcasted_iota(jnp.int32, (top - low, 1), 0) + (low + begin - start)
        return jnp.where((r >= 0) & (r < IMG), scores[low:top], -1e30)

    return jnp.concatenate([masked(0, 16), scores[16 : SPAN - 16], masked(SPAN - 16, SPAN)], axis=0)


def query_valid(size, row, low, top):
    lane = lax.broadcasted_iota(jnp.int32, (1, 2 * size), 1)
    pos = jnp.where(lane < size, lane, lane - size) + row
    return (pos >= low) & (pos < top)


def pad_rows(img_ref, images, rows):
    r = lax.broadcasted_iota(jnp.int32, (rows, LANES), 0) + REACH
    inside = jnp.zeros((rows, LANES), jnp.bool_)
    for i in range(images):
        start = img_ref[i]
        inside = inside | ((r >= start) & (r < start + IMG))
    return ~inside


def fwd_kernel(images, img_ref, q_ref, k_ref, v_ref, o_ref, lse_ref, acc, lists, counts):
    rows = acc.shape[0]
    make_items(img_ref, lists, counts, rows, images)
    acc[...] = jnp.zeros_like(acc)

    def body(kind, size, n, carry):
        row, low, top, start, begin = item_scalars(lists, kind, n)
        qm = query_valid(size, row, low, top)
        done = []
        for u in range(FP):
            cols = slice(u * LANES, (u + 1) * LANES)
            q2 = halves(q_ref[pl.ds(pl.multiple_of(row + REACH, 16), size), cols])
            kw = k_ref[pl.ds(begin, SPAN), cols]
            vw = v_ref[pl.ds(begin, SPAN), cols]
            s = lax.dot_general(kw, q2, (((1,), (1,)), ((), ())), preferred_element_type=f32)
            s = mask_keys(s, start, begin)
            m = jnp.max(s, axis=0, keepdims=True)
            e = jnp.exp(s - m)
            l = jnp.sum(e, axis=0, keepdims=True)
            ot = lax.dot_general(vw, e.astype(bf16), (((0,), (0,)), ((), ())), preferred_element_type=f32)
            ot = ot * jnp.where(qm, 1.0 / l, 0.0)
            done.append((jnp.concatenate([ot[:HEAD, :size], ot[HEAD:, size:]], axis=0).T, m + jnp.log(l)))
        for u in range(FP):
            cols = slice(u * LANES, (u + 1) * LANES)
            acc[pl.ds(row, size), cols] += done[u][0]
            lse_ref[u, pl.ds(kind * SLOTS + n, 1), : 2 * size] = done[u][1]
        return carry

    for kind, size in enumerate(CHUNKS):
        lax.fori_loop(0, counts[kind], functools.partial(body, kind, size), 0)
    pad = pad_rows(img_ref, images, rows)
    for u in range(FP):
        cols = slice(u * LANES, (u + 1) * LANES)
        own = v_ref[pl.ds(REACH, rows), cols].astype(f32)
        o_ref[:, cols] = jnp.where(pad, own, acc[:, cols]).astype(bf16)


def attention_forward(img, q, k, v, first, pairs):
    win = k.shape[0]
    rows = win - 2 * REACH
    images = img.shape[0]
    spec = lambda r: pl.BlockSpec((r, FP * LANES), lambda p, *_: (0, first // FP + p))
    return pl.pallas_call(
        functools.partial(fwd_kernel, images),
        grid_spec=pltpu.PrefetchScalarGridSpec(
            num_scalar_prefetch=1,
            grid=(pairs // FP,),
            in_specs=[spec(win), spec(win), spec(win)],
            out_specs=[
                pl.BlockSpec((rows, FP * LANES), lambda p, *_: (0, p)),
                pl.BlockSpec((FP, 3 * SLOTS, 2 * CHUNKS[0]), lambda p, *_: (p, 0, 0)),
            ],
            scratch_shapes=[
                pltpu.VMEM((rows, FP * LANES), f32), pltpu.SMEM((3 * SLOTS * 4,), jnp.int32), pltpu.SMEM((3,), jnp.int32)
            ],
        ),
        out_shape=[
            jax.ShapeDtypeStruct((rows, pairs * LANES), bf16),
            jax.ShapeDtypeStruct((pairs, 3 * SLOTS, 2 * CHUNKS[0]), f32),
        ],
        compiler_params=pltpu.CompilerParams(vmem_limit_bytes=VMEM, dimension_semantics=("arbitrary",)),
        cost_estimate=spent(5 * pairs),
        name="attention_forward",
    )(img, q, k, v)


def bwd_kernel(images, img_ref, q_ref, k_ref, v_ref, g_ref, lse_ref,
               dq_ref, dk_ref, dv_ref, left_ref, right_ref, dq_acc, dk_acc, dv_acc, lists, counts):
    rows = dq_acc.shape[0]
    make_items(img_ref, lists, counts, rows, images)
    dq_acc[...] = jnp.zeros_like(dq_acc)
    dk_acc[...] = jnp.zeros_like(dk_acc)
    dv_acc[...] = jnp.zeros_like(dv_acc)

    def body(kind, size, n, carry):
        row, low, top, start, begin = item_scalars(lists, kind, n)
        qm = query_valid(size, row, low, top)
        done = []
        for u in range(PP):
            cols = slice(u * LANES, (u + 1) * LANES)
            q2 = halves(q_ref[pl.ds(pl.multiple_of(row + REACH, 16), size), cols])
            g2 = halves(g_ref[pl.ds(row, size), cols])
            kw = k_ref[pl.ds(begin, SPAN), cols]
            vw = v_ref[pl.ds(begin, SPAN), cols]
            lse = jnp.where(qm, lse_ref[u, pl.ds(kind * SLOTS + n, 1), : 2 * size], 1e30)
            s = lax.dot_general(kw, q2, (((1,), (1,)), ((), ())), preferred_element_type=f32)
            dp = lax.dot_general(vw, g2, (((1,), (1,)), ((), ())), preferred_element_type=f32)
            p = jnp.exp(mask_keys(s, start, begin) - lse)
            inner = jnp.sum(p * dp, axis=0, keepdims=True)
            ds = (p * (dp - inner)).astype(bf16)
            dv = jnp.dot(p.astype(bf16), g2, preferred_element_type=f32)
            dk = jnp.dot(ds, q2, preferred_element_type=f32)
            dqt = lax.dot_general(kw, ds, (((0,), (0,)), ((), ())), preferred_element_type=f32)
            done.append((dv, dk, jnp.concatenate([dqt[:HEAD, :size], dqt[HEAD:, size:]], axis=0).T))
        for u in range(PP):
            cols = slice(u * LANES, (u + 1) * LANES)
            dv, dk, dq = done[u]
            dv_acc[pl.ds(begin, SPAN), cols] += dv
            dk_acc[pl.ds(begin, SPAN), cols] += dk
            dq_acc[pl.ds(row, size), cols] += dq
        return carry

    for kind, size in enumerate(CHUNKS):
        lax.fori_loop(0, counts[kind], functools.partial(body, kind, size), 0)
    pad = pad_rows(img_ref, images, rows)
    dq_ref[...] = (dq_acc[...] * 0.125).astype(bf16)
    dk_ref[...] = dk_acc[pl.ds(REACH, rows), :]
    for u in range(PP):
        cols = slice(u * LANES, (u + 1) * LANES)
        dv_ref[:, cols] = dv_acc[pl.ds(REACH, rows), cols] + jnp.where(pad, g_ref[:, cols].astype(f32), 0.0)
    left_ref[0] = dk_acc[pl.ds(0, REACH), :].astype(bf16)
    left_ref[1] = dv_acc[pl.ds(0, REACH), :].astype(bf16)
    right_ref[0] = dk_acc[pl.ds(REACH + rows, REACH), :].astype(bf16)
    right_ref[1] = dv_acc[pl.ds(REACH + rows, REACH), :].astype(bf16)


def attention_backward(img, q, k, v, g, lse, first, pairs):
    win = k.shape[0]
    rows = win - 2 * REACH
    images = img.shape[0]
    C = PP * LANES
    spec = lambda r: pl.BlockSpec((r, C), lambda p, *_: (0, first // PP + p))
    out = lambda r: pl.BlockSpec((r, C), lambda p, *_: (0, p))
    edge = pl.BlockSpec((2, REACH, C), lambda p, *_: (0, 0, p))
    sds = jax.ShapeDtypeStruct
    cols = pairs * LANES
    return pl.pallas_call(
        functools.partial(bwd_kernel, images),
        grid_spec=pltpu.PrefetchScalarGridSpec(
            num_scalar_prefetch=1,
            grid=(pairs // PP,),
            in_specs=[spec(win), spec(win), spec(win), spec(rows),
                      pl.BlockSpec((PP, 3 * SLOTS, 2 * CHUNKS[0]), lambda p, *_: (first // PP + p, 0, 0))],
            out_specs=[out(rows), out(rows), out(rows), edge, edge],
            scratch_shapes=[pltpu.VMEM((rows, C), f32), pltpu.VMEM((win, C), f32), pltpu.VMEM((win, C), f32),
                            pltpu.SMEM((3 * SLOTS * 4,), jnp.int32), pltpu.SMEM((3,), jnp.int32)],
        ),
        out_shape=[sds((rows, cols), bf16), sds((rows, cols), f32), sds((rows, cols), f32),
                   sds((2, REACH, cols), bf16), sds((2, REACH, cols), bf16)],
        compiler_params=pltpu.CompilerParams(vmem_limit_bytes=VMEM, dimension_semantics=("arbitrary",)),
        cost_estimate=spent(6.5 * pairs),
        name="attention_backward",
    )(img, q, k, v, g, lse)


FT = 512
ROWS = 1024


def contract(a, b, dims):
    return lax.dot_general(a, b, (dims, ((), ())), preferred_element_type=f32)


def feed_kernel(
    table, normed, cot, middle, bias_final, wide, tall, bias_hidden,
    result, grad_normed, bias_grad, hidden_near, hidden_far, active,
    total, normed_t, final, grad_pre, hidden_grad,
):
    step = pl.program_id(0)
    tiles = pl.num_programs(0)
    rows, width = normed.shape
    half, _, piece, _ = hidden_near.shape
    devices = tall.shape[0] // 32
    depth = FT // devices

    @pl.when(step == 0)
    def _():
        total[...] = middle[...] + bias_final[...]
        grad_normed[...] = jnp.zeros_like(grad_normed)
        normed_t[...] = normed[...].T

    for d in range(devices):
        for i in range(4):
            final[d * depth + i * 32 : d * depth + (i + 1) * 32, :] = tall[d * 32 : (d + 1) * 32, i * width : (i + 1) * width]
    for r in range(0, rows, ROWS):
        cut = slice(r, r + ROWS)
        pre = contract(normed[cut, :], wide[...], ((1,), (0,))) + bias_hidden[...]
        grad = contract(cot[cut, :], final[...], ((1,), (1,)))
        phi = 0.5 + 0.5 * lax.erf(pre * (0.5**0.5))
        slope = phi + pre * jnp.exp(pre * pre * -0.5) * ((0.5 / math.pi) ** 0.5)
        active[cut, :] = (pre * phi).astype(bf16)
        grad_pre[cut, :] = (grad * slope).astype(bf16)
        total[cut, :] += contract(active[cut, :], final[...], ((1,), (0,)))
        grad_normed[cut, :] += contract(grad_pre[cut, :], wide[...], ((1,), (1,)))
    bias_grad[...] = jnp.sum(grad_pre[...].astype(f32), axis=0, keepdims=True)
    hidden_grad[...] = contract(normed_t[...], grad_pre[...], ((1,), (0,)))
    for place in range(2 * half):
        rows_of = hidden_grad[pl.ds(pl.multiple_of(table[place] * piece, piece), piece), :].astype(bf16)
        if place < half:
            hidden_near[place, 0] = rows_of
        else:
            hidden_far[place - half, 0] = rows_of

    @pl.when(step == tiles - 1)
    def _():
        result[...] = total[...].astype(bf16)


def final_kernel(home, active, cot, final_near, final_far, final_grad, sems):
    step = pl.program_id(0)
    tiles = pl.num_programs(0)
    slot = lax.rem(step, 2)
    half, depth, width = final_near.shape
    devices = FT // depth

    def copy_out(slot, d, target):
        return pltpu.make_async_copy(final_grad.at[slot, d], target, sems.at[slot, d])

    def wait_out(slot):
        for d in range(devices):
            copy_out(slot, d, final_near.at[0]).wait()

    @pl.when(step >= 2)
    def _():
        wait_out(slot)

    final_grad[slot] = contract(active[...], cot[...], ((0,), (0,))).astype(bf16).reshape(devices, depth, width)
    for d in range(devices):
        at = home[step * devices + d]

        @pl.when(at < half)
        def _():
            copy_out(slot, d, final_near.at[at]).start()

        @pl.when(at >= half)
        def _():
            copy_out(slot, d, final_far.at[at - half]).start()

    @pl.when(step == tiles - 1)
    def _():
        for d in range(devices):
            copy_out(1 - slot, d, final_near.at[0]).wait()
            copy_out(slot, d, final_near.at[0]).wait()


def final_share(active, cot, home):
    rows, width = cot.shape
    units = active.shape[1]
    depth = units // PIECES
    piece = jax.ShapeDtypeStruct((PIECES // 2, depth, width), bf16)
    return pl.pallas_call(
        final_kernel,
        grid_spec=pltpu.PrefetchScalarGridSpec(
            num_scalar_prefetch=1,
            grid=(units // FT,),
            in_specs=[
                pl.BlockSpec((rows, FT), lambda t, *_: (0, t)),
                pl.BlockSpec((rows, width), lambda t, *_: (0, 0), pipeline_mode=pl.Buffered(1)),
            ],
            out_specs=[pl.BlockSpec(memory_space=pl.ANY)] * 2,
            scratch_shapes=[pltpu.VMEM((2, FT // depth, depth, width), bf16), pltpu.SemaphoreType.DMA((2, FT // depth))],
        ),
        out_shape=[piece, piece],
        compiler_params=pltpu.CompilerParams(vmem_limit_bytes=VMEM, dimension_semantics=("arbitrary",)),
        cost_estimate=spent(14),
        name="final_share",
    )(home, active, cot)


def feed_forward(normed, cot, middle, bias_final, feed, bias_hidden, table):
    rows, width = normed.shape
    units = bias_hidden.shape[1]
    whole = lambda *shape: pl.BlockSpec(shape, lambda t, *_: (0,) * len(shape), pipeline_mode=pl.Buffered(1))
    sds = jax.ShapeDtypeStruct
    depth = units // PIECES
    devices = FT // depth
    line = pl.BlockSpec((1, FT), lambda t, *_: (0, t))
    square = whole(rows, width)
    wide_piece = sds((PIECES // 2, units // width, width // PIECES, width), bf16)
    blocks = width // FT
    edge = pl.BlockSpec((PIECES // 2, 1, width // PIECES, FT), lambda t, *_: (0, t // blocks, 0, t % blocks))
    return pl.pallas_call(
        feed_kernel,
        grid_spec=pltpu.PrefetchScalarGridSpec(
            num_scalar_prefetch=1,
            grid=(units // FT,),
            in_specs=[
                square, square, square, whole(1, width),
                pl.BlockSpec((width, FT), lambda t, *_: (0, t)),
                pl.BlockSpec((devices * 32, 4 * width), lambda t, *_: (t, 1)),
                line,
            ],
            out_specs=[square, square, line, edge, edge, pl.BlockSpec((rows, FT), lambda t, *_: (0, t))],
            scratch_shapes=[
                pltpu.VMEM((rows, width), f32), pltpu.VMEM((width, rows), bf16), pltpu.VMEM((FT, width), bf16),
                pltpu.VMEM((rows, FT), bf16), pltpu.VMEM((width, FT), f32),
            ],
        ),
        out_shape=[
            sds((rows, width), bf16), sds((rows, width), f32), sds((1, units), f32),
            wide_piece, wide_piece, sds((rows, units), bf16),
        ],
        compiler_params=pltpu.CompilerParams(vmem_limit_bytes=VMEM, dimension_semantics=("arbitrary",)),
        cost_estimate=spent(57),
        name="feed_forward",
    )(table, normed, cot, middle, bias_final, feed, feed, bias_hidden)


def project_kernel(
    table_one, table_two, x, one_near, one_far, two_near, two_far,
    q_out, k_out, v_out, normed_out, weight, weight_out, vectors, small,
):
    half, piece, split = one_near.shape
    width = x.shape[1]
    wide = weight.shape[1]

    @pl.when(pl.program_id(0) == 0)
    def _():
        for place in range(2 * half):
            a, b, at = (one_near, two_near, place) if place < half else (one_far, two_far, place - half)
            rows = pl.ds(pl.multiple_of(table_one[place] * piece, piece), piece)
            weight[rows, :split] = a[at]
            rows = pl.ds(pl.multiple_of(table_two[place] * piece, piece), piece)
            weight[rows, split:] = b[at, :, : wide - split]
            weight_out[rows, :] = b[at, :, wide - split : wide - split + width]
            small[rows, :] = b[at, :, wide - split + width : wide - split + width + LANES].astype(f32)
        vectors[...] = small[...].T[: vectors.shape[0]]

    values = x[...].astype(f32)
    center = values - jnp.mean(values, axis=-1, keepdims=True)
    spread_of = jnp.mean(center * center, axis=-1, keepdims=True)
    normed = (center * lax.rsqrt(spread_of + norm_epsilon) * vectors[0:1, :] + vectors[1:2, :]).astype(bf16)
    normed_out[...] = normed
    cols = width // GROUPS
    needs_queries = (pl.program_id(0) == 1) | (pl.program_id(0) == 2)
    for group in range(GROUPS):
        out = slice(group * cols, (group + 1) * cols)
        begin = 3 * group * cols
        keys = jnp.dot(normed, weight[:, begin + cols : begin + 2 * cols], preferred_element_type=f32)
        values = jnp.dot(normed, weight[:, begin + 2 * cols : begin + 3 * cols], preferred_element_type=f32)
        k_out[:, out] = keys.astype(bf16)
        v_out[:, out] = (values + vectors[3:4, out]).astype(bf16)

        @pl.when(needs_queries)
        def _():
            queries = jnp.dot(normed, weight[:, begin : begin + cols], preferred_element_type=f32)
            q_out[:, out] = (queries + vectors[2:3, out]).astype(bf16) * jnp.asarray(HEAD**-0.5, bf16)


def project(window, one, two, tables):
    rows, width = window.shape
    half, piece, split = one[0].shape
    block = rows // 4
    whole = lambda *shape: pl.BlockSpec(shape, lambda t, *_: (0,) * len(shape), pipeline_mode=pl.Buffered(1))
    strip = pl.BlockSpec((block, width), lambda t, *_: (t, 0))
    sds = jax.ShapeDtypeStruct
    return pl.pallas_call(
        project_kernel,
        grid_spec=pltpu.PrefetchScalarGridSpec(
            num_scalar_prefetch=2,
            grid=(4,),
            in_specs=[strip] + [whole(half, piece, split)] * 2 + [whole(*two[0].shape)] * 2,
            out_specs=[strip] * 4 + [whole(width, 3 * width), whole(width, width), whole(16, width)],
            scratch_shapes=[pltpu.VMEM((width, LANES), f32)],
        ),
        out_shape=[sds((rows, width), bf16)] * 4 + [sds((width, 3 * width), bf16), sds((width, width), bf16), sds((16, width), f32)],
        compiler_params=pltpu.CompilerParams(vmem_limit_bytes=VMEM, dimension_semantics=("arbitrary",)),
        cost_estimate=spent(24),
        name="project",
    )(*tables, window, *one, *two)


CW = 256


def share_kernel(
    extra, table, normed, dq, dk, dv, left, right, *refs,
):
    mixed, branch = refs[:2] if extra else (None, None)
    packed, sums, near, far, normed_t, product, x = refs[2 if extra else 0 :]
    step = pl.program_id(0)
    rows = dq.shape[0]
    half, piece, _ = near.shape

    @pl.when(step == 0)
    def _():
        normed_t[...] = normed[pl.ds(REACH, rows), :].T

    def halo(own, number):
        x[...] = own[...].astype(bf16)
        edge = rows - REACH
        x[:edge, :] = (own[:edge, :] + left[number, :edge, :].astype(f32)).astype(bf16)
        x[edge:REACH, :] = (own[edge:REACH, :] + left[number, edge:, :].astype(f32) + right[number, : REACH - edge, :].astype(f32)).astype(bf16)
        x[REACH:, :] = (own[REACH:, :] + right[number, REACH - edge :, :].astype(f32)).astype(bf16)

    @pl.when(step < 2)
    def _():
        x[...] = dq[...]

    @pl.when((step >= 2) & (step < 4))
    def _():
        halo(dk, 0)

    @pl.when((step >= 4) & (step < 6))
    def _():
        halo(dv, 1)

    if extra:
        @pl.when(step == 6)
        def _():
            normed_t[...] = mixed[...].T

        @pl.when(step >= 6)
        def _():
            x[...] = branch[...]

    @pl.when(step < 6)
    def _():
        packed[...] = x[...]

    sums[...] = jnp.sum(x[...].astype(f32), axis=0, keepdims=True)
    product[...] = jnp.dot(normed_t[...], x[...], preferred_element_type=f32)
    for place in range(2 * half):
        rows_of = product[pl.ds(pl.multiple_of(table[place] * piece, piece), piece), :].astype(bf16)
        if place < half:
            near[place] = rows_of
        else:
            far[place - half] = rows_of


def weight_share(normed, dq, dk, dv, left, right, table, extra=()):
    rows, cols = dq.shape
    win, width = normed.shape
    steps = 6 + (4 if extra else 0)
    whole = lambda *shape: pl.BlockSpec(shape, lambda t, *_: (0,) * len(shape), pipeline_mode=pl.Buffered(1))
    clip = lambda t, low, top: jnp.minimum(jnp.maximum(t - low, 0), top)
    tall = lambda low, top: pl.BlockSpec((rows, CW), lambda t, *_: (0, clip(t, low, top)))
    edge = pl.BlockSpec((2, REACH, CW), lambda t, *_: (0, 0, jnp.where(t < 4, clip(t, 2, 1), clip(t, 4, 1))))
    piece = pl.BlockSpec((PIECES // 2, width // PIECES, CW), lambda t, *_: (0, 0, t))
    sds = jax.ShapeDtypeStruct
    pieces = sds((PIECES // 2, width // PIECES, steps * CW), bf16)
    return pl.pallas_call(
        functools.partial(share_kernel, bool(extra)),
        grid_spec=pltpu.PrefetchScalarGridSpec(
            num_scalar_prefetch=1,
            grid=(steps,),
            in_specs=[whole(win, width), tall(0, 1), tall(2, 1), tall(4, 1), edge, edge]
            + ([whole(rows, width), tall(6, 3)] if extra else []),
            out_specs=[tall(0, 5), pl.BlockSpec((1, CW), lambda t, *_: (0, t))]
            + [piece] * 2,
            scratch_shapes=[pltpu.VMEM((width, rows), bf16), pltpu.VMEM((width, CW), f32), pltpu.VMEM((rows, CW), bf16)],
        ),
        out_shape=[sds((rows, 6 * CW), bf16), sds((1, steps * CW), f32), pieces, pieces],
        compiler_params=pltpu.CompilerParams(vmem_limit_bytes=VMEM, dimension_semantics=("arbitrary",)),
        cost_estimate=spent(10 if extra else 7),
        name="weight_share",
    )(table, normed, dq, dk, dv, left, right, *extra)


def norm_backward(values, gain, grad):
    center = values - jnp.mean(values, axis=-1, keepdims=True)
    scale = lax.rsqrt(jnp.mean(center * center, axis=-1, keepdims=True) + norm_epsilon)
    unit = center * scale
    scaled = grad * gain
    moved = scaled - jnp.mean(scaled, axis=-1, keepdims=True) - unit * jnp.mean(scaled * unit, axis=-1, keepdims=True)
    column = lambda x: jnp.sum(x, axis=0, keepdims=True)
    return scale * moved, column(grad * unit), column(grad)


def branch_kernel(grad, middle, cot, weight_out, vectors, total, branch, mixed, sums):
    @pl.when(pl.program_id(0) == 0)
    def _():
        sums[...] = jnp.zeros_like(sums)

    up = cot[...].astype(f32)
    moved, gain_sum, bias_sum = norm_backward(middle[...], vectors[5:6, :], grad[...])
    total[...] = up + moved
    branch[...] = total[...].astype(bf16)
    mixed[...] = contract(branch[...], weight_out[...], ((1,), (1,))).astype(bf16)
    sums[0:1, :] += gain_sum
    sums[1:2, :] += bias_sum
    sums[2:3, :] += jnp.sum(up, axis=0, keepdims=True)


def input_kernel(one, two, weight, tokens, middle_grad, vectors, out, sums):
    @pl.when(pl.program_id(0) == 0)
    def _():
        sums[...] = jnp.zeros_like(sums)

    cols = one.shape[1]
    grad = contract(one[...], weight[:, :cols], ((1,), (1,))) + contract(two[...], weight[:, cols:], ((1,), (1,)))
    moved, gain_sum, bias_sum = norm_backward(tokens[...].astype(f32), vectors[0:1, :], grad)
    out[...] = (middle_grad[...] + moved).astype(bf16)
    sums[0:1, :] += gain_sum
    sums[1:2, :] += bias_sum


def row_blocks(kernel, name, blocked, whole, outs, us):
    rows, width = blocked[0].shape[0], outs[0][0]
    block = rows // 4
    strip = lambda cols: pl.BlockSpec((block, cols), lambda t: (t, 0))
    fixed = lambda *shape: pl.BlockSpec(shape, lambda t: (0,) * len(shape), pipeline_mode=pl.Buffered(1))
    return pl.pallas_call(
        kernel,
        grid=(4,),
        in_specs=[strip(a.shape[1]) for a in blocked] + [fixed(*a.shape) for a in whole],
        out_specs=[strip(cols) for cols, _ in outs] + [fixed(8, width)],
        out_shape=[jax.ShapeDtypeStruct((rows, cols), kind) for cols, kind in outs] + [jax.ShapeDtypeStruct((8, width), f32)],
        compiler_params=pltpu.CompilerParams(vmem_limit_bytes=VMEM, dimension_semantics=("arbitrary",)),
        cost_estimate=spent(us),
        name=name,
    )(*blocked, *whole)


def branch_gradient(grad, middle, cot, weight_out, vectors):
    width = middle.shape[1]
    outs = [(width, f32), (width, bf16), (width, bf16)]
    return row_blocks(branch_kernel, "branch_gradient", [grad, middle, cot], [weight_out, vectors], outs, 10)


def input_gradient(one, two, tokens, middle_grad, weight, vectors):
    def kernel(one, two, tokens, middle_grad, weight, vectors, out, sums):
        input_kernel(one, two, weight, tokens, middle_grad, vectors, out, sums)

    return row_blocks(kernel, "input_gradient", [one, two, tokens, middle_grad], [weight, vectors], [(tokens.shape[1], bf16)], 12)


def bit_orders(count):
    bits = [1 << i for i in range(count.bit_length() - 1)]
    return (bits[0], bits[2], bits[1], *bits[3:]), (bits[0], bits[1], bits[2], *bits[3:])


def exchange(x, bit, count):
    return lax.ppermute(x, "dev", [(i, i ^ bit) for i in range(count)])


def owners(order, me):
    table = []
    for place in range(PIECES):
        offset = 0
        for i, bit in enumerate(order):
            if (place >> (len(order) - 1 - i)) & 1:
                offset |= bit
        table.append(offset)
    return jnp.array(table, jnp.int32) ^ me


def places(order, me):
    offset = jnp.arange(PIECES, dtype=jnp.int32) ^ me
    return sum(jnp.where(offset & bit != 0, 1 << (len(order) - 1 - i), 0) for i, bit in enumerate(order)).astype(jnp.int32)


def gather_step(held, order, step, count):
    bit = order[len(order) - 1 - step]
    arrived = exchange(held, bit, count)
    return (held, arrived) if bit == order[0] else jnp.concatenate([held, arrived], axis=0)


def total(parts, kind=bf16):
    return functools.reduce(lambda a, b: a + b, [p.astype(f32) for p in parts]).astype(kind)


def straight(parts, bits, count):
    size = parts[0].shape[0] // (len(bits) + 1)
    return [exchange(total([p[(i + 1) * size : (i + 2) * size] for p in parts]), bit, count) for i, bit in enumerate(bits)]


def scatter_whole(near, far, count):
    whole = jnp.concatenate([near, far], axis=0).reshape(-1, near.shape[2])
    return lax.psum_scatter(whole.astype(f32), "dev", scatter_dimension=0, tiled=True)


def layer_norm(values, gain, bias):
    center = values - jnp.mean(values, axis=-1, keepdims=True)
    spread_of = jnp.mean(center * center, axis=-1, keepdims=True)
    return center * lax.rsqrt(spread_of + norm_epsilon) * gain + bias


def exact_gelu(values):
    return jax.nn.gelu(values, approximate=False)


def image_starts(segment_ids, me, rows):
    padded = jnp.pad(segment_ids, (REACH, REACH), constant_values=-2)
    window = lax.dynamic_slice_in_dim(padded, me * rows, rows + 2 * REACH, 0)
    own = window[REACH : REACH + rows]
    far = jnp.int32(1 << 20)
    first = jnp.min(jnp.where(own >= 0, own, far))
    places = jnp.arange(rows + 2 * REACH, dtype=jnp.int32)
    images = (rows - 2) // IMG + 2
    starts = []
    for i in range(images):
        start = jnp.min(jnp.where(window == first + i, places, far))
        starts.append(jnp.where(start == far, -far, start))
    return jnp.stack(starts)


def per_device(
    tokens,
    segment_ids,
    first_gain,
    first_bias,
    qkv_weight,
    query_bias,
    value_bias,
    out_weight,
    out_bias,
    second_gain,
    second_bias,
    hidden_weight,
    hidden_bias,
    final_weight,
    final_bias,
    cotangent,
):
    count = lax.axis_size("dev")
    me = lax.axis_index("dev")
    direct = count == PIECES
    rows, width = tokens.shape
    hidden_width = hidden_weight.shape[1]
    pairs = width // LANES
    part = width // count
    part_rows = width // PIECES
    half = PIECES // 2
    unit = hidden_width // PIECES
    orders = bit_orders(PIECES)
    tables = [owners(order, me) if direct else jnp.arange(PIECES, dtype=jnp.int32) for order in orders]
    home = places(orders[0], me) if direct else jnp.arange(PIECES, dtype=jnp.int32)
    sync = lax.optimization_barrier
    img = image_starts(segment_ids, me, rows)
    to_right = [(i, i + 1) for i in range(count - 1)]
    to_left = [(i + 1, i) for i in range(count - 1)]
    send = lambda left, right: (lax.ppermute(right, "dev", to_right), lax.ppermute(left, "dev", to_left))

    vectors = [first_gain, first_bias, query_bias, value_bias, out_bias, second_gain, second_bias, final_bias]
    small = sync(jnp.concatenate([jnp.stack(vectors, axis=1), hidden_bias.reshape(part, -1)], axis=1)).astype(bf16)
    small = jnp.pad(small, ((0, 0), (0, LANES - small.shape[1])))
    cols = width // GROUPS
    qkv_low = qkv_weight.astype(bf16)
    qkv_low = jnp.concatenate(
        [qkv_low[:, i * width + g * cols : i * width + (g + 1) * cols] for g in range(GROUPS) for i in range(3)], axis=1
    )
    split = 2 * width
    early = jnp.concatenate([qkv_low, out_weight.astype(bf16), small], axis=1)
    hidden_low = hidden_weight.astype(bf16)
    final_low = final_weight.astype(bf16)
    if direct:
        feed = jnp.concatenate([hidden_low] + [final_low[32 * i : 32 * (i + 1)] for i in range(4)], axis=1)
        halo = send(tokens[:REACH], tokens[rows - REACH :])
        line = [exchange(early[None], bit, count) for bit in (orders[0][4], orders[0][3], orders[0][3] | orders[0][4])]
        line, halo, feed = sync((line, halo, feed)) if FEED_AFTER == 1 else (*sync((line, halo)), feed)
        held = [jnp.concatenate([p[..., cut] for p in (early[None], *line)], axis=0) for cut in (slice(0, split), slice(split, None))]
        held = [gather_step(h, o, 2, count) for h, o in zip(held, orders)]
        if FEED_AFTER == 2:
            held, feed = sync((held, feed))
        held = [gather_step(h, o, 3, count) for h, o in zip(held, orders)]
        if FEED_AFTER == 3:
            held, feed = sync((held, feed))
        held = [gather_step(h, o, 4, count) for h, o in zip(held, orders)]
        feed = lax.all_gather(feed, "dev", axis=0, tiled=True)
        one, two = held
    else:
        early = lax.all_gather(early, "dev", axis=0, tiled=True).reshape(PIECES, width // PIECES, -1)
        one, two = [jnp.split(p, 2) for p in (early[..., :split], early[..., split:])]
        hidden_low = lax.all_gather(hidden_low, "dev", axis=0, tiled=True)
        final_low = lax.all_gather(final_low, "dev", axis=0, tiled=True)
        final_low = final_low.reshape(PIECES, 4, 32, width).transpose(0, 2, 1, 3).reshape(width, 4 * width)
        feed = jnp.concatenate([hidden_low, final_low], axis=1)
        halo = send(tokens[:REACH], tokens[rows - REACH :])
    window = jnp.concatenate([halo[0], tokens, halo[1]], axis=0)
    inputs = tokens.astype(f32)
    queries, key_rows, value_rows, normed, weight_qkv, weight_out, vectors = project(window, one, two, tables)
    gain_one, bias_one, bias_query, bias_value, bias_out, gain_two, bias_two, bias_final = [vectors[i] for i in range(8)]
    bias_hidden = vectors[8 : 8 + hidden_width // width].T.reshape(1, hidden_width)
    mixed_low, totals = attention_forward(img, queries, key_rows, value_rows, 0, pairs)
    middle = inputs + (jnp.dot(mixed_low, weight_out, preferred_element_type=f32) + bias_out)
    normed_two = layer_norm(middle, gain_two, bias_two).astype(bf16)
    result, grad_normed_two, hidden_bias_grad, *hidden_grads, active = feed_forward(
        normed_two, cotangent, middle, bias_final[None], feed, bias_hidden, tables[1]
    )
    step = pairs // GROUPS
    blocks = lambda pair: [g.reshape(g.shape[0], -1, part_rows, width) for g in pair]
    hidden_grads = blocks(hidden_grads)
    if direct:
        hidden_got = [hidden_grads[0], exchange(hidden_grads[1], orders[1][0], count)]
    final_grads = blocks(final_share(active, cotangent, home))
    if direct:
        hidden_got, final_grads, grad_normed_two = sync((hidden_got, final_grads, grad_normed_two))
        final_got = [final_grads[0], exchange(final_grads[1], orders[0][0], count)]
        away = total([p[8:] for p in hidden_got])
        away, grad_normed_two = sync((away, grad_normed_two))
        moving = [exchange(away, orders[1][1], count)]
    middle_grad, grad_branch, grad_mixed, sums_mid = branch_gradient(grad_normed_two, middle, cotangent, weight_out, vectors)
    if direct:
        final_got, grad_mixed = sync((final_got, grad_mixed))
        away = total([p[8:] for p in final_got])
        away, grad_mixed = sync((away, grad_mixed))
        moving.append(exchange(away, orders[0][1], count))
        got = [hidden_got, final_got]
        turns = orders[1], orders[0]
    else:
        grads = [hidden_grads, final_grads]
    first = attention_backward(img, queries, key_rows, value_rows, grad_mixed, totals, 0, step)
    if direct:
        grad_mixed, first = sync((grad_mixed, first))
    halo = send(*first[3:])
    second = attention_backward(img, queries, key_rows, value_rows, grad_mixed, totals, step, step)
    if direct:
        moving, first, second, halo, normed, grad_branch = sync((moving, first, second, halo, normed, grad_branch))
        got = [parts + [m] for parts, m in zip(got, moving)]
        away = [total([p[4:8] for p in parts]) for parts in got]
        away, first, second, halo, normed, grad_branch = sync((away, first, second, halo, normed, grad_branch))
        moving = [exchange(a, order[2], count) for a, order in zip(away, turns)]
    next_halo = send(*second[3:])
    packed_one, sums_one, *share_one = weight_share(normed, *first[:3], *halo, tables[0], (mixed_low, grad_branch))
    if direct:
        moving, second, next_halo, normed, share_one = sync((moving, second, next_halo, normed, share_one))
        got = [parts + [m] for parts, m in zip(got, moving)]
        away = jnp.concatenate([total([p[2:4] for p in parts]) for parts in got], axis=0)
        away, second, next_halo, normed, share_one = sync((away, second, next_halo, normed, share_one))
        lined = exchange(away, orders[0][3], count)
        share_one = [share_one[0], exchange(share_one[1], orders[0][0], count)]
    packed_two, sums_two, *share_two = weight_share(normed, *second[:3], *next_halo, tables[0])
    plane = (orders[0][2], orders[0][1], orders[0][1] | orders[0][2])
    line = (orders[0][4], orders[0][3], orders[0][3] | orders[0][4])
    if direct:
        share_one, share_two, packed_one, packed_two = sync((share_one, share_two, packed_one, packed_two))
        plane_one = straight(share_one, plane, count)
        share_two = [share_two[0], exchange(share_two[1], orders[0][0], count)]
    input_grad, sums_first = input_gradient(packed_one, packed_two, tokens, middle_grad, weight_qkv, vectors)
    pick = lambda i: jnp.concatenate([s[:, i * cols : (i + 1) * cols] for s in (sums_one, sums_two)], axis=1)
    sums = jnp.concatenate([sums_first[:2], pick(0), pick(2), sums_one[:, 3 * cols :], sums_mid[:3]], axis=0)
    sums = jnp.concatenate(
        [sums.reshape(8, count, part).transpose(1, 0, 2).reshape(count, 8 * part), hidden_bias_grad.reshape(count, -1)], axis=1
    )
    if direct:
        lined, plane_one, share_one, share_two, input_grad, sums = sync((lined, plane_one, share_one, share_two, input_grad, sums))
        got = [parts + [lined[2 * i : 2 * i + 2]] for i, parts in enumerate(got)]
        ended = exchange(jnp.concatenate([total([p[1:2] for p in parts]) for parts in got], axis=0), orders[0][4], count)
        plane_two = straight(share_two, plane, count)
        share_one = [p[:4] for p in share_one] + plane_one
        lined = exchange(total([p[2:4] for p in share_one]), orders[0][3], count)
        sums = lax.all_to_all(sums, "dev", 0, 0, tiled=True)
        lined, plane_two, share_two, sums, ended = sync((lined, plane_two, share_two, sums, ended))
        share_one = [p[:2] for p in share_one] + [lined]
        share_two = [p[:4] for p in share_two] + plane_two
        last_one = exchange(total([p[1:2] for p in share_one]), orders[0][4], count)
        last_two = straight(share_two, line, count)
        finals = [total([p[0] for p in parts] + [ended[i]], f32) for i, parts in enumerate(got)]
        hidden_shard = finals[0].transpose(1, 0, 2).reshape(part, hidden_width)
        final_shard = finals[1].reshape(-1, width)
        shards_one = total([p[0] for p in share_one] + [last_one[0]], f32)
        shards_two = total([p[0] for p in share_two] + [p[0] for p in last_two], f32)
    else:
        sums = lax.all_to_all(sums, "dev", 0, 0, tiled=True)
        shards_one, shards_two = scatter_whole(*share_one, count), scatter_whole(*share_two, count)
        finals = [jnp.concatenate(g, axis=0) for g in grads]
        finals[0] = finals[0].transpose(0, 2, 1, 3).reshape(width, hidden_width)
        finals[1] = finals[1].reshape(hidden_width, width)
        hidden_shard, final_shard = [lax.psum_scatter(p.astype(f32), "dev", scatter_dimension=0, tiled=True) for p in finals]
    sums = jnp.sum(sums, axis=0)
    own = [sums[i * part : (i + 1) * part] for i in range(8)]
    own_hidden = sums[8 * part :]
    out_shard = shards_one[:, 3 * cols :]
    qkv_shard = jnp.concatenate([h[:, i * cols : (i + 1) * cols] for i in range(3) for h in (shards_one, shards_two)], axis=1)
    return (
        result,
        input_grad,
        own[0],
        own[1],
        qkv_shard,
        own[2],
        own[3],
        out_shard,
        own[4],
        own[5],
        own[6],
        hidden_shard,
        own_hidden,
        final_shard,
        own[7],
    )


def solution(mesh):
    split = P("dev", None)
    line = P("dev")
    return jax.shard_map(
        per_device,
        mesh=mesh,
        in_specs=(split, P(), line, line, split, line, line, split, line, line, line, split, line, split, line, split),
        out_specs=(split, split, line, line, split, line, line, split, line, line, line, split, line, split, line),
        check_vma=False,
    )
```

```python
import functools
import math

import jax
import jax.numpy as jnp
from jax import lax
from jax.experimental import pallas as pl
from jax.experimental.pallas import tpu as pltpu
from jax.sharding import PartitionSpec as P

IMG = 577
REACH = IMG - 1
HEAD = 64
SPAN = 592
LANES = 128
PP = 2
PIECES = 32
PACE = 1.0e5
FEED_AFTER = 2
GROUPS = 2
VMEM = 60 * 1024 * 1024
f32 = jnp.float32
bf16 = jnp.bfloat16

norm_epsilon = 1e-06


def spent(us):
    return pl.CostEstimate(flops=0, bytes_accessed=int(us * PACE), transcendentals=0)


FP = 4
SLOTS = 8
CHUNKS = (384, 256, 128)


def make_items(img_ref, lists, counts, rows, images):
    for kind in range(len(CHUNKS)):
        counts[kind] = 0

    def add(kind, first, begin, end, start):
        size = CHUNKS[kind]
        n = counts[kind]
        base = (kind * SLOTS + n) * 4
        lists[base] = jnp.minimum(first, rows - size)
        lists[base + 1] = jnp.maximum(first, begin)
        lists[base + 2] = jnp.minimum(first + size, end)
        lists[base + 3] = start
        counts[kind] = n + 1

    for i in range(images):
        start = img_ref[i]
        begin = jnp.maximum(start - REACH, 0)
        end = jnp.minimum(start - REACH + IMG, rows)
        low = (begin // 16) * 16
        left = jnp.where(end > begin, end - low, 0)

        @pl.when(left > 512)
        def _():
            add(0, low, begin, end, start)
            add(1, low + 384, begin, end, start)

        @pl.when((left > 384) & (left <= 512))
        def _():
            add(1, low, begin, end, start)
            add(1, low + 256, begin, end, start)

        @pl.when((left > 256) & (left <= 384))
        def _():
            add(0, low, begin, end, start)

        @pl.when((left > 128) & (left <= 256))
        def _():
            add(1, low, begin, end, start)

        @pl.when((left > 0) & (left <= 128))
        def _():
            add(2, low, begin, end, start)


def item_scalars(lists, kind, n):
    base = (kind * SLOTS + n) * 4
    start = lists[base + 3]
    begin = pl.multiple_of((start // 16) * 16, 16)
    return pl.multiple_of(lists[base], 16), lists[base + 1], lists[base + 2], start, begin


def halves(x):
    lane = lax.broadcasted_iota(jnp.int32, x.shape, 1)
    zero = jnp.zeros_like(x)
    return jnp.concatenate([jnp.where(lane < HEAD, x, zero), jnp.where(lane >= HEAD, x, zero)], axis=0)


def mask_keys(scores, start, begin):
    def masked(low, top):
        r = lax.broadcasted_iota(jnp.int32, (top - low, 1), 0) + (low + begin - start)
        return jnp.where((r >= 0) & (r < IMG), scores[low:top], -1e30)

    return jnp.concatenate([masked(0, 16), scores[16 : SPAN - 16], masked(SPAN - 16, SPAN)], axis=0)


def query_valid(size, row, low, top):
    lane = lax.broadcasted_iota(jnp.int32, (1, 2 * size), 1)
    pos = jnp.where(lane < size, lane, lane - size) + row
    return (pos >= low) & (pos < top)


def pad_rows(img_ref, images, rows):
    r = lax.broadcasted_iota(jnp.int32, (rows, LANES), 0) + REACH
    inside = jnp.zeros((rows, LANES), jnp.bool_)
    for i in range(images):
        start = img_ref[i]
        inside = inside | ((r >= start) & (r < start + IMG))
    return ~inside


def fwd_kernel(images, img_ref, q_ref, k_ref, v_ref, o_ref, lse_ref, acc, lists, counts):
    rows = acc.shape[0]
    make_items(img_ref, lists, counts, rows, images)
    acc[...] = jnp.zeros_like(acc)

    def body(kind, size, n, carry):
        row, low, top, start, begin = item_scalars(lists, kind, n)
        qm = query_valid(size, row, low, top)
        done = []
        for u in range(FP):
            cols = slice(u * LANES, (u + 1) * LANES)
            q2 = halves(q_ref[pl.ds(pl.multiple_of(row + REACH, 16), size), cols])
            kw = k_ref[pl.ds(begin, SPAN), cols]
            vw = v_ref[pl.ds(begin, SPAN), cols]
            s = lax.dot_general(kw, q2, (((1,), (1,)), ((), ())), preferred_element_type=f32)
            s = mask_keys(s, start, begin)
            m = jnp.max(s, axis=0, keepdims=True)
            e = jnp.exp(s - m)
            l = jnp.sum(e, axis=0, keepdims=True)
            ot = lax.dot_general(vw, e.astype(bf16), (((0,), (0,)), ((), ())), preferred_element_type=f32)
            ot = ot * jnp.where(qm, 1.0 / l, 0.0)
            done.append((jnp.concatenate([ot[:HEAD, :size], ot[HEAD:, size:]], axis=0).T, m + jnp.log(l)))
        for u in range(FP):
            cols = slice(u * LANES, (u + 1) * LANES)
            acc[pl.ds(row, size), cols] += done[u][0]
            lse_ref[u, pl.ds(kind * SLOTS + n, 1), : 2 * size] = done[u][1]
        return carry

    for kind, size in enumerate(CHUNKS):
        lax.fori_loop(0, counts[kind], functools.partial(body, kind, size), 0)
    pad = pad_rows(img_ref, images, rows)
    for u in range(FP):
        cols = slice(u * LANES, (u + 1) * LANES)
        own = v_ref[pl.ds(REACH, rows), cols].astype(f32)
        o_ref[:, cols] = jnp.where(pad, own, acc[:, cols]).astype(bf16)


def attention_forward(img, q, k, v, first, pairs):
    win = k.shape[0]
    rows = win - 2 * REACH
    images = img.shape[0]
    spec = lambda r: pl.BlockSpec((r, FP * LANES), lambda p, *_: (0, first // FP + p))
    return pl.pallas_call(
        functools.partial(fwd_kernel, images),
        grid_spec=pltpu.PrefetchScalarGridSpec(
            num_scalar_prefetch=1,
            grid=(pairs // FP,),
            in_specs=[spec(win), spec(win), spec(win)],
            out_specs=[
                pl.BlockSpec((rows, FP * LANES), lambda p, *_: (0, p)),
                pl.BlockSpec((FP, 3 * SLOTS, 2 * CHUNKS[0]), lambda p, *_: (p, 0, 0)),
            ],
            scratch_shapes=[
                pltpu.VMEM((rows, FP * LANES), f32), pltpu.SMEM((3 * SLOTS * 4,), jnp.int32), pltpu.SMEM((3,), jnp.int32)
            ],
        ),
        out_shape=[
            jax.ShapeDtypeStruct((rows, pairs * LANES), bf16),
            jax.ShapeDtypeStruct((pairs, 3 * SLOTS, 2 * CHUNKS[0]), f32),
        ],
        compiler_params=pltpu.CompilerParams(vmem_limit_bytes=VMEM, dimension_semantics=("arbitrary",)),
        cost_estimate=spent(5 * pairs),
        name="attention_forward",
    )(img, q, k, v)


def bwd_kernel(images, img_ref, q_ref, k_ref, v_ref, g_ref, lse_ref,
               dq_ref, dk_ref, dv_ref, left_ref, right_ref, dq_acc, dk_acc, dv_acc, lists, counts):
    rows = dq_acc.shape[0]
    make_items(img_ref, lists, counts, rows, images)
    dq_acc[...] = jnp.zeros_like(dq_acc)
    dk_acc[...] = jnp.zeros_like(dk_acc)
    dv_acc[...] = jnp.zeros_like(dv_acc)

    def body(kind, size, n, carry):
        row, low, top, start, begin = item_scalars(lists, kind, n)
        qm = query_valid(size, row, low, top)
        done = []
        for u in range(PP):
            cols = slice(u * LANES, (u + 1) * LANES)
            q2 = halves(q_ref[pl.ds(pl.multiple_of(row + REACH, 16), size), cols])
            g2 = halves(g_ref[pl.ds(row, size), cols])
            kw = k_ref[pl.ds(begin, SPAN), cols]
            vw = v_ref[pl.ds(begin, SPAN), cols]
            lse = jnp.where(qm, lse_ref[u, pl.ds(kind * SLOTS + n, 1), : 2 * size], 1e30)
            s = lax.dot_general(kw, q2, (((1,), (1,)), ((), ())), preferred_element_type=f32)
            dp = lax.dot_general(vw, g2, (((1,), (1,)), ((), ())), preferred_element_type=f32)
            p = jnp.exp(mask_keys(s, start, begin) - lse)
            inner = jnp.sum(p * dp, axis=0, keepdims=True)
            ds = (p * (dp - inner)).astype(bf16)
            dv = jnp.dot(p.astype(bf16), g2, preferred_element_type=f32)
            dk = jnp.dot(ds, q2, preferred_element_type=f32)
            dqt = lax.dot_general(kw, ds, (((0,), (0,)), ((), ())), preferred_element_type=f32)
            done.append((dv, dk, jnp.concatenate([dqt[:HEAD, :size], dqt[HEAD:, size:]], axis=0).T))
        for u in range(PP):
            cols = slice(u * LANES, (u + 1) * LANES)
            dv, dk, dq = done[u]
            dv_acc[pl.ds(begin, SPAN), cols] += dv
            dk_acc[pl.ds(begin, SPAN), cols] += dk
            dq_acc[pl.ds(row, size), cols] += dq
        return carry

    for kind, size in enumerate(CHUNKS):
        lax.fori_loop(0, counts[kind], functools.partial(body, kind, size), 0)
    pad = pad_rows(img_ref, images, rows)
    dq_ref[...] = (dq_acc[...] * 0.125).astype(bf16)
    dk_ref[...] = dk_acc[pl.ds(REACH, rows), :]
    for u in range(PP):
        cols = slice(u * LANES, (u + 1) * LANES)
        dv_ref[:, cols] = dv_acc[pl.ds(REACH, rows), cols] + jnp.where(pad, g_ref[:, cols].astype(f32), 0.0)
    left_ref[0] = dk_acc[pl.ds(0, REACH), :].astype(bf16)
    left_ref[1] = dv_acc[pl.ds(0, REACH), :].astype(bf16)
    right_ref[0] = dk_acc[pl.ds(REACH + rows, REACH), :].astype(bf16)
    right_ref[1] = dv_acc[pl.ds(REACH + rows, REACH), :].astype(bf16)


def attention_backward(img, q, k, v, g, lse, first, pairs):
    win = k.shape[0]
    rows = win - 2 * REACH
    images = img.shape[0]
    C = PP * LANES
    spec = lambda r: pl.BlockSpec((r, C), lambda p, *_: (0, first // PP + p))
    out = lambda r: pl.BlockSpec((r, C), lambda p, *_: (0, p))
    edge = pl.BlockSpec((2, REACH, C), lambda p, *_: (0, 0, p))
    sds = jax.ShapeDtypeStruct
    cols = pairs * LANES
    return pl.pallas_call(
        functools.partial(bwd_kernel, images),
        grid_spec=pltpu.PrefetchScalarGridSpec(
            num_scalar_prefetch=1,
            grid=(pairs // PP,),
            in_specs=[spec(win), spec(win), spec(win), spec(rows),
                      pl.BlockSpec((PP, 3 * SLOTS, 2 * CHUNKS[0]), lambda p, *_: (first // PP + p, 0, 0))],
            out_specs=[out(rows), out(rows), out(rows), edge, edge],
            scratch_shapes=[pltpu.VMEM((rows, C), f32), pltpu.VMEM((win, C), f32), pltpu.VMEM((win, C), f32),
                            pltpu.SMEM((3 * SLOTS * 4,), jnp.int32), pltpu.SMEM((3,), jnp.int32)],
        ),
        out_shape=[sds((rows, cols), bf16), sds((rows, cols), f32), sds((rows, cols), f32),
                   sds((2, REACH, cols), bf16), sds((2, REACH, cols), bf16)],
        compiler_params=pltpu.CompilerParams(vmem_limit_bytes=VMEM, dimension_semantics=("arbitrary",)),
        cost_estimate=spent(6.5 * pairs),
        name="attention_backward",
    )(img, q, k, v, g, lse)


FT = 512
FINAL_TILE = 1024
ROWS = 1024


def contract(a, b, dims):
    return lax.dot_general(a, b, (dims, ((), ())), preferred_element_type=f32)


def feed_kernel(
    table, normed, cot, middle, bias_final, wide, tall, bias_hidden,
    result, grad_normed, bias_grad, hidden_near, hidden_far, active,
    total, normed_t, final, grad_pre, hidden_grad,
):
    step = pl.program_id(0)
    tiles = pl.num_programs(0)
    rows, width = normed.shape
    half, _, piece, _ = hidden_near.shape
    devices = tall.shape[0] // 32
    depth = FT // devices

    @pl.when(step == 0)
    def _():
        total[...] = middle[...] + bias_final[...]
        grad_normed[...] = jnp.zeros_like(grad_normed)
        normed_t[...] = normed[...].T

    for d in range(devices):
        for i in range(4):
            final[d * depth + i * 32 : d * depth + (i + 1) * 32, :] = tall[d * 32 : (d + 1) * 32, i * width : (i + 1) * width]
    for r in range(0, rows, ROWS):
        cut = slice(r, r + ROWS)
        pre = contract(normed[cut, :], wide[...], ((1,), (0,))) + bias_hidden[...]
        grad = contract(cot[cut, :], final[...], ((1,), (1,)))
        phi = 0.5 + 0.5 * lax.erf(pre * (0.5**0.5))
        slope = phi + pre * jnp.exp(pre * pre * -0.5) * ((0.5 / math.pi) ** 0.5)
        active[cut, :] = (pre * phi).astype(bf16)
        grad_pre[cut, :] = (grad * slope).astype(bf16)
        total[cut, :] += contract(active[cut, :], final[...], ((1,), (0,)))
        grad_normed[cut, :] += contract(grad_pre[cut, :], wide[...], ((1,), (1,)))
    bias_grad[...] = jnp.sum(grad_pre[...].astype(f32), axis=0, keepdims=True)
    hidden_grad[...] = contract(normed_t[...], grad_pre[...], ((1,), (0,)))
    for place in range(2 * half):
        rows_of = hidden_grad[pl.ds(pl.multiple_of(table[place] * piece, piece), piece), :].astype(bf16)
        if place < half:
            hidden_near[place, 0] = rows_of
        else:
            hidden_far[place - half, 0] = rows_of

    @pl.when(step == tiles - 1)
    def _():
        result[...] = total[...].astype(bf16)


def final_kernel(home, active, cot, final_near, final_far, final_grad, sems):
    step = pl.program_id(0)
    tiles = pl.num_programs(0)
    slot = lax.rem(step, 2)
    half, depth, width = final_near.shape
    devices = FINAL_TILE // depth

    def copy_out(slot, d, target):
        return pltpu.make_async_copy(final_grad.at[slot, d], target, sems.at[slot, d])

    def wait_out(slot):
        for d in range(devices):
            copy_out(slot, d, final_near.at[0]).wait()

    @pl.when(step >= 2)
    def _():
        wait_out(slot)

    final_grad[slot] = contract(active[...], cot[...], ((0,), (0,))).astype(bf16).reshape(devices, depth, width)
    for d in range(devices):
        at = home[step * devices + d]

        @pl.when(at < half)
        def _():
            copy_out(slot, d, final_near.at[at]).start()

        @pl.when(at >= half)
        def _():
            copy_out(slot, d, final_far.at[at - half]).start()

    @pl.when(step == tiles - 1)
    def _():
        for d in range(devices):
            copy_out(1 - slot, d, final_near.at[0]).wait()
            copy_out(slot, d, final_near.at[0]).wait()


def final_share(active, cot, home):
    rows, width = cot.shape
    units = active.shape[1]
    depth = units // PIECES
    piece = jax.ShapeDtypeStruct((PIECES // 2, depth, width), bf16)
    return pl.pallas_call(
        final_kernel,
        grid_spec=pltpu.PrefetchScalarGridSpec(
            num_scalar_prefetch=1,
            grid=(units // FINAL_TILE,),
            in_specs=[
                pl.BlockSpec((rows, FINAL_TILE), lambda t, *_: (0, t)),
                pl.BlockSpec((rows, width), lambda t, *_: (0, 0), pipeline_mode=pl.Buffered(1)),
            ],
            out_specs=[pl.BlockSpec(memory_space=pl.ANY)] * 2,
            scratch_shapes=[pltpu.VMEM((2, FINAL_TILE // depth, depth, width), bf16), pltpu.SemaphoreType.DMA((2, FINAL_TILE // depth))],
        ),
        out_shape=[piece, piece],
        compiler_params=pltpu.CompilerParams(vmem_limit_bytes=VMEM, dimension_semantics=("arbitrary",)),
        cost_estimate=spent(14),
        name="final_share",
    )(home, active, cot)


def feed_forward(normed, cot, middle, bias_final, feed, bias_hidden, table):
    rows, width = normed.shape
    units = bias_hidden.shape[1]
    whole = lambda *shape: pl.BlockSpec(shape, lambda t, *_: (0,) * len(shape), pipeline_mode=pl.Buffered(1))
    sds = jax.ShapeDtypeStruct
    depth = units // PIECES
    devices = FT // depth
    line = pl.BlockSpec((1, FT), lambda t, *_: (0, t))
    square = whole(rows, width)
    wide_piece = sds((PIECES // 2, units // width, width // PIECES, width), bf16)
    blocks = width // FT
    edge = pl.BlockSpec((PIECES // 2, 1, width // PIECES, FT), lambda t, *_: (0, t // blocks, 0, t % blocks))
    return pl.pallas_call(
        feed_kernel,
        grid_spec=pltpu.PrefetchScalarGridSpec(
            num_scalar_prefetch=1,
            grid=(units // FT,),
            in_specs=[
                square, square, square, whole(1, width),
                pl.BlockSpec((width, FT), lambda t, *_: (0, t)),
                pl.BlockSpec((devices * 32, 4 * width), lambda t, *_: (t, 1)),
                line,
            ],
            out_specs=[square, square, line, edge, edge, pl.BlockSpec((rows, FT), lambda t, *_: (0, t))],
            scratch_shapes=[
                pltpu.VMEM((rows, width), f32), pltpu.VMEM((width, rows), bf16), pltpu.VMEM((FT, width), bf16),
                pltpu.VMEM((rows, FT), bf16), pltpu.VMEM((width, FT), f32),
            ],
        ),
        out_shape=[
            sds((rows, width), bf16), sds((rows, width), f32), sds((1, units), f32),
            wide_piece, wide_piece, sds((rows, units), bf16),
        ],
        compiler_params=pltpu.CompilerParams(vmem_limit_bytes=VMEM, dimension_semantics=("arbitrary",)),
        cost_estimate=spent(57),
        name="feed_forward",
    )(table, normed, cot, middle, bias_final, feed, feed, bias_hidden)


def project_kernel(
    table_one, table_two, x, one_near, one_far, two_near, two_far,
    q_out, k_out, v_out, normed_out, weight, weight_out, vectors, small,
):
    half, piece, split = one_near.shape
    width = x.shape[1]
    wide = weight.shape[1]

    @pl.when(pl.program_id(0) == 0)
    def _():
        for place in range(2 * half):
            a, b, at = (one_near, two_near, place) if place < half else (one_far, two_far, place - half)
            rows = pl.ds(pl.multiple_of(table_one[place] * piece, piece), piece)
            weight[rows, :split] = a[at]
            rows = pl.ds(pl.multiple_of(table_two[place] * piece, piece), piece)
            weight[rows, split:] = b[at, :, : wide - split]
            weight_out[rows, :] = b[at, :, wide - split : wide - split + width]
            small[rows, :] = b[at, :, wide - split + width : wide - split + width + LANES].astype(f32)
        vectors[...] = small[...].T[: vectors.shape[0]]

    values = x[...].astype(f32)
    center = values - jnp.mean(values, axis=-1, keepdims=True)
    spread_of = jnp.mean(center * center, axis=-1, keepdims=True)
    normed = (center * lax.rsqrt(spread_of + norm_epsilon) * vectors[0:1, :] + vectors[1:2, :]).astype(bf16)
    normed_out[...] = normed
    cols = width // GROUPS
    needs_queries = (pl.program_id(0) == 1) | (pl.program_id(0) == 2)
    for group in range(GROUPS):
        out = slice(group * cols, (group + 1) * cols)
        begin = 3 * group * cols
        keys = jnp.dot(normed, weight[:, begin + cols : begin + 2 * cols], preferred_element_type=f32)
        values = jnp.dot(normed, weight[:, begin + 2 * cols : begin + 3 * cols], preferred_element_type=f32)
        k_out[:, out] = keys.astype(bf16)
        v_out[:, out] = (values + vectors[3:4, out]).astype(bf16)

        @pl.when(needs_queries)
        def _():
            queries = jnp.dot(normed, weight[:, begin : begin + cols], preferred_element_type=f32)
            q_out[:, out] = (queries + vectors[2:3, out]).astype(bf16) * jnp.asarray(HEAD**-0.5, bf16)


def project(window, one, two, tables):
    rows, width = window.shape
    half, piece, split = one[0].shape
    block = rows // 4
    whole = lambda *shape: pl.BlockSpec(shape, lambda t, *_: (0,) * len(shape), pipeline_mode=pl.Buffered(1))
    strip = pl.BlockSpec((block, width), lambda t, *_: (t, 0))
    sds = jax.ShapeDtypeStruct
    return pl.pallas_call(
        project_kernel,
        grid_spec=pltpu.PrefetchScalarGridSpec(
            num_scalar_prefetch=2,
            grid=(4,),
            in_specs=[strip] + [whole(half, piece, split)] * 2 + [whole(*two[0].shape)] * 2,
            out_specs=[strip] * 4 + [whole(width, 3 * width), whole(width, width), whole(16, width)],
            scratch_shapes=[pltpu.VMEM((width, LANES), f32)],
        ),
        out_shape=[sds((rows, width), bf16)] * 4 + [sds((width, 3 * width), bf16), sds((width, width), bf16), sds((16, width), f32)],
        compiler_params=pltpu.CompilerParams(vmem_limit_bytes=VMEM, dimension_semantics=("arbitrary",)),
        cost_estimate=spent(24),
        name="project",
    )(*tables, window, *one, *two)


CW = 256


def share_kernel(
    extra, table, normed, dq, dk, dv, left, right, *refs,
):
    if extra:
        mixed, branch, packed, sums, near, far, normed_t, mixed_t, product, x = refs
    else:
        packed, sums, near, far, product, x = refs
        normed_t = normed
    step = pl.program_id(0)
    rows = dq.shape[0]
    half, piece, _ = near.shape

    if extra:
        @pl.when(step == 0)
        def _():
            normed_t[...] = normed[pl.ds(REACH, rows), :].T

    def halo(own, number):
        x[...] = own[...].astype(bf16)
        edge = rows - REACH
        x[:edge, :] = (own[:edge, :] + left[number, :edge, :].astype(f32)).astype(bf16)
        x[edge:REACH, :] = (own[edge:REACH, :] + left[number, edge:, :].astype(f32) + right[number, : REACH - edge, :].astype(f32)).astype(bf16)
        x[REACH:, :] = (own[REACH:, :] + right[number, REACH - edge :, :].astype(f32)).astype(bf16)

    @pl.when(step < 2)
    def _():
        x[...] = dq[...]

    @pl.when((step >= 2) & (step < 4))
    def _():
        halo(dk, 0)

    @pl.when((step >= 4) & (step < 6))
    def _():
        halo(dv, 1)

    if extra:
        @pl.when(step == 6)
        def _():
            mixed_t[...] = mixed[...].T

        @pl.when(step >= 6)
        def _():
            x[...] = branch[...]

    @pl.when(step < 6)
    def _():
        packed[...] = x[...]

    sums[...] = jnp.sum(x[...].astype(f32), axis=0, keepdims=True)
    if extra:
        @pl.when(step < 6)
        def _():
            product[...] = jnp.dot(normed_t[...], x[...], preferred_element_type=f32)

        @pl.when(step >= 6)
        def _():
            product[...] = jnp.dot(mixed_t[...], x[...], preferred_element_type=f32)
    else:
        product[...] = jnp.dot(normed_t[...], x[...], preferred_element_type=f32)
    for place in range(2 * half):
        rows_of = product[pl.ds(pl.multiple_of(table[place] * piece, piece), piece), :].astype(bf16)
        if place < half:
            near[place] = rows_of
        else:
            far[place - half] = rows_of


def weight_share(normed, dq, dk, dv, left, right, table, extra=()):
    rows, cols = dq.shape
    width = normed.shape[1]
    steps = 6 + (4 if extra else 0)
    whole = lambda *shape: pl.BlockSpec(shape, lambda t, *_: (0,) * len(shape), pipeline_mode=pl.Buffered(1))
    clip = lambda t, low, top: jnp.minimum(jnp.maximum(t - low, 0), top)
    tall = lambda low, top: pl.BlockSpec((rows, CW), lambda t, *_: (0, clip(t, low, top)))
    edge = pl.BlockSpec((2, REACH, CW), lambda t, *_: (0, 0, jnp.where(t < 4, clip(t, 2, 1), clip(t, 4, 1))))
    piece = pl.BlockSpec((PIECES // 2, width // PIECES, CW), lambda t, *_: (0, 0, t))
    sds = jax.ShapeDtypeStruct
    pieces = sds((PIECES // 2, width // PIECES, steps * CW), bf16)
    return pl.pallas_call(
        functools.partial(share_kernel, bool(extra)),
        grid_spec=pltpu.PrefetchScalarGridSpec(
            num_scalar_prefetch=1,
            grid=(steps,),
            in_specs=[whole(*normed.shape), tall(0, 1), tall(2, 1), tall(4, 1), edge, edge]
            + ([whole(rows, width), tall(6, 3)] if extra else []),
            out_specs=[tall(0, 5), pl.BlockSpec((1, CW), lambda t, *_: (0, t))]
            + [piece] * 2 + ([whole(width, rows)] if extra else []),
            scratch_shapes=([pltpu.VMEM((width, rows), bf16)] if extra else [])
            + [pltpu.VMEM((width, CW), f32), pltpu.VMEM((rows, CW), bf16)],
        ),
        out_shape=[sds((rows, 6 * CW), bf16), sds((1, steps * CW), f32), pieces, pieces] + ([sds((width, rows), bf16)] if extra else []),
        compiler_params=pltpu.CompilerParams(vmem_limit_bytes=VMEM, dimension_semantics=("arbitrary",)),
        cost_estimate=spent(10 if extra else 7),
        name="weight_share",
    )(table, normed, dq, dk, dv, left, right, *extra)


def norm_backward(values, gain, grad):
    center = values - jnp.mean(values, axis=-1, keepdims=True)
    scale = lax.rsqrt(jnp.mean(center * center, axis=-1, keepdims=True) + norm_epsilon)
    unit = center * scale
    scaled = grad * gain
    moved = scaled - jnp.mean(scaled, axis=-1, keepdims=True) - unit * jnp.mean(scaled * unit, axis=-1, keepdims=True)
    column = lambda x: jnp.sum(x, axis=0, keepdims=True)
    return scale * moved, column(grad * unit), column(grad)


def branch_kernel(grad, middle, cot, weight_out, vectors, total, branch, mixed, sums):
    @pl.when(pl.program_id(0) == 0)
    def _():
        sums[...] = jnp.zeros_like(sums)

    up = cot[...].astype(f32)
    moved, gain_sum, bias_sum = norm_backward(middle[...], vectors[5:6, :], grad[...])
    total[...] = up + moved
    branch[...] = total[...].astype(bf16)
    mixed[...] = contract(branch[...], weight_out[...], ((1,), (1,))).astype(bf16)
    sums[0:1, :] += gain_sum
    sums[1:2, :] += bias_sum
    sums[2:3, :] += jnp.sum(up, axis=0, keepdims=True)


def input_kernel(one, two, weight, tokens, middle_grad, vectors, out, sums):
    @pl.when(pl.program_id(0) == 0)
    def _():
        sums[...] = jnp.zeros_like(sums)

    cols = one.shape[1]
    grad = contract(one[...], weight[:, :cols], ((1,), (1,))) + contract(two[...], weight[:, cols:], ((1,), (1,)))
    moved, gain_sum, bias_sum = norm_backward(tokens[...].astype(f32), vectors[0:1, :], grad)
    out[...] = (middle_grad[...] + moved).astype(bf16)
    sums[0:1, :] += gain_sum
    sums[1:2, :] += bias_sum


def row_blocks(kernel, name, blocked, whole, outs, us):
    rows, width = blocked[0].shape[0], outs[0][0]
    block = rows // 4
    strip = lambda cols: pl.BlockSpec((block, cols), lambda t: (t, 0))
    fixed = lambda *shape: pl.BlockSpec(shape, lambda t: (0,) * len(shape), pipeline_mode=pl.Buffered(1))
    return pl.pallas_call(
        kernel,
        grid=(4,),
        in_specs=[strip(a.shape[1]) for a in blocked] + [fixed(*a.shape) for a in whole],
        out_specs=[strip(cols) for cols, _ in outs] + [fixed(8, width)],
        out_shape=[jax.ShapeDtypeStruct((rows, cols), kind) for cols, kind in outs] + [jax.ShapeDtypeStruct((8, width), f32)],
        compiler_params=pltpu.CompilerParams(vmem_limit_bytes=VMEM, dimension_semantics=("arbitrary",)),
        cost_estimate=spent(us),
        name=name,
    )(*blocked, *whole)


def branch_gradient(grad, middle, cot, weight_out, vectors):
    width = middle.shape[1]
    outs = [(width, f32), (width, bf16), (width, bf16)]
    return row_blocks(branch_kernel, "branch_gradient", [grad, middle, cot], [weight_out, vectors], outs, 10)


def input_gradient(one, two, tokens, middle_grad, weight, vectors):
    def kernel(one, two, tokens, middle_grad, weight, vectors, out, sums):
        input_kernel(one, two, weight, tokens, middle_grad, vectors, out, sums)

    return row_blocks(kernel, "input_gradient", [one, two, tokens, middle_grad], [weight, vectors], [(tokens.shape[1], bf16)], 12)


def bit_orders(count):
    bits = [1 << i for i in range(count.bit_length() - 1)]
    return (bits[0], bits[2], bits[1], *bits[3:]), (bits[0], bits[1], bits[2], *bits[3:])


def exchange(x, bit, count):
    return lax.ppermute(x, "dev", [(i, i ^ bit) for i in range(count)])


def owners(order, me):
    table = []
    for place in range(PIECES):
        offset = 0
        for i, bit in enumerate(order):
            if (place >> (len(order) - 1 - i)) & 1:
                offset |= bit
        table.append(offset)
    return jnp.array(table, jnp.int32) ^ me


def places(order, me):
    offset = jnp.arange(PIECES, dtype=jnp.int32) ^ me
    return sum(jnp.where(offset & bit != 0, 1 << (len(order) - 1 - i), 0) for i, bit in enumerate(order)).astype(jnp.int32)


def gather_step(held, order, step, count):
    bit = order[len(order) - 1 - step]
    arrived = exchange(held, bit, count)
    return (held, arrived) if bit == order[0] else jnp.concatenate([held, arrived], axis=0)


def total(parts, kind=bf16):
    return functools.reduce(lambda a, b: a + b, [p.astype(f32) for p in parts]).astype(kind)


def straight(parts, bits, count):
    size = parts[0].shape[0] // (len(bits) + 1)
    return [exchange(total([p[(i + 1) * size : (i + 2) * size] for p in parts]), bit, count) for i, bit in enumerate(bits)]


def scatter_whole(near, far, count):
    whole = jnp.concatenate([near, far], axis=0).reshape(-1, near.shape[2])
    return lax.psum_scatter(whole.astype(f32), "dev", scatter_dimension=0, tiled=True)


def layer_norm(values, gain, bias):
    center = values - jnp.mean(values, axis=-1, keepdims=True)
    spread_of = jnp.mean(center * center, axis=-1, keepdims=True)
    return center * lax.rsqrt(spread_of + norm_epsilon) * gain + bias


def exact_gelu(values):
    return jax.nn.gelu(values, approximate=False)


def image_starts(segment_ids, me, rows):
    padded = jnp.pad(segment_ids, (REACH, REACH), constant_values=-2)
    window = lax.dynamic_slice_in_dim(padded, me * rows, rows + 2 * REACH, 0)
    own = window[REACH : REACH + rows]
    far = jnp.int32(1 << 20)
    first = jnp.min(jnp.where(own >= 0, own, far))
    places = jnp.arange(rows + 2 * REACH, dtype=jnp.int32)
    images = (rows - 2) // IMG + 2
    starts = []
    for i in range(images):
        start = jnp.min(jnp.where(window == first + i, places, far))
        starts.append(jnp.where(start == far, -far, start))
    return jnp.stack(starts)


def per_device(
    tokens,
    segment_ids,
    first_gain,
    first_bias,
    qkv_weight,
    query_bias,
    value_bias,
    out_weight,
    out_bias,
    second_gain,
    second_bias,
    hidden_weight,
    hidden_bias,
    final_weight,
    final_bias,
    cotangent,
):
    count = lax.axis_size("dev")
    me = lax.axis_index("dev")
    direct = count == PIECES
    rows, width = tokens.shape
    hidden_width = hidden_weight.shape[1]
    pairs = width // LANES
    part = width // count
    part_rows = width // PIECES
    half = PIECES // 2
    unit = hidden_width // PIECES
    orders = bit_orders(PIECES)
    tables = [owners(order, me) if direct else jnp.arange(PIECES, dtype=jnp.int32) for order in orders]
    home = places(orders[0], me) if direct else jnp.arange(PIECES, dtype=jnp.int32)
    sync = lax.optimization_barrier
    img = image_starts(segment_ids, me, rows)
    to_right = [(i, i + 1) for i in range(count - 1)]
    to_left = [(i + 1, i) for i in range(count - 1)]
    send = lambda left, right: (lax.ppermute(right, "dev", to_right), lax.ppermute(left, "dev", to_left))

    vectors = [first_gain, first_bias, query_bias, value_bias, out_bias, second_gain, second_bias, final_bias]
    small = sync(jnp.concatenate([jnp.stack(vectors, axis=1), hidden_bias.reshape(part, -1)], axis=1)).astype(bf16)
    small = jnp.pad(small, ((0, 0), (0, LANES - small.shape[1])))
    cols = width // GROUPS
    qkv_low = qkv_weight.astype(bf16)
    qkv_low = jnp.concatenate(
        [qkv_low[:, i * width + g * cols : i * width + (g + 1) * cols] for g in range(GROUPS) for i in range(3)], axis=1
    )
    split = 2 * width
    early = jnp.concatenate([qkv_low, out_weight.astype(bf16), small], axis=1)
    hidden_low = hidden_weight.astype(bf16)
    final_low = final_weight.astype(bf16)
    if direct:
        feed = jnp.concatenate([hidden_low] + [final_low[32 * i : 32 * (i + 1)] for i in range(4)], axis=1)
        halo = send(tokens[:REACH], tokens[rows - REACH :])
        line = [exchange(early[None], bit, count) for bit in (orders[0][4], orders[0][3], orders[0][3] | orders[0][4])]
        line, halo, feed = sync((line, halo, feed)) if FEED_AFTER == 1 else (*sync((line, halo)), feed)
        held = [jnp.concatenate([p[..., cut] for p in (early[None], *line)], axis=0) for cut in (slice(0, split), slice(split, None))]
        held = [gather_step(h, o, 2, count) for h, o in zip(held, orders)]
        if FEED_AFTER == 2:
            held, feed = sync((held, feed))
        held = [gather_step(h, o, 3, count) for h, o in zip(held, orders)]
        if FEED_AFTER == 3:
            held, feed = sync((held, feed))
        held = [gather_step(h, o, 4, count) for h, o in zip(held, orders)]
        feed = lax.all_gather(feed, "dev", axis=0, tiled=True)
        one, two = held
    else:
        early = lax.all_gather(early, "dev", axis=0, tiled=True).reshape(PIECES, width // PIECES, -1)
        one, two = [jnp.split(p, 2) for p in (early[..., :split], early[..., split:])]
        hidden_low = lax.all_gather(hidden_low, "dev", axis=0, tiled=True)
        final_low = lax.all_gather(final_low, "dev", axis=0, tiled=True)
        final_low = final_low.reshape(PIECES, 4, 32, width).transpose(0, 2, 1, 3).reshape(width, 4 * width)
        feed = jnp.concatenate([hidden_low, final_low], axis=1)
        halo = send(tokens[:REACH], tokens[rows - REACH :])
    window = jnp.concatenate([halo[0], tokens, halo[1]], axis=0)
    inputs = tokens.astype(f32)
    queries, key_rows, value_rows, normed, weight_qkv, weight_out, vectors = project(window, one, two, tables)
    gain_one, bias_one, bias_query, bias_value, bias_out, gain_two, bias_two, bias_final = [vectors[i] for i in range(8)]
    bias_hidden = vectors[8 : 8 + hidden_width // width].T.reshape(1, hidden_width)
    mixed_low, totals = attention_forward(img, queries, key_rows, value_rows, 0, pairs)
    middle = inputs + (jnp.dot(mixed_low, weight_out, preferred_element_type=f32) + bias_out)
    normed_two = layer_norm(middle, gain_two, bias_two).astype(bf16)
    result, grad_normed_two, hidden_bias_grad, *hidden_grads, active = feed_forward(
        normed_two, cotangent, middle, bias_final[None], feed, bias_hidden, tables[1]
    )
    step = pairs // GROUPS
    blocks = lambda pair: [g.reshape(g.shape[0], -1, part_rows, width) for g in pair]
    hidden_grads = blocks(hidden_grads)
    if direct:
        hidden_got = [hidden_grads[0], exchange(hidden_grads[1], orders[1][0], count)]
    final_grads = blocks(final_share(active, cotangent, home))
    if direct:
        hidden_got, final_grads, grad_normed_two = sync((hidden_got, final_grads, grad_normed_two))
        final_got = [final_grads[0], exchange(final_grads[1], orders[0][0], count)]
        away = total([p[8:] for p in hidden_got])
        away, grad_normed_two = sync((away, grad_normed_two))
        moving = [exchange(away, orders[1][1], count)]
    middle_grad, grad_branch, grad_mixed, sums_mid = branch_gradient(grad_normed_two, middle, cotangent, weight_out, vectors)
    if direct:
        final_got, grad_mixed = sync((final_got, grad_mixed))
        away = total([p[8:] for p in final_got])
        away, grad_mixed = sync((away, grad_mixed))
        moving.append(exchange(away, orders[0][1], count))
        got = [hidden_got, final_got]
        turns = orders[1], orders[0]
    else:
        grads = [hidden_grads, final_grads]
    first = attention_backward(img, queries, key_rows, value_rows, grad_mixed, totals, 0, step)
    if direct:
        grad_mixed, first = sync((grad_mixed, first))
    halo = send(*first[3:])
    second = attention_backward(img, queries, key_rows, value_rows, grad_mixed, totals, step, step)
    if direct:
        moving, first, second, halo, normed, grad_branch = sync((moving, first, second, halo, normed, grad_branch))
        got = [parts + [m] for parts, m in zip(got, moving)]
        away = [total([p[4:8] for p in parts]) for parts in got]
        away, first, second, halo, normed, grad_branch = sync((away, first, second, halo, normed, grad_branch))
        moving = [exchange(a, order[2], count) for a, order in zip(away, turns)]
    next_halo = send(*second[3:])
    packed_one, sums_one, *share_one, turned = weight_share(normed, *first[:3], *halo, tables[0], (mixed_low, grad_branch))
    if direct:
        moving, second, next_halo, turned, share_one = sync((moving, second, next_halo, turned, share_one))
        got = [parts + [m] for parts, m in zip(got, moving)]
        away = jnp.concatenate([total([p[2:4] for p in parts]) for parts in got], axis=0)
        away, second, next_halo, turned, share_one = sync((away, second, next_halo, turned, share_one))
        lined = exchange(away, orders[0][3], count)
        share_one = [share_one[0], exchange(share_one[1], orders[0][0], count)]
    packed_two, sums_two, *share_two = weight_share(turned, *second[:3], *next_halo, tables[0])
    plane = (orders[0][2], orders[0][1], orders[0][1] | orders[0][2])
    line = (orders[0][4], orders[0][3], orders[0][3] | orders[0][4])
    if direct:
        share_one, share_two, packed_one, packed_two = sync((share_one, share_two, packed_one, packed_two))
        plane_one = straight(share_one, plane, count)
        share_two = [share_two[0], exchange(share_two[1], orders[0][0], count)]
    input_grad, sums_first = input_gradient(packed_one, packed_two, tokens, middle_grad, weight_qkv, vectors)
    pick = lambda i: jnp.concatenate([s[:, i * cols : (i + 1) * cols] for s in (sums_one, sums_two)], axis=1)
    sums = jnp.concatenate([sums_first[:2], pick(0), pick(2), sums_one[:, 3 * cols :], sums_mid[:3]], axis=0)
    sums = jnp.concatenate(
        [sums.reshape(8, count, part).transpose(1, 0, 2).reshape(count, 8 * part), hidden_bias_grad.reshape(count, -1)], axis=1
    )
    if direct:
        sums = lax.all_to_all(sums, "dev", 0, 0, tiled=True)
        lined, plane_one, share_one, share_two, input_grad, sums = sync((lined, plane_one, share_one, share_two, input_grad, sums))
        got = [parts + [lined[2 * i : 2 * i + 2]] for i, parts in enumerate(got)]
        ended = exchange(jnp.concatenate([total([p[1:2] for p in parts]) for parts in got], axis=0), orders[0][4], count)
        plane_two = straight(share_two, plane, count)
        share_one = [p[:4] for p in share_one] + plane_one
        lined = exchange(total([p[2:4] for p in share_one]), orders[0][3], count)
        lined, plane_two, share_two, sums, ended, got = sync((lined, plane_two, share_two, sums, ended, got))
        share_one = [p[:2] for p in share_one] + [lined]
        share_two = [p[:4] for p in share_two] + plane_two
        away = [total([p[1:2] for p in share_one])] + [total([p[i : i + 1] for p in share_two]) for i in (1, 2, 3)]
        away, ended, got = sync((away, ended, got))
        last_one, *last_two = [exchange(a, bit, count) for a, bit in zip(away, (orders[0][4], *line))]
        finals = [total([p[0] for p in parts] + [ended[i]], f32) for i, parts in enumerate(got)]
        hidden_shard = finals[0].transpose(1, 0, 2).reshape(part, hidden_width)
        final_shard = finals[1].reshape(-1, width)
        shards_one = total([p[0] for p in share_one] + [last_one[0]], f32)
        shards_two = total([p[0] for p in share_two] + [p[0] for p in last_two], f32)
    else:
        sums = lax.all_to_all(sums, "dev", 0, 0, tiled=True)
        shards_one, shards_two = scatter_whole(*share_one, count), scatter_whole(*share_two, count)
        finals = [jnp.concatenate(g, axis=0) for g in grads]
        finals[0] = finals[0].transpose(0, 2, 1, 3).reshape(width, hidden_width)
        finals[1] = finals[1].reshape(hidden_width, width)
        hidden_shard, final_shard = [lax.psum_scatter(p.astype(f32), "dev", scatter_dimension=0, tiled=True) for p in finals]
    sums = jnp.sum(sums, axis=0)
    own = [sums[i * part : (i + 1) * part] for i in range(8)]
    own_hidden = sums[8 * part :]
    out_shard = shards_one[:, 3 * cols :]
    qkv_shard = jnp.concatenate([h[:, i * cols : (i + 1) * cols] for i in range(3) for h in (shards_one, shards_two)], axis=1)
    return (
        result,
        input_grad,
        own[0],
        own[1],
        qkv_shard,
        own[2],
        own[3],
        out_shard,
        own[4],
        own[5],
        own[6],
        hidden_shard,
        own_hidden,
        final_shard,
        own[7],
    )


def solution(mesh):
    split = P("dev", None)
    line = P("dev")
    return jax.shard_map(
        per_device,
        mesh=mesh,
        in_specs=(split, P(), line, line, split, line, line, split, line, line, line, split, line, split, line, split),
        out_specs=(split, split, line, line, split, line, line, split, line, line, line, split, line, split, line),
        check_vma=False,
    )
```

```python
import functools
import math

import jax
import jax.numpy as jnp
from jax import lax
from jax.experimental import pallas as pl
from jax.experimental.pallas import tpu as pltpu
from jax.sharding import PartitionSpec as P

IMG = 577
REACH = IMG - 1
HEAD = 64
SPAN = 592
LANES = 128
PP = 2
PIECES = 32
PACE = 1.0e5
FEED_AFTER = 2
GROUPS = 2
VMEM = 60 * 1024 * 1024
f32 = jnp.float32
bf16 = jnp.bfloat16

norm_epsilon = 1e-06


def spent(us):
    return pl.CostEstimate(flops=0, bytes_accessed=int(us * PACE), transcendentals=0)


FP = 4
SLOTS = 8
CHUNKS = (384, 256, 128)


def make_items(img_ref, lists, counts, rows, images):
    for kind in range(len(CHUNKS)):
        counts[kind] = 0

    def add(kind, first, begin, end, start):
        size = CHUNKS[kind]
        n = counts[kind]
        base = (kind * SLOTS + n) * 4
        lists[base] = jnp.minimum(first, rows - size)
        lists[base + 1] = jnp.maximum(first, begin)
        lists[base + 2] = jnp.minimum(first + size, end)
        lists[base + 3] = start
        counts[kind] = n + 1

    for i in range(images):
        start = img_ref[i]
        begin = jnp.maximum(start - REACH, 0)
        end = jnp.minimum(start - REACH + IMG, rows)
        low = (begin // 16) * 16
        left = jnp.where(end > begin, end - low, 0)

        @pl.when(left > 512)
        def _():
            add(0, low, begin, end, start)
            add(1, low + 384, begin, end, start)

        @pl.when((left > 384) & (left <= 512))
        def _():
            add(1, low, begin, end, start)
            add(1, low + 256, begin, end, start)

        @pl.when((left > 256) & (left <= 384))
        def _():
            add(0, low, begin, end, start)

        @pl.when((left > 128) & (left <= 256))
        def _():
            add(1, low, begin, end, start)

        @pl.when((left > 0) & (left <= 128))
        def _():
            add(2, low, begin, end, start)


def item_scalars(lists, kind, n):
    base = (kind * SLOTS + n) * 4
    start = lists[base + 3]
    begin = pl.multiple_of((start // 16) * 16, 16)
    return pl.multiple_of(lists[base], 16), lists[base + 1], lists[base + 2], start, begin


def halves(x):
    lane = lax.broadcasted_iota(jnp.int32, x.shape, 1)
    zero = jnp.zeros_like(x)
    return jnp.concatenate([jnp.where(lane < HEAD, x, zero), jnp.where(lane >= HEAD, x, zero)], axis=0)


def mask_keys(scores, start, begin):
    def masked(low, top):
        r = lax.broadcasted_iota(jnp.int32, (top - low, 1), 0) + (low + begin - start)
        return jnp.where((r >= 0) & (r < IMG), scores[low:top], -1e30)

    return jnp.concatenate([masked(0, 16), scores[16 : SPAN - 16], masked(SPAN - 16, SPAN)], axis=0)


def query_valid(size, row, low, top):
    lane = lax.broadcasted_iota(jnp.int32, (1, 2 * size), 1)
    pos = jnp.where(lane < size, lane, lane - size) + row
    return (pos >= low) & (pos < top)


def pad_rows(img_ref, images, rows):
    r = lax.broadcasted_iota(jnp.int32, (rows, LANES), 0) + REACH
    inside = jnp.zeros((rows, LANES), jnp.bool_)
    for i in range(images):
        start = img_ref[i]
        inside = inside | ((r >= start) & (r < start + IMG))
    return ~inside


def fwd_kernel(images, img_ref, q_ref, k_ref, v_ref, o_ref, lse_ref, acc, lists, counts):
    rows = acc.shape[0]
    make_items(img_ref, lists, counts, rows, images)
    acc[...] = jnp.zeros_like(acc)

    def body(kind, size, n, carry):
        row, low, top, start, begin = item_scalars(lists, kind, n)
        qm = query_valid(size, row, low, top)
        done = []
        for u in range(FP):
            cols = slice(u * LANES, (u + 1) * LANES)
            q2 = halves(q_ref[pl.ds(pl.multiple_of(row + REACH, 16), size), cols])
            kw = k_ref[pl.ds(begin, SPAN), cols]
            vw = v_ref[pl.ds(begin, SPAN), cols]
            s = lax.dot_general(kw, q2, (((1,), (1,)), ((), ())), preferred_element_type=f32)
            s = mask_keys(s, start, begin)
            m = jnp.max(s, axis=0, keepdims=True)
            e = jnp.exp(s - m)
            l = jnp.sum(e, axis=0, keepdims=True)
            ot = lax.dot_general(vw, e.astype(bf16), (((0,), (0,)), ((), ())), preferred_element_type=f32)
            ot = ot * jnp.where(qm, 1.0 / l, 0.0)
            done.append((jnp.concatenate([ot[:HEAD, :size], ot[HEAD:, size:]], axis=0).T, m + jnp.log(l)))
        for u in range(FP):
            cols = slice(u * LANES, (u + 1) * LANES)
            acc[pl.ds(row, size), cols] += done[u][0]
            lse_ref[u, pl.ds(kind * SLOTS + n, 1), : 2 * size] = done[u][1]
        return carry

    for kind, size in enumerate(CHUNKS):
        lax.fori_loop(0, counts[kind], functools.partial(body, kind, size), 0)
    pad = pad_rows(img_ref, images, rows)
    for u in range(FP):
        cols = slice(u * LANES, (u + 1) * LANES)
        own = v_ref[pl.ds(REACH, rows), cols].astype(f32)
        o_ref[:, cols] = jnp.where(pad, own, acc[:, cols]).astype(bf16)


def attention_forward(img, q, k, v, first, pairs):
    win = k.shape[0]
    rows = win - 2 * REACH
    images = img.shape[0]
    spec = lambda r: pl.BlockSpec((r, FP * LANES), lambda p, *_: (0, first // FP + p))
    return pl.pallas_call(
        functools.partial(fwd_kernel, images),
        grid_spec=pltpu.PrefetchScalarGridSpec(
            num_scalar_prefetch=1,
            grid=(pairs // FP,),
            in_specs=[spec(win), spec(win), spec(win)],
            out_specs=[
                pl.BlockSpec((rows, FP * LANES), lambda p, *_: (0, p)),
                pl.BlockSpec((FP, 3 * SLOTS, 2 * CHUNKS[0]), lambda p, *_: (p, 0, 0)),
            ],
            scratch_shapes=[
                pltpu.VMEM((rows, FP * LANES), f32), pltpu.SMEM((3 * SLOTS * 4,), jnp.int32), pltpu.SMEM((3,), jnp.int32)
            ],
        ),
        out_shape=[
            jax.ShapeDtypeStruct((rows, pairs * LANES), bf16),
            jax.ShapeDtypeStruct((pairs, 3 * SLOTS, 2 * CHUNKS[0]), f32),
        ],
        compiler_params=pltpu.CompilerParams(vmem_limit_bytes=VMEM, dimension_semantics=("arbitrary",)),
        cost_estimate=spent(5 * pairs),
        name="attention_forward",
    )(img, q, k, v)


def bwd_kernel(images, img_ref, q_ref, k_ref, v_ref, g_ref, lse_ref,
               dq_ref, dk_ref, dv_ref, left_ref, right_ref, dq_acc, dk_acc, dv_acc, lists, counts):
    rows = dq_acc.shape[0]
    make_items(img_ref, lists, counts, rows, images)
    dq_acc[...] = jnp.zeros_like(dq_acc)
    dk_acc[...] = jnp.zeros_like(dk_acc)
    dv_acc[...] = jnp.zeros_like(dv_acc)

    def body(kind, size, n, carry):
        row, low, top, start, begin = item_scalars(lists, kind, n)
        qm = query_valid(size, row, low, top)
        done = []
        for u in range(PP):
            cols = slice(u * LANES, (u + 1) * LANES)
            q2 = halves(q_ref[pl.ds(pl.multiple_of(row + REACH, 16), size), cols])
            g2 = halves(g_ref[pl.ds(row, size), cols])
            kw = k_ref[pl.ds(begin, SPAN), cols]
            vw = v_ref[pl.ds(begin, SPAN), cols]
            lse = jnp.where(qm, lse_ref[u, pl.ds(kind * SLOTS + n, 1), : 2 * size], 1e30)
            s = lax.dot_general(kw, q2, (((1,), (1,)), ((), ())), preferred_element_type=f32)
            dp = lax.dot_general(vw, g2, (((1,), (1,)), ((), ())), preferred_element_type=f32)
            p = jnp.exp(mask_keys(s, start, begin) - lse)
            inner = jnp.sum(p * dp, axis=0, keepdims=True)
            ds = (p * (dp - inner)).astype(bf16)
            dv = jnp.dot(p.astype(bf16), g2, preferred_element_type=f32)
            dk = jnp.dot(ds, q2, preferred_element_type=f32)
            dqt = lax.dot_general(kw, ds, (((0,), (0,)), ((), ())), preferred_element_type=f32)
            done.append((dv, dk, jnp.concatenate([dqt[:HEAD, :size], dqt[HEAD:, size:]], axis=0).T))
        for u in range(PP):
            cols = slice(u * LANES, (u + 1) * LANES)
            dv, dk, dq = done[u]
            dv_acc[pl.ds(begin, SPAN), cols] += dv
            dk_acc[pl.ds(begin, SPAN), cols] += dk
            dq_acc[pl.ds(row, size), cols] += dq
        return carry

    for kind, size in enumerate(CHUNKS):
        lax.fori_loop(0, counts[kind], functools.partial(body, kind, size), 0)
    pad = pad_rows(img_ref, images, rows)
    dq_ref[...] = (dq_acc[...] * 0.125).astype(bf16)
    dk_ref[...] = dk_acc[pl.ds(REACH, rows), :]
    for u in range(PP):
        cols = slice(u * LANES, (u + 1) * LANES)
        dv_ref[:, cols] = dv_acc[pl.ds(REACH, rows), cols] + jnp.where(pad, g_ref[:, cols].astype(f32), 0.0)
    left_ref[0] = dk_acc[pl.ds(0, REACH), :].astype(bf16)
    left_ref[1] = dv_acc[pl.ds(0, REACH), :].astype(bf16)
    right_ref[0] = dk_acc[pl.ds(REACH + rows, REACH), :].astype(bf16)
    right_ref[1] = dv_acc[pl.ds(REACH + rows, REACH), :].astype(bf16)


def attention_backward(img, q, k, v, g, lse, first, pairs):
    win = k.shape[0]
    rows = win - 2 * REACH
    images = img.shape[0]
    C = PP * LANES
    spec = lambda r: pl.BlockSpec((r, C), lambda p, *_: (0, first // PP + p))
    out = lambda r: pl.BlockSpec((r, C), lambda p, *_: (0, p))
    edge = pl.BlockSpec((2, REACH, C), lambda p, *_: (0, 0, p))
    sds = jax.ShapeDtypeStruct
    cols = pairs * LANES
    return pl.pallas_call(
        functools.partial(bwd_kernel, images),
        grid_spec=pltpu.PrefetchScalarGridSpec(
            num_scalar_prefetch=1,
            grid=(pairs // PP,),
            in_specs=[spec(win), spec(win), spec(win), spec(rows),
                      pl.BlockSpec((PP, 3 * SLOTS, 2 * CHUNKS[0]), lambda p, *_: (first // PP + p, 0, 0))],
            out_specs=[out(rows), out(rows), out(rows), edge, edge],
            scratch_shapes=[pltpu.VMEM((rows, C), f32), pltpu.VMEM((win, C), f32), pltpu.VMEM((win, C), f32),
                            pltpu.SMEM((3 * SLOTS * 4,), jnp.int32), pltpu.SMEM((3,), jnp.int32)],
        ),
        out_shape=[sds((rows, cols), bf16), sds((rows, cols), f32), sds((rows, cols), f32),
                   sds((2, REACH, cols), bf16), sds((2, REACH, cols), bf16)],
        compiler_params=pltpu.CompilerParams(vmem_limit_bytes=VMEM, dimension_semantics=("arbitrary",)),
        cost_estimate=spent(6.5 * pairs),
        name="attention_backward",
    )(img, q, k, v, g, lse)


FT = 512
FINAL_TILE = 1024
ROWS = 1024


def contract(a, b, dims):
    return lax.dot_general(a, b, (dims, ((), ())), preferred_element_type=f32)


def feed_kernel(
    table, normed, cot, middle, bias_final, wide, tall, bias_hidden,
    result, grad_normed, bias_grad, hidden_near, hidden_far, active,
    total, normed_t, final, grad_pre, hidden_grad,
):
    step = pl.program_id(0)
    tiles = pl.num_programs(0)
    rows, width = normed.shape
    half, _, piece, _ = hidden_near.shape
    devices = tall.shape[0] // 32
    depth = FT // devices

    @pl.when(step == 0)
    def _():
        total[...] = middle[...] + bias_final[...]
        grad_normed[...] = jnp.zeros_like(grad_normed)
        normed_t[...] = normed[...].T

    for d in range(devices):
        for i in range(4):
            final[d * depth + i * 32 : d * depth + (i + 1) * 32, :] = tall[d * 32 : (d + 1) * 32, i * width : (i + 1) * width]
    for r in range(0, rows, ROWS):
        cut = slice(r, r + ROWS)
        pre = contract(normed[cut, :], wide[...], ((1,), (0,))) + bias_hidden[...]
        grad = contract(cot[cut, :], final[...], ((1,), (1,)))
        phi = 0.5 + 0.5 * lax.erf(pre * (0.5**0.5))
        slope = phi + pre * jnp.exp(pre * pre * -0.5) * ((0.5 / math.pi) ** 0.5)
        active[cut, :] = (pre * phi).astype(bf16)
        grad_pre[cut, :] = (grad * slope).astype(bf16)
        total[cut, :] += contract(active[cut, :], final[...], ((1,), (0,)))
        grad_normed[cut, :] += contract(grad_pre[cut, :], wide[...], ((1,), (1,)))
    bias_grad[...] = jnp.sum(grad_pre[...].astype(f32), axis=0, keepdims=True)
    hidden_grad[...] = contract(normed_t[...], grad_pre[...], ((1,), (0,)))
    for place in range(2 * half):
        rows_of = hidden_grad[pl.ds(pl.multiple_of(table[place] * piece, piece), piece), :].astype(bf16)
        if place < half:
            hidden_near[place, 0] = rows_of
        else:
            hidden_far[place - half, 0] = rows_of

    @pl.when(step == tiles - 1)
    def _():
        result[...] = total[...].astype(bf16)


def final_kernel(home, active, cot, final_near, final_far, final_grad, sems):
    step = pl.program_id(0)
    tiles = pl.num_programs(0)
    slot = lax.rem(step, 2)
    half, depth, width = final_near.shape
    devices = FINAL_TILE // depth

    def copy_out(slot, d, target):
        return pltpu.make_async_copy(final_grad.at[slot, d], target, sems.at[slot, d])

    def wait_out(slot):
        for d in range(devices):
            copy_out(slot, d, final_near.at[0]).wait()

    @pl.when(step >= 2)
    def _():
        wait_out(slot)

    final_grad[slot] = contract(active[...], cot[...], ((0,), (0,))).astype(bf16).reshape(devices, depth, width)
    for d in range(devices):
        at = home[step * devices + d]

        @pl.when(at < half)
        def _():
            copy_out(slot, d, final_near.at[at]).start()

        @pl.when(at >= half)
        def _():
            copy_out(slot, d, final_far.at[at - half]).start()

    @pl.when(step == tiles - 1)
    def _():
        for d in range(devices):
            copy_out(1 - slot, d, final_near.at[0]).wait()
            copy_out(slot, d, final_near.at[0]).wait()


def final_share(active, cot, home):
    rows, width = cot.shape
    units = active.shape[1]
    depth = units // PIECES
    piece = jax.ShapeDtypeStruct((PIECES // 2, depth, width), bf16)
    return pl.pallas_call(
        final_kernel,
        grid_spec=pltpu.PrefetchScalarGridSpec(
            num_scalar_prefetch=1,
            grid=(units // FINAL_TILE,),
            in_specs=[
                pl.BlockSpec((rows, FINAL_TILE), lambda t, *_: (0, t)),
                pl.BlockSpec((rows, width), lambda t, *_: (0, 0), pipeline_mode=pl.Buffered(1)),
            ],
            out_specs=[pl.BlockSpec(memory_space=pl.ANY)] * 2,
            scratch_shapes=[pltpu.VMEM((2, FINAL_TILE // depth, depth, width), bf16), pltpu.SemaphoreType.DMA((2, FINAL_TILE // depth))],
        ),
        out_shape=[piece, piece],
        compiler_params=pltpu.CompilerParams(vmem_limit_bytes=VMEM, dimension_semantics=("arbitrary",)),
        cost_estimate=spent(14),
        name="final_share",
    )(home, active, cot)


def feed_forward(normed, cot, middle, bias_final, feed, bias_hidden, table):
    rows, width = normed.shape
    units = bias_hidden.shape[1]
    whole = lambda *shape: pl.BlockSpec(shape, lambda t, *_: (0,) * len(shape), pipeline_mode=pl.Buffered(1))
    sds = jax.ShapeDtypeStruct
    depth = units // PIECES
    devices = FT // depth
    line = pl.BlockSpec((1, FT), lambda t, *_: (0, t))
    square = whole(rows, width)
    wide_piece = sds((PIECES // 2, units // width, width // PIECES, width), bf16)
    blocks = width // FT
    edge = pl.BlockSpec((PIECES // 2, 1, width // PIECES, FT), lambda t, *_: (0, t // blocks, 0, t % blocks))
    return pl.pallas_call(
        feed_kernel,
        grid_spec=pltpu.PrefetchScalarGridSpec(
            num_scalar_prefetch=1,
            grid=(units // FT,),
            in_specs=[
                square, square, square, whole(1, width),
                pl.BlockSpec((width, FT), lambda t, *_: (0, t)),
                pl.BlockSpec((devices * 32, 4 * width), lambda t, *_: (t, 1)),
                line,
            ],
            out_specs=[square, square, line, edge, edge, pl.BlockSpec((rows, FT), lambda t, *_: (0, t))],
            scratch_shapes=[
                pltpu.VMEM((rows, width), f32), pltpu.VMEM((width, rows), bf16), pltpu.VMEM((FT, width), bf16),
                pltpu.VMEM((rows, FT), bf16), pltpu.VMEM((width, FT), f32),
            ],
        ),
        out_shape=[
            sds((rows, width), bf16), sds((rows, width), f32), sds((1, units), f32),
            wide_piece, wide_piece, sds((rows, units), bf16),
        ],
        compiler_params=pltpu.CompilerParams(vmem_limit_bytes=VMEM, dimension_semantics=("arbitrary",)),
        cost_estimate=spent(57),
        name="feed_forward",
    )(table, normed, cot, middle, bias_final, feed, feed, bias_hidden)


def project_kernel(
    table_one, table_two, x, one_near, one_far, two_near, two_far,
    q_out, k_out, v_out, normed_out, weight, weight_out, vectors, small,
):
    half, piece, split = one_near.shape
    width = x.shape[1]
    wide = weight.shape[1]

    @pl.when(pl.program_id(0) == 0)
    def _():
        for place in range(2 * half):
            a, b, at = (one_near, two_near, place) if place < half else (one_far, two_far, place - half)
            rows = pl.ds(pl.multiple_of(table_one[place] * piece, piece), piece)
            weight[rows, :split] = a[at]
            rows = pl.ds(pl.multiple_of(table_two[place] * piece, piece), piece)
            weight[rows, split:] = b[at, :, : wide - split]
            weight_out[rows, :] = b[at, :, wide - split : wide - split + width]
            small[rows, :] = b[at, :, wide - split + width : wide - split + width + LANES].astype(f32)
        vectors[...] = small[...].T[: vectors.shape[0]]

    values = x[...].astype(f32)
    center = values - jnp.mean(values, axis=-1, keepdims=True)
    spread_of = jnp.mean(center * center, axis=-1, keepdims=True)
    normed = (center * lax.rsqrt(spread_of + norm_epsilon) * vectors[0:1, :] + vectors[1:2, :]).astype(bf16)
    normed_out[...] = normed
    cols = width // GROUPS
    needs_queries = (pl.program_id(0) == 1) | (pl.program_id(0) == 2)
    for group in range(GROUPS):
        out = slice(group * cols, (group + 1) * cols)
        begin = 3 * group * cols
        keys = jnp.dot(normed, weight[:, begin + cols : begin + 2 * cols], preferred_element_type=f32)
        values = jnp.dot(normed, weight[:, begin + 2 * cols : begin + 3 * cols], preferred_element_type=f32)
        k_out[:, out] = keys.astype(bf16)
        v_out[:, out] = (values + vectors[3:4, out]).astype(bf16)

        @pl.when(needs_queries)
        def _():
            queries = jnp.dot(normed, weight[:, begin : begin + cols], preferred_element_type=f32)
            q_out[:, out] = (queries + vectors[2:3, out]).astype(bf16) * jnp.asarray(HEAD**-0.5, bf16)


def project(window, one, two, tables):
    rows, width = window.shape
    half, piece, split = one[0].shape
    block = rows // 4
    whole = lambda *shape: pl.BlockSpec(shape, lambda t, *_: (0,) * len(shape), pipeline_mode=pl.Buffered(1))
    strip = pl.BlockSpec((block, width), lambda t, *_: (t, 0))
    sds = jax.ShapeDtypeStruct
    return pl.pallas_call(
        project_kernel,
        grid_spec=pltpu.PrefetchScalarGridSpec(
            num_scalar_prefetch=2,
            grid=(4,),
            in_specs=[strip] + [whole(half, piece, split)] * 2 + [whole(*two[0].shape)] * 2,
            out_specs=[strip] * 4 + [whole(width, 3 * width), whole(width, width), whole(16, width)],
            scratch_shapes=[pltpu.VMEM((width, LANES), f32)],
        ),
        out_shape=[sds((rows, width), bf16)] * 4 + [sds((width, 3 * width), bf16), sds((width, width), bf16), sds((16, width), f32)],
        compiler_params=pltpu.CompilerParams(vmem_limit_bytes=VMEM, dimension_semantics=("arbitrary",)),
        cost_estimate=spent(24),
        name="project",
    )(*tables, window, *one, *two)


CW = 256


def share_kernel(
    extra, table, normed, dq, dk, dv, left, right, *refs,
):
    if extra:
        mixed, branch, packed, sums, near, far, normed_t, mixed_t, product, x = refs
    else:
        packed, sums, near, far, product, x = refs
        normed_t = normed
    step = pl.program_id(0)
    rows = dq.shape[0]
    half, piece, _ = near.shape

    if extra:
        @pl.when(step == 0)
        def _():
            normed_t[...] = normed[pl.ds(REACH, rows), :].T

    def halo(own, number):
        x[...] = own[...].astype(bf16)
        edge = rows - REACH
        x[:edge, :] = (own[:edge, :] + left[number, :edge, :].astype(f32)).astype(bf16)
        x[edge:REACH, :] = (own[edge:REACH, :] + left[number, edge:, :].astype(f32) + right[number, : REACH - edge, :].astype(f32)).astype(bf16)
        x[REACH:, :] = (own[REACH:, :] + right[number, REACH - edge :, :].astype(f32)).astype(bf16)

    @pl.when(step < 2)
    def _():
        x[...] = dq[...]

    @pl.when((step >= 2) & (step < 4))
    def _():
        halo(dk, 0)

    @pl.when((step >= 4) & (step < 6))
    def _():
        halo(dv, 1)

    if extra:
        @pl.when(step == 6)
        def _():
            mixed_t[...] = mixed[...].T

        @pl.when(step >= 6)
        def _():
            x[...] = branch[...]

    @pl.when(step < 6)
    def _():
        packed[...] = x[...]

    sums[...] = jnp.sum(x[...].astype(f32), axis=0, keepdims=True)
    if extra:
        @pl.when(step < 6)
        def _():
            product[...] = jnp.dot(normed_t[...], x[...], preferred_element_type=f32)

        @pl.when(step >= 6)
        def _():
            product[...] = jnp.dot(mixed_t[...], x[...], preferred_element_type=f32)
    else:
        product[...] = jnp.dot(normed_t[...], x[...], preferred_element_type=f32)
    for place in range(2 * half):
        rows_of = product[pl.ds(pl.multiple_of(table[place] * piece, piece), piece), :].astype(bf16)
        if place < half:
            near[place] = rows_of
        else:
            far[place - half] = rows_of


def weight_share(normed, dq, dk, dv, left, right, table, extra=()):
    rows, cols = dq.shape
    width = normed.shape[1]
    steps = 6 + (4 if extra else 0)
    whole = lambda *shape: pl.BlockSpec(shape, lambda t, *_: (0,) * len(shape), pipeline_mode=pl.Buffered(1))
    clip = lambda t, low, top: jnp.minimum(jnp.maximum(t - low, 0), top)
    tall = lambda low, top: pl.BlockSpec((rows, CW), lambda t, *_: (0, clip(t, low, top)))
    edge = pl.BlockSpec((2, REACH, CW), lambda t, *_: (0, 0, jnp.where(t < 4, clip(t, 2, 1), clip(t, 4, 1))))
    piece = pl.BlockSpec((PIECES // 2, width // PIECES, CW), lambda t, *_: (0, 0, t))
    sds = jax.ShapeDtypeStruct
    pieces = sds((PIECES // 2, width // PIECES, steps * CW), bf16)
    return pl.pallas_call(
        functools.partial(share_kernel, bool(extra)),
        grid_spec=pltpu.PrefetchScalarGridSpec(
            num_scalar_prefetch=1,
            grid=(steps,),
            in_specs=[whole(*normed.shape), tall(0, 1), tall(2, 1), tall(4, 1), edge, edge]
            + ([whole(rows, width), tall(6, 3)] if extra else []),
            out_specs=[tall(0, 5), pl.BlockSpec((1, CW), lambda t, *_: (0, t))]
            + [piece] * 2 + ([whole(width, rows)] if extra else []),
            scratch_shapes=([pltpu.VMEM((width, rows), bf16)] if extra else [])
            + [pltpu.VMEM((width, CW), f32), pltpu.VMEM((rows, CW), bf16)],
        ),
        out_shape=[sds((rows, 6 * CW), bf16), sds((1, steps * CW), f32), pieces, pieces] + ([sds((width, rows), bf16)] if extra else []),
        compiler_params=pltpu.CompilerParams(vmem_limit_bytes=VMEM, dimension_semantics=("arbitrary",)),
        cost_estimate=spent(10 if extra else 7),
        name="weight_share",
    )(table, normed, dq, dk, dv, left, right, *extra)


def norm_backward(values, gain, grad):
    center = values - jnp.mean(values, axis=-1, keepdims=True)
    scale = lax.rsqrt(jnp.mean(center * center, axis=-1, keepdims=True) + norm_epsilon)
    unit = center * scale
    scaled = grad * gain
    moved = scaled - jnp.mean(scaled, axis=-1, keepdims=True) - unit * jnp.mean(scaled * unit, axis=-1, keepdims=True)
    column = lambda x: jnp.sum(x, axis=0, keepdims=True)
    return scale * moved, column(grad * unit), column(grad)


def branch_kernel(grad, middle, cot, weight_out, vectors, total, branch, mixed, sums):
    @pl.when(pl.program_id(0) == 0)
    def _():
        sums[...] = jnp.zeros_like(sums)

    up = cot[...].astype(f32)
    moved, gain_sum, bias_sum = norm_backward(middle[...], vectors[5:6, :], grad[...])
    total[...] = up + moved
    branch[...] = total[...].astype(bf16)
    mixed[...] = contract(branch[...], weight_out[...], ((1,), (1,))).astype(bf16)
    sums[0:1, :] += gain_sum
    sums[1:2, :] += bias_sum
    sums[2:3, :] += jnp.sum(up, axis=0, keepdims=True)


def input_kernel(one, two, weight, tokens, middle_grad, vectors, out, sums):
    @pl.when(pl.program_id(0) == 0)
    def _():
        sums[...] = jnp.zeros_like(sums)

    cols = one.shape[1]
    grad = contract(one[...], weight[:, :cols], ((1,), (1,))) + contract(two[...], weight[:, cols:], ((1,), (1,)))
    moved, gain_sum, bias_sum = norm_backward(tokens[...].astype(f32), vectors[0:1, :], grad)
    out[...] = (middle_grad[...] + moved).astype(bf16)
    sums[0:1, :] += gain_sum
    sums[1:2, :] += bias_sum


def row_blocks(kernel, name, blocked, whole, outs, us):
    rows, width = blocked[0].shape[0], outs[0][0]
    block = rows // 4
    strip = lambda cols: pl.BlockSpec((block, cols), lambda t: (t, 0))
    fixed = lambda *shape: pl.BlockSpec(shape, lambda t: (0,) * len(shape), pipeline_mode=pl.Buffered(1))
    return pl.pallas_call(
        kernel,
        grid=(4,),
        in_specs=[strip(a.shape[1]) for a in blocked] + [fixed(*a.shape) for a in whole],
        out_specs=[strip(cols) for cols, _ in outs] + [fixed(8, width)],
        out_shape=[jax.ShapeDtypeStruct((rows, cols), kind) for cols, kind in outs] + [jax.ShapeDtypeStruct((8, width), f32)],
        compiler_params=pltpu.CompilerParams(vmem_limit_bytes=VMEM, dimension_semantics=("arbitrary",)),
        cost_estimate=spent(us),
        name=name,
    )(*blocked, *whole)


def branch_gradient(grad, middle, cot, weight_out, vectors):
    width = middle.shape[1]
    outs = [(width, f32), (width, bf16), (width, bf16)]
    return row_blocks(branch_kernel, "branch_gradient", [grad, middle, cot], [weight_out, vectors], outs, 10)


def input_gradient(one, two, tokens, middle_grad, weight, vectors):
    def kernel(one, two, tokens, middle_grad, weight, vectors, out, sums):
        input_kernel(one, two, weight, tokens, middle_grad, vectors, out, sums)

    return row_blocks(kernel, "input_gradient", [one, two, tokens, middle_grad], [weight, vectors], [(tokens.shape[1], bf16)], 12)


def bit_orders(count):
    bits = [1 << i for i in range(count.bit_length() - 1)]
    return (bits[0], bits[2], bits[1], *bits[3:]), (bits[0], bits[1], bits[2], *bits[3:])


def exchange(x, bit, count):
    return lax.ppermute(x, "dev", [(i, i ^ bit) for i in range(count)])


def owners(order, me):
    table = []
    for place in range(PIECES):
        offset = 0
        for i, bit in enumerate(order):
            if (place >> (len(order) - 1 - i)) & 1:
                offset |= bit
        table.append(offset)
    return jnp.array(table, jnp.int32) ^ me


def places(order, me):
    offset = jnp.arange(PIECES, dtype=jnp.int32) ^ me
    return sum(jnp.where(offset & bit != 0, 1 << (len(order) - 1 - i), 0) for i, bit in enumerate(order)).astype(jnp.int32)


def gather_step(held, order, step, count):
    bit = order[len(order) - 1 - step]
    arrived = exchange(held, bit, count)
    return (held, arrived) if bit == order[0] else jnp.concatenate([held, arrived], axis=0)


def total(parts, kind=bf16):
    return functools.reduce(lambda a, b: a + b, [p.astype(f32) for p in parts]).astype(kind)


def straight(parts, bits, count):
    size = parts[0].shape[0] // (len(bits) + 1)
    return [exchange(total([p[(i + 1) * size : (i + 2) * size] for p in parts]), bit, count) for i, bit in enumerate(bits)]


def scatter_whole(near, far, count):
    whole = jnp.concatenate([near, far], axis=0).reshape(-1, near.shape[2])
    return lax.psum_scatter(whole.astype(f32), "dev", scatter_dimension=0, tiled=True)


def layer_norm(values, gain, bias):
    center = values - jnp.mean(values, axis=-1, keepdims=True)
    spread_of = jnp.mean(center * center, axis=-1, keepdims=True)
    return center * lax.rsqrt(spread_of + norm_epsilon) * gain + bias


def exact_gelu(values):
    return jax.nn.gelu(values, approximate=False)


def image_starts(segment_ids, me, rows):
    padded = jnp.pad(segment_ids, (REACH, REACH), constant_values=-2)
    window = lax.dynamic_slice_in_dim(padded, me * rows, rows + 2 * REACH, 0)
    own = window[REACH : REACH + rows]
    far = jnp.int32(1 << 20)
    first = jnp.min(jnp.where(own >= 0, own, far))
    places = jnp.arange(rows + 2 * REACH, dtype=jnp.int32)
    images = (rows - 2) // IMG + 2
    starts = []
    for i in range(images):
        start = jnp.min(jnp.where(window == first + i, places, far))
        starts.append(jnp.where(start == far, -far, start))
    return jnp.stack(starts)


def per_device(
    tokens,
    segment_ids,
    first_gain,
    first_bias,
    qkv_weight,
    query_bias,
    value_bias,
    out_weight,
    out_bias,
    second_gain,
    second_bias,
    hidden_weight,
    hidden_bias,
    final_weight,
    final_bias,
    cotangent,
):
    count = lax.axis_size("dev")
    me = lax.axis_index("dev")
    direct = count == PIECES
    rows, width = tokens.shape
    hidden_width = hidden_weight.shape[1]
    pairs = width // LANES
    part = width // count
    part_rows = width // PIECES
    half = PIECES // 2
    unit = hidden_width // PIECES
    orders = bit_orders(PIECES)
    tables = [owners(order, me) if direct else jnp.arange(PIECES, dtype=jnp.int32) for order in orders]
    home = places(orders[0], me) if direct else jnp.arange(PIECES, dtype=jnp.int32)
    sync = lax.optimization_barrier
    img = image_starts(segment_ids, me, rows)
    to_right = [(i, i + 1) for i in range(count - 1)]
    to_left = [(i + 1, i) for i in range(count - 1)]
    send = lambda left, right: (lax.ppermute(right, "dev", to_right), lax.ppermute(left, "dev", to_left))

    vectors = [first_gain, first_bias, query_bias, value_bias, out_bias, second_gain, second_bias, final_bias]
    small = sync(jnp.concatenate([jnp.stack(vectors), hidden_bias.reshape(-1, part)], axis=0)).T.astype(bf16)
    small = jnp.pad(small, ((0, 0), (0, LANES - small.shape[1])))
    cols = width // GROUPS
    qkv_low = qkv_weight.astype(bf16)
    qkv_low = jnp.concatenate(
        [qkv_low[:, i * width + g * cols : i * width + (g + 1) * cols] for g in range(GROUPS) for i in range(3)], axis=1
    )
    split = 2 * width
    early = jnp.concatenate([qkv_low, out_weight.astype(bf16), small], axis=1)
    hidden_low = hidden_weight.astype(bf16)
    final_low = final_weight.astype(bf16)
    if direct:
        feed = jnp.concatenate([hidden_low] + [final_low[32 * i : 32 * (i + 1)] for i in range(4)], axis=1)
        halo = send(tokens[:REACH], tokens[rows - REACH :])
        line = [exchange(early[None], bit, count) for bit in (orders[0][4], orders[0][3], orders[0][3] | orders[0][4])]
        line, halo, feed = sync((line, halo, feed)) if FEED_AFTER == 1 else (*sync((line, halo)), feed)
        held = [jnp.concatenate([p[..., cut] for p in (early[None], *line)], axis=0) for cut in (slice(0, split), slice(split, None))]
        held = [gather_step(h, o, 2, count) for h, o in zip(held, orders)]
        if FEED_AFTER == 2:
            held, feed = sync((held, feed))
        held = [gather_step(h, o, 3, count) for h, o in zip(held, orders)]
        if FEED_AFTER == 3:
            held, feed = sync((held, feed))
        held = [gather_step(h, o, 4, count) for h, o in zip(held, orders)]
        feed = lax.all_gather(feed, "dev", axis=0, tiled=True)
        one, two = held
    else:
        early = lax.all_gather(early, "dev", axis=0, tiled=True).reshape(PIECES, width // PIECES, -1)
        one, two = [jnp.split(p, 2) for p in (early[..., :split], early[..., split:])]
        hidden_low = lax.all_gather(hidden_low, "dev", axis=0, tiled=True)
        final_low = lax.all_gather(final_low, "dev", axis=0, tiled=True)
        final_low = final_low.reshape(PIECES, 4, 32, width).transpose(0, 2, 1, 3).reshape(width, 4 * width)
        feed = jnp.concatenate([hidden_low, final_low], axis=1)
        halo = send(tokens[:REACH], tokens[rows - REACH :])
    window = jnp.concatenate([halo[0], tokens, halo[1]], axis=0)
    inputs = tokens.astype(f32)
    queries, key_rows, value_rows, normed, weight_qkv, weight_out, vectors = project(window, one, two, tables)
    gain_one, bias_one, bias_query, bias_value, bias_out, gain_two, bias_two, bias_final = [vectors[i] for i in range(8)]
    bias_hidden = vectors[8 : 8 + hidden_width // width].reshape(-1, count, part).transpose(1, 0, 2).reshape(1, hidden_width)
    mixed_low, totals = attention_forward(img, queries, key_rows, value_rows, 0, pairs)
    middle = inputs + (jnp.dot(mixed_low, weight_out, preferred_element_type=f32) + bias_out)
    normed_two = layer_norm(middle, gain_two, bias_two).astype(bf16)
    result, grad_normed_two, hidden_bias_grad, *hidden_grads, active = feed_forward(
        normed_two, cotangent, middle, bias_final[None], feed, bias_hidden, tables[1]
    )
    step = pairs // GROUPS
    blocks = lambda pair: [g.reshape(g.shape[0], -1, part_rows, width) for g in pair]
    hidden_grads = blocks(hidden_grads)
    if direct:
        hidden_got = [hidden_grads[0], exchange(hidden_grads[1], orders[1][0], count)]
    final_grads = blocks(final_share(active, cotangent, home))
    if direct:
        hidden_got, final_grads, grad_normed_two = sync((hidden_got, final_grads, grad_normed_two))
        final_got = [final_grads[0], exchange(final_grads[1], orders[0][0], count)]
        away = total([p[8:] for p in hidden_got])
        away, grad_normed_two = sync((away, grad_normed_two))
        moving = [exchange(away, orders[1][1], count)]
    middle_grad, grad_branch, grad_mixed, sums_mid = branch_gradient(grad_normed_two, middle, cotangent, weight_out, vectors)
    if direct:
        final_got, grad_mixed = sync((final_got, grad_mixed))
        away = total([p[8:] for p in final_got])
        away, grad_mixed = sync((away, grad_mixed))
        moving.append(exchange(away, orders[0][1], count))
        got = [hidden_got, final_got]
        turns = orders[1], orders[0]
    else:
        grads = [hidden_grads, final_grads]
    first = attention_backward(img, queries, key_rows, value_rows, grad_mixed, totals, 0, step)
    if direct:
        grad_mixed, first = sync((grad_mixed, first))
    halo = send(*first[3:])
    second = attention_backward(img, queries, key_rows, value_rows, grad_mixed, totals, step, step)
    if direct:
        moving, first, second, halo, normed, grad_branch = sync((moving, first, second, halo, normed, grad_branch))
        got = [parts + [m] for parts, m in zip(got, moving)]
        away = [total([p[4:8] for p in parts]) for parts in got]
        away, first, second, halo, normed, grad_branch = sync((away, first, second, halo, normed, grad_branch))
        moving = [exchange(a, order[2], count) for a, order in zip(away, turns)]
    next_halo = send(*second[3:])
    packed_one, sums_one, *share_one, turned = weight_share(normed, *first[:3], *halo, tables[0], (mixed_low, grad_branch))
    if direct:
        moving, second, next_halo, turned, share_one = sync((moving, second, next_halo, turned, share_one))
        got = [parts + [m] for parts, m in zip(got, moving)]
        away = jnp.concatenate([total([p[2:4] for p in parts]) for parts in got], axis=0)
        away, second, next_halo, turned, share_one = sync((away, second, next_halo, turned, share_one))
        lined = exchange(away, orders[0][3], count)
        share_one = [share_one[0], exchange(share_one[1], orders[0][0], count)]
    packed_two, sums_two, *share_two = weight_share(turned, *second[:3], *next_halo, tables[0])
    plane = (orders[0][2], orders[0][1], orders[0][1] | orders[0][2])
    line = (orders[0][4], orders[0][3], orders[0][3] | orders[0][4])
    if direct:
        share_one, share_two, packed_one, packed_two = sync((share_one, share_two, packed_one, packed_two))
        plane_one = straight(share_one, plane, count)
        share_two = [share_two[0], exchange(share_two[1], orders[0][0], count)]
    input_grad, sums_first = input_gradient(packed_one, packed_two, tokens, middle_grad, weight_qkv, vectors)
    pick = lambda i: jnp.concatenate([s[:, i * cols : (i + 1) * cols] for s in (sums_one, sums_two)], axis=1)
    sums = jnp.concatenate([sums_first[:2], pick(0), pick(2), sums_one[:, 3 * cols :], sums_mid[:3]], axis=0)
    sums = jnp.concatenate(
        [sums.reshape(8, count, part).transpose(1, 0, 2).reshape(count, 8 * part), hidden_bias_grad.reshape(count, -1)], axis=1
    )
    if direct:
        sums = lax.all_to_all(sums, "dev", 0, 0, tiled=True)
        lined, plane_one, share_one, share_two, input_grad, sums = sync((lined, plane_one, share_one, share_two, input_grad, sums))
        got = [parts + [lined[2 * i : 2 * i + 2]] for i, parts in enumerate(got)]
        ended = exchange(jnp.concatenate([total([p[1:2] for p in parts]) for parts in got], axis=0), orders[0][4], count)
        plane_two = straight(share_two, plane, count)
        share_one = [p[:4] for p in share_one] + plane_one
        lined = exchange(total([p[2:4] for p in share_one]), orders[0][3], count)
        lined, plane_two, share_two, sums, ended, got = sync((lined, plane_two, share_two, sums, ended, got))
        share_one = [p[:2] for p in share_one] + [lined]
        share_two = [p[:4] for p in share_two] + plane_two
        away = [total([p[1:2] for p in share_one])] + [total([p[i : i + 1] for p in share_two]) for i in (1, 2, 3)]
        away, ended, got = sync((away, ended, got))
        last_one, *last_two = [exchange(a, bit, count) for a, bit in zip(away, (orders[0][4], *line))]
        finals = [total([p[0] for p in parts] + [ended[i]], f32) for i, parts in enumerate(got)]
        hidden_shard = finals[0].transpose(1, 0, 2).reshape(part, hidden_width)
        final_shard = finals[1].reshape(-1, width)
        shards_one = total([p[0] for p in share_one] + [last_one[0]], f32)
        shards_two = total([p[0] for p in share_two] + [p[0] for p in last_two], f32)
    else:
        sums = lax.all_to_all(sums, "dev", 0, 0, tiled=True)
        shards_one, shards_two = scatter_whole(*share_one, count), scatter_whole(*share_two, count)
        finals = [jnp.concatenate(g, axis=0) for g in grads]
        finals[0] = finals[0].transpose(0, 2, 1, 3).reshape(width, hidden_width)
        finals[1] = finals[1].reshape(hidden_width, width)
        hidden_shard, final_shard = [lax.psum_scatter(p.astype(f32), "dev", scatter_dimension=0, tiled=True) for p in finals]
    sums = jnp.sum(sums, axis=0)
    own = [sums[i * part : (i + 1) * part] for i in range(8)]
    own_hidden = sums[8 * part :]
    out_shard = shards_one[:, 3 * cols :]
    qkv_shard = jnp.concatenate([h[:, i * cols : (i + 1) * cols] for i in range(3) for h in (shards_one, shards_two)], axis=1)
    return (
        result,
        input_grad,
        own[0],
        own[1],
        qkv_shard,
        own[2],
        own[3],
        out_shard,
        own[4],
        own[5],
        own[6],
        hidden_shard,
        own_hidden,
        final_shard,
        own[7],
    )


def solution(mesh):
    split = P("dev", None)
    line = P("dev")
    return jax.shard_map(
        per_device,
        mesh=mesh,
        in_specs=(split, P(), line, line, split, line, line, split, line, line, line, split, line, split, line, split),
        out_specs=(split, split, line, line, split, line, line, split, line, line, line, split, line, split, line),
        check_vma=False,
    )
```

```python
import functools
import math

import jax
import jax.numpy as jnp
from jax import lax
from jax.experimental import pallas as pl
from jax.experimental.pallas import tpu as pltpu
from jax.sharding import PartitionSpec as P

IMG = 577
REACH = IMG - 1
HEAD = 64
SPAN = 592
LANES = 128
PP = 2
PIECES = 32
PACE = 1.0e5
FEED_AFTER = 2
GROUPS = 2
VMEM = 60 * 1024 * 1024
f32 = jnp.float32
bf16 = jnp.bfloat16

norm_epsilon = 1e-06


def spent(us):
    return pl.CostEstimate(flops=0, bytes_accessed=int(us * PACE), transcendentals=0)


FP = 4
SLOTS = 8
CHUNKS = (384, 256, 128)


def make_items(img_ref, lists, counts, rows, images):
    for kind in range(len(CHUNKS)):
        counts[kind] = 0

    def add(kind, first, begin, end, start):
        size = CHUNKS[kind]
        n = counts[kind]
        base = (kind * SLOTS + n) * 4
        lists[base] = jnp.minimum(first, rows - size)
        lists[base + 1] = jnp.maximum(first, begin)
        lists[base + 2] = jnp.minimum(first + size, end)
        lists[base + 3] = start
        counts[kind] = n + 1

    for i in range(images):
        start = img_ref[i]
        begin = jnp.maximum(start - REACH, 0)
        end = jnp.minimum(start - REACH + IMG, rows)
        low = (begin // 16) * 16
        left = jnp.where(end > begin, end - low, 0)

        @pl.when(left > 512)
        def _():
            add(0, low, begin, end, start)
            add(1, low + 384, begin, end, start)

        @pl.when((left > 384) & (left <= 512))
        def _():
            add(1, low, begin, end, start)
            add(1, low + 256, begin, end, start)

        @pl.when((left > 256) & (left <= 384))
        def _():
            add(0, low, begin, end, start)

        @pl.when((left > 128) & (left <= 256))
        def _():
            add(1, low, begin, end, start)

        @pl.when((left > 0) & (left <= 128))
        def _():
            add(2, low, begin, end, start)


def item_scalars(lists, kind, n):
    base = (kind * SLOTS + n) * 4
    start = lists[base + 3]
    begin = pl.multiple_of((start // 16) * 16, 16)
    return pl.multiple_of(lists[base], 16), lists[base + 1], lists[base + 2], start, begin


def halves(x):
    lane = lax.broadcasted_iota(jnp.int32, x.shape, 1)
    zero = jnp.zeros_like(x)
    return jnp.concatenate([jnp.where(lane < HEAD, x, zero), jnp.where(lane >= HEAD, x, zero)], axis=0)


def mask_keys(scores, start, begin):
    def masked(low, top):
        r = lax.broadcasted_iota(jnp.int32, (top - low, 1), 0) + (low + begin - start)
        return jnp.where((r >= 0) & (r < IMG), scores[low:top], -1e30)

    return jnp.concatenate([masked(0, 16), scores[16 : SPAN - 16], masked(SPAN - 16, SPAN)], axis=0)


def query_valid(size, row, low, top):
    lane = lax.broadcasted_iota(jnp.int32, (1, 2 * size), 1)
    pos = jnp.where(lane < size, lane, lane - size) + row
    return (pos >= low) & (pos < top)


def pad_rows(img_ref, images, rows):
    r = lax.broadcasted_iota(jnp.int32, (rows, LANES), 0) + REACH
    inside = jnp.zeros((rows, LANES), jnp.bool_)
    for i in range(images):
        start = img_ref[i]
        inside = inside | ((r >= start) & (r < start + IMG))
    return ~inside


def fwd_kernel(images, img_ref, q_ref, k_ref, v_ref, o_ref, lse_ref, acc, lists, counts):
    rows = acc.shape[0]
    make_items(img_ref, lists, counts, rows, images)
    acc[...] = jnp.zeros_like(acc)

    def body(kind, size, n, carry):
        row, low, top, start, begin = item_scalars(lists, kind, n)
        qm = query_valid(size, row, low, top)
        done = []
        for u in range(FP):
            cols = slice(u * LANES, (u + 1) * LANES)
            q2 = halves(q_ref[pl.ds(pl.multiple_of(row + REACH, 16), size), cols])
            kw = k_ref[pl.ds(begin, SPAN), cols]
            vw = v_ref[pl.ds(begin, SPAN), cols]
            s = lax.dot_general(kw, q2, (((1,), (1,)), ((), ())), preferred_element_type=f32)
            s = mask_keys(s, start, begin)
            m = jnp.max(s, axis=0, keepdims=True)
            e = jnp.exp(s - m)
            l = jnp.sum(e, axis=0, keepdims=True)
            ot = lax.dot_general(vw, e.astype(bf16), (((0,), (0,)), ((), ())), preferred_element_type=f32)
            ot = ot * jnp.where(qm, 1.0 / l, 0.0)
            done.append((jnp.concatenate([ot[:HEAD, :size], ot[HEAD:, size:]], axis=0).T, m + jnp.log(l)))
        for u in range(FP):
            cols = slice(u * LANES, (u + 1) * LANES)
            acc[pl.ds(row, size), cols] += done[u][0]
            lse_ref[u, pl.ds(kind * SLOTS + n, 1), : 2 * size] = done[u][1]
        return carry

    for kind, size in enumerate(CHUNKS):
        lax.fori_loop(0, counts[kind], functools.partial(body, kind, size), 0)
    pad = pad_rows(img_ref, images, rows)
    for u in range(FP):
        cols = slice(u * LANES, (u + 1) * LANES)
        own = v_ref[pl.ds(REACH, rows), cols].astype(f32)
        o_ref[:, cols] = jnp.where(pad, own, acc[:, cols]).astype(bf16)


def attention_forward(img, q, k, v, first, pairs):
    win = k.shape[0]
    rows = win - 2 * REACH
    images = img.shape[0]
    spec = lambda r: pl.BlockSpec((r, FP * LANES), lambda p, *_: (0, first // FP + p))
    return pl.pallas_call(
        functools.partial(fwd_kernel, images),
        grid_spec=pltpu.PrefetchScalarGridSpec(
            num_scalar_prefetch=1,
            grid=(pairs // FP,),
            in_specs=[spec(win), spec(win), spec(win)],
            out_specs=[
                pl.BlockSpec((rows, FP * LANES), lambda p, *_: (0, p)),
                pl.BlockSpec((FP, 3 * SLOTS, 2 * CHUNKS[0]), lambda p, *_: (p, 0, 0)),
            ],
            scratch_shapes=[
                pltpu.VMEM((rows, FP * LANES), f32), pltpu.SMEM((3 * SLOTS * 4,), jnp.int32), pltpu.SMEM((3,), jnp.int32)
            ],
        ),
        out_shape=[
            jax.ShapeDtypeStruct((rows, pairs * LANES), bf16),
            jax.ShapeDtypeStruct((pairs, 3 * SLOTS, 2 * CHUNKS[0]), f32),
        ],
        compiler_params=pltpu.CompilerParams(vmem_limit_bytes=VMEM, dimension_semantics=("arbitrary",)),
        cost_estimate=spent(5 * pairs),
        name="attention_forward",
    )(img, q, k, v)


def bwd_kernel(images, img_ref, q_ref, k_ref, v_ref, g_ref, lse_ref,
               dq_ref, dk_ref, dv_ref, left_ref, right_ref, dq_acc, dk_acc, dv_acc, lists, counts):
    rows = dq_acc.shape[0]
    make_items(img_ref, lists, counts, rows, images)
    dq_acc[...] = jnp.zeros_like(dq_acc)
    dk_acc[...] = jnp.zeros_like(dk_acc)
    dv_acc[...] = jnp.zeros_like(dv_acc)

    def body(kind, size, n, carry):
        row, low, top, start, begin = item_scalars(lists, kind, n)
        qm = query_valid(size, row, low, top)
        done = []
        for u in range(PP):
            cols = slice(u * LANES, (u + 1) * LANES)
            q2 = halves(q_ref[pl.ds(pl.multiple_of(row + REACH, 16), size), cols])
            g2 = halves(g_ref[pl.ds(row, size), cols])
            kw = k_ref[pl.ds(begin, SPAN), cols]
            vw = v_ref[pl.ds(begin, SPAN), cols]
            lse = jnp.where(qm, lse_ref[u, pl.ds(kind * SLOTS + n, 1), : 2 * size], 1e30)
            s = lax.dot_general(kw, q2, (((1,), (1,)), ((), ())), preferred_element_type=f32)
            dp = lax.dot_general(vw, g2, (((1,), (1,)), ((), ())), preferred_element_type=f32)
            p = jnp.exp(mask_keys(s, start, begin) - lse)
            inner = jnp.sum(p * dp, axis=0, keepdims=True)
            ds = (p * (dp - inner)).astype(bf16)
            dv = jnp.dot(p.astype(bf16), g2, preferred_element_type=f32)
            dk = jnp.dot(ds, q2, preferred_element_type=f32)
            dqt = lax.dot_general(kw, ds, (((0,), (0,)), ((), ())), preferred_element_type=f32)
            done.append((dv, dk, jnp.concatenate([dqt[:HEAD, :size], dqt[HEAD:, size:]], axis=0).T))
        for u in range(PP):
            cols = slice(u * LANES, (u + 1) * LANES)
            dv, dk, dq = done[u]
            dv_acc[pl.ds(begin, SPAN), cols] += dv
            dk_acc[pl.ds(begin, SPAN), cols] += dk
            dq_acc[pl.ds(row, size), cols] += dq
        return carry

    for kind, size in enumerate(CHUNKS):
        lax.fori_loop(0, counts[kind], functools.partial(body, kind, size), 0)
    pad = pad_rows(img_ref, images, rows)
    dq_ref[...] = (dq_acc[...] * 0.125).astype(bf16)
    dk_ref[...] = dk_acc[pl.ds(REACH, rows), :]
    for u in range(PP):
        cols = slice(u * LANES, (u + 1) * LANES)
        dv_ref[:, cols] = dv_acc[pl.ds(REACH, rows), cols] + jnp.where(pad, g_ref[:, cols].astype(f32), 0.0)
    left_ref[0] = dk_acc[pl.ds(0, REACH), :].astype(bf16)
    left_ref[1] = dv_acc[pl.ds(0, REACH), :].astype(bf16)
    right_ref[0] = dk_acc[pl.ds(REACH + rows, REACH), :].astype(bf16)
    right_ref[1] = dv_acc[pl.ds(REACH + rows, REACH), :].astype(bf16)


def attention_backward(img, q, k, v, g, lse, first, pairs):
    win = k.shape[0]
    rows = win - 2 * REACH
    images = img.shape[0]
    C = PP * LANES
    spec = lambda r: pl.BlockSpec((r, C), lambda p, *_: (0, first // PP + p))
    out = lambda r: pl.BlockSpec((r, C), lambda p, *_: (0, p))
    edge = pl.BlockSpec((2, REACH, C), lambda p, *_: (0, 0, p))
    sds = jax.ShapeDtypeStruct
    cols = pairs * LANES
    return pl.pallas_call(
        functools.partial(bwd_kernel, images),
        grid_spec=pltpu.PrefetchScalarGridSpec(
            num_scalar_prefetch=1,
            grid=(pairs // PP,),
            in_specs=[spec(win), spec(win), spec(win), spec(rows),
                      pl.BlockSpec((PP, 3 * SLOTS, 2 * CHUNKS[0]), lambda p, *_: (first // PP + p, 0, 0))],
            out_specs=[out(rows), out(rows), out(rows), edge, edge],
            scratch_shapes=[pltpu.VMEM((rows, C), f32), pltpu.VMEM((win, C), f32), pltpu.VMEM((win, C), f32),
                            pltpu.SMEM((3 * SLOTS * 4,), jnp.int32), pltpu.SMEM((3,), jnp.int32)],
        ),
        out_shape=[sds((rows, cols), bf16), sds((rows, cols), f32), sds((rows, cols), f32),
                   sds((2, REACH, cols), bf16), sds((2, REACH, cols), bf16)],
        compiler_params=pltpu.CompilerParams(vmem_limit_bytes=VMEM, dimension_semantics=("arbitrary",)),
        cost_estimate=spent(6.5 * pairs),
        name="attention_backward",
    )(img, q, k, v, g, lse)


FT = 512
FINAL_TILE = 1024
ROWS = 1024


def contract(a, b, dims):
    return lax.dot_general(a, b, (dims, ((), ())), preferred_element_type=f32)


def feed_kernel(
    table, normed, cot, middle, bias_final, wide, tall, bias_hidden,
    result, grad_normed, bias_grad, hidden_near, hidden_far, active,
    total, normed_t, final, grad_pre, hidden_grad,
):
    step = pl.program_id(0)
    tiles = pl.num_programs(0)
    rows, width = normed.shape
    half, _, piece, _ = hidden_near.shape
    devices = tall.shape[0] // 32
    depth = FT // devices

    @pl.when(step == 0)
    def _():
        total[...] = middle[...] + bias_final[...]
        grad_normed[...] = jnp.zeros_like(grad_normed)
        normed_t[...] = normed[...].T

    for d in range(devices):
        for i in range(4):
            final[d * depth + i * 32 : d * depth + (i + 1) * 32, :] = tall[d * 32 : (d + 1) * 32, i * width : (i + 1) * width]
    for r in range(0, rows, ROWS):
        cut = slice(r, r + ROWS)
        pre = contract(normed[cut, :], wide[...], ((1,), (0,))) + bias_hidden[...]
        grad = contract(cot[cut, :], final[...], ((1,), (1,)))
        phi = 0.5 + 0.5 * lax.erf(pre * (0.5**0.5))
        slope = phi + pre * jnp.exp(pre * pre * -0.5) * ((0.5 / math.pi) ** 0.5)
        active[cut, :] = (pre * phi).astype(bf16)
        grad_pre[cut, :] = (grad * slope).astype(bf16)
        total[cut, :] += contract(active[cut, :], final[...], ((1,), (0,)))
        grad_normed[cut, :] += contract(grad_pre[cut, :], wide[...], ((1,), (1,)))
    bias_grad[...] = jnp.sum(grad_pre[...].astype(f32), axis=0, keepdims=True)
    hidden_grad[...] = contract(normed_t[...], grad_pre[...], ((1,), (0,)))
    for place in range(2 * half):
        rows_of = hidden_grad[pl.ds(pl.multiple_of(table[place] * piece, piece), piece), :].astype(bf16)
        if place < half:
            hidden_near[place, 0] = rows_of
        else:
            hidden_far[place - half, 0] = rows_of

    @pl.when(step == tiles - 1)
    def _():
        result[...] = total[...].astype(bf16)


def final_kernel(home, active, cot, final_near, final_far, final_grad, sems):
    step = pl.program_id(0)
    tiles = pl.num_programs(0)
    slot = lax.rem(step, 2)
    half, depth, width = final_near.shape
    devices = FINAL_TILE // depth

    def copy_out(slot, d, target):
        return pltpu.make_async_copy(final_grad.at[slot, d], target, sems.at[slot, d])

    def wait_out(slot):
        for d in range(devices):
            copy_out(slot, d, final_near.at[0]).wait()

    @pl.when(step >= 2)
    def _():
        wait_out(slot)

    final_grad[slot] = contract(active[...], cot[...], ((0,), (0,))).astype(bf16).reshape(devices, depth, width)
    for d in range(devices):
        at = home[step * devices + d]

        @pl.when(at < half)
        def _():
            copy_out(slot, d, final_near.at[at]).start()

        @pl.when(at >= half)
        def _():
            copy_out(slot, d, final_far.at[at - half]).start()

    @pl.when(step == tiles - 1)
    def _():
        for d in range(devices):
            copy_out(1 - slot, d, final_near.at[0]).wait()
            copy_out(slot, d, final_near.at[0]).wait()


def final_share(active, cot, home):
    rows, width = cot.shape
    units = active.shape[1]
    depth = units // PIECES
    piece = jax.ShapeDtypeStruct((PIECES // 2, depth, width), bf16)
    return pl.pallas_call(
        final_kernel,
        grid_spec=pltpu.PrefetchScalarGridSpec(
            num_scalar_prefetch=1,
            grid=(units // FINAL_TILE,),
            in_specs=[
                pl.BlockSpec((rows, FINAL_TILE), lambda t, *_: (0, t)),
                pl.BlockSpec((rows, width), lambda t, *_: (0, 0), pipeline_mode=pl.Buffered(1)),
            ],
            out_specs=[pl.BlockSpec(memory_space=pl.ANY)] * 2,
            scratch_shapes=[pltpu.VMEM((2, FINAL_TILE // depth, depth, width), bf16), pltpu.SemaphoreType.DMA((2, FINAL_TILE // depth))],
        ),
        out_shape=[piece, piece],
        compiler_params=pltpu.CompilerParams(vmem_limit_bytes=VMEM, dimension_semantics=("arbitrary",)),
        cost_estimate=spent(14),
        name="final_share",
    )(home, active, cot)


def feed_forward(normed, cot, middle, bias_final, feed, bias_hidden, table):
    rows, width = normed.shape
    units = bias_hidden.shape[1]
    whole = lambda *shape: pl.BlockSpec(shape, lambda t, *_: (0,) * len(shape), pipeline_mode=pl.Buffered(1))
    sds = jax.ShapeDtypeStruct
    depth = units // PIECES
    devices = FT // depth
    line = pl.BlockSpec((1, FT), lambda t, *_: (0, t))
    square = whole(rows, width)
    wide_piece = sds((PIECES // 2, units // width, width // PIECES, width), bf16)
    blocks = width // FT
    edge = pl.BlockSpec((PIECES // 2, 1, width // PIECES, FT), lambda t, *_: (0, t // blocks, 0, t % blocks))
    return pl.pallas_call(
        feed_kernel,
        grid_spec=pltpu.PrefetchScalarGridSpec(
            num_scalar_prefetch=1,
            grid=(units // FT,),
            in_specs=[
                square, square, square, whole(1, width),
                pl.BlockSpec((width, FT), lambda t, *_: (0, t)),
                pl.BlockSpec((devices * 32, 4 * width), lambda t, *_: (t, 1)),
                line,
            ],
            out_specs=[square, square, line, edge, edge, pl.BlockSpec((rows, FT), lambda t, *_: (0, t))],
            scratch_shapes=[
                pltpu.VMEM((rows, width), f32), pltpu.VMEM((width, rows), bf16), pltpu.VMEM((FT, width), bf16),
                pltpu.VMEM((rows, FT), bf16), pltpu.VMEM((width, FT), f32),
            ],
        ),
        out_shape=[
            sds((rows, width), bf16), sds((rows, width), f32), sds((1, units), f32),
            wide_piece, wide_piece, sds((rows, units), bf16),
        ],
        compiler_params=pltpu.CompilerParams(vmem_limit_bytes=VMEM, dimension_semantics=("arbitrary",)),
        cost_estimate=spent(57),
        name="feed_forward",
    )(table, normed, cot, middle, bias_final, feed, feed, bias_hidden)


def project_kernel(
    table_one, table_two, x, one_near, one_far, two_near, two_far,
    q_out, k_out, v_out, normed_out, weight, weight_out, vectors, small,
):
    half, piece, split = one_near.shape
    width = x.shape[1]
    wide = weight.shape[1]

    @pl.when(pl.program_id(0) == 0)
    def _():
        for place in range(2 * half):
            a, b, at = (one_near, two_near, place) if place < half else (one_far, two_far, place - half)
            rows = pl.ds(pl.multiple_of(table_one[place] * piece, piece), piece)
            weight[rows, :split] = a[at]
            rows = pl.ds(pl.multiple_of(table_two[place] * piece, piece), piece)
            weight[rows, split:] = b[at, :, : wide - split]
            weight_out[rows, :] = b[at, :, wide - split : wide - split + width]
            small[rows, :] = b[at, :, wide - split + width : wide - split + width + LANES].astype(f32)
        vectors[...] = small[...].T[: vectors.shape[0]]

    values = x[...].astype(f32)
    center = values - jnp.mean(values, axis=-1, keepdims=True)
    spread_of = jnp.mean(center * center, axis=-1, keepdims=True)
    normed = (center * lax.rsqrt(spread_of + norm_epsilon) * vectors[0:1, :] + vectors[1:2, :]).astype(bf16)
    normed_out[...] = normed
    cols = width // GROUPS
    needs_queries = (pl.program_id(0) == 1) | (pl.program_id(0) == 2)
    for group in range(GROUPS):
        out = slice(group * cols, (group + 1) * cols)
        begin = 3 * group * cols
        keys = jnp.dot(normed, weight[:, begin + cols : begin + 2 * cols], preferred_element_type=f32)
        values = jnp.dot(normed, weight[:, begin + 2 * cols : begin + 3 * cols], preferred_element_type=f32)
        k_out[:, out] = keys.astype(bf16)
        v_out[:, out] = (values + vectors[3:4, out]).astype(bf16)

        @pl.when(needs_queries)
        def _():
            queries = jnp.dot(normed, weight[:, begin : begin + cols], preferred_element_type=f32)
            q_out[:, out] = (queries + vectors[2:3, out]).astype(bf16) * jnp.asarray(HEAD**-0.5, bf16)


def project(window, one, two, tables):
    rows, width = window.shape
    half, piece, split = one[0].shape
    block = rows // 4
    whole = lambda *shape: pl.BlockSpec(shape, lambda t, *_: (0,) * len(shape), pipeline_mode=pl.Buffered(1))
    strip = pl.BlockSpec((block, width), lambda t, *_: (t, 0))
    sds = jax.ShapeDtypeStruct
    return pl.pallas_call(
        project_kernel,
        grid_spec=pltpu.PrefetchScalarGridSpec(
            num_scalar_prefetch=2,
            grid=(4,),
            in_specs=[strip] + [whole(half, piece, split)] * 2 + [whole(*two[0].shape)] * 2,
            out_specs=[strip] * 4 + [whole(width, 3 * width), whole(width, width), whole(16, width)],
            scratch_shapes=[pltpu.VMEM((width, LANES), f32)],
        ),
        out_shape=[sds((rows, width), bf16)] * 4 + [sds((width, 3 * width), bf16), sds((width, width), bf16), sds((16, width), f32)],
        compiler_params=pltpu.CompilerParams(vmem_limit_bytes=VMEM, dimension_semantics=("arbitrary",)),
        cost_estimate=spent(24),
        name="project",
    )(*tables, window, *one, *two)


CW = 256


def share_kernel(
    extra, table, normed, dq, dk, dv, left, right, *refs,
):
    if extra:
        mixed, branch, packed, sums, near, far, normed_t, mixed_t, product, x = refs
    else:
        packed, sums, near, far, product, x = refs
        normed_t = normed
    step = pl.program_id(0)
    rows = dq.shape[0]
    half, piece, _ = near.shape

    if extra:
        @pl.when(step == 0)
        def _():
            normed_t[...] = normed[pl.ds(REACH, rows), :].T

    def halo(own, number):
        x[...] = own[...].astype(bf16)
        edge = rows - REACH
        x[:edge, :] = (own[:edge, :] + left[number, :edge, :].astype(f32)).astype(bf16)
        x[edge:REACH, :] = (own[edge:REACH, :] + left[number, edge:, :].astype(f32) + right[number, : REACH - edge, :].astype(f32)).astype(bf16)
        x[REACH:, :] = (own[REACH:, :] + right[number, REACH - edge :, :].astype(f32)).astype(bf16)

    @pl.when(step < 2)
    def _():
        x[...] = dq[...]

    @pl.when((step >= 2) & (step < 4))
    def _():
        halo(dk, 0)

    @pl.when((step >= 4) & (step < 6))
    def _():
        halo(dv, 1)

    if extra:
        @pl.when(step == 6)
        def _():
            mixed_t[...] = mixed[...].T

        @pl.when(step >= 6)
        def _():
            x[...] = branch[...]

    @pl.when(step < 6)
    def _():
        packed[...] = x[...]

    sums[...] = jnp.sum(x[...].astype(f32), axis=0, keepdims=True)
    if extra:
        @pl.when(step < 6)
        def _():
            product[...] = jnp.dot(normed_t[...], x[...], preferred_element_type=f32)

        @pl.when(step >= 6)
        def _():
            product[...] = jnp.dot(mixed_t[...], x[...], preferred_element_type=f32)
    else:
        product[...] = jnp.dot(normed_t[...], x[...], preferred_element_type=f32)
    for place in range(2 * half):
        rows_of = product[pl.ds(pl.multiple_of(table[place] * piece, piece), piece), :].astype(bf16)
        if place < half:
            near[place] = rows_of
        else:
            far[place - half] = rows_of


def weight_share(normed, dq, dk, dv, left, right, table, extra=()):
    rows, cols = dq.shape
    width = normed.shape[1]
    steps = 6 + (4 if extra else 0)
    whole = lambda *shape: pl.BlockSpec(shape, lambda t, *_: (0,) * len(shape), pipeline_mode=pl.Buffered(1))
    clip = lambda t, low, top: jnp.minimum(jnp.maximum(t - low, 0), top)
    tall = lambda low, top: pl.BlockSpec((rows, CW), lambda t, *_: (0, clip(t, low, top)))
    edge = pl.BlockSpec((2, REACH, CW), lambda t, *_: (0, 0, jnp.where(t < 4, clip(t, 2, 1), clip(t, 4, 1))))
    piece = pl.BlockSpec((PIECES // 2, width // PIECES, CW), lambda t, *_: (0, 0, t))
    sds = jax.ShapeDtypeStruct
    pieces = sds((PIECES // 2, width // PIECES, steps * CW), bf16)
    return pl.pallas_call(
        functools.partial(share_kernel, bool(extra)),
        grid_spec=pltpu.PrefetchScalarGridSpec(
            num_scalar_prefetch=1,
            grid=(steps,),
            in_specs=[whole(*normed.shape), tall(0, 1), tall(2, 1), tall(4, 1), edge, edge]
            + ([whole(rows, width), tall(6, 3)] if extra else []),
            out_specs=[tall(0, 5), pl.BlockSpec((1, CW), lambda t, *_: (0, t))]
            + [piece] * 2 + ([whole(width, rows)] if extra else []),
            scratch_shapes=([pltpu.VMEM((width, rows), bf16)] if extra else [])
            + [pltpu.VMEM((width, CW), f32), pltpu.VMEM((rows, CW), bf16)],
        ),
        out_shape=[sds((rows, 6 * CW), bf16), sds((1, steps * CW), f32), pieces, pieces] + ([sds((width, rows), bf16)] if extra else []),
        compiler_params=pltpu.CompilerParams(vmem_limit_bytes=VMEM, dimension_semantics=("arbitrary",)),
        cost_estimate=spent(10 if extra else 7),
        name="weight_share",
    )(table, normed, dq, dk, dv, left, right, *extra)


def norm_backward(values, gain, grad):
    center = values - jnp.mean(values, axis=-1, keepdims=True)
    scale = lax.rsqrt(jnp.mean(center * center, axis=-1, keepdims=True) + norm_epsilon)
    unit = center * scale
    scaled = grad * gain
    moved = scaled - jnp.mean(scaled, axis=-1, keepdims=True) - unit * jnp.mean(scaled * unit, axis=-1, keepdims=True)
    column = lambda x: jnp.sum(x, axis=0, keepdims=True)
    return scale * moved, column(grad * unit), column(grad)


def branch_kernel(grad, middle, cot, weight_out, vectors, total, branch, mixed, sums):
    @pl.when(pl.program_id(0) == 0)
    def _():
        sums[...] = jnp.zeros_like(sums)

    up = cot[...].astype(f32)
    moved, gain_sum, bias_sum = norm_backward(middle[...], vectors[5:6, :], grad[...])
    total[...] = up + moved
    branch[...] = total[...].astype(bf16)
    mixed[...] = contract(branch[...], weight_out[...], ((1,), (1,))).astype(bf16)
    sums[0:1, :] += gain_sum
    sums[1:2, :] += bias_sum
    sums[2:3, :] += jnp.sum(up, axis=0, keepdims=True)


def input_kernel(one, two, weight, tokens, middle_grad, vectors, out, sums):
    @pl.when(pl.program_id(0) == 0)
    def _():
        sums[...] = jnp.zeros_like(sums)

    cols = one.shape[1]
    grad = contract(one[...], weight[:, :cols], ((1,), (1,))) + contract(two[...], weight[:, cols:], ((1,), (1,)))
    moved, gain_sum, bias_sum = norm_backward(tokens[...].astype(f32), vectors[0:1, :], grad)
    out[...] = (middle_grad[...] + moved).astype(bf16)
    sums[0:1, :] += gain_sum
    sums[1:2, :] += bias_sum


def row_blocks(kernel, name, blocked, whole, outs, us, parts):
    rows, width = blocked[0].shape[0], outs[0][0]
    block = rows // parts
    strip = lambda cols: pl.BlockSpec((block, cols), lambda t: (t, 0))
    fixed = lambda *shape: pl.BlockSpec(shape, lambda t: (0,) * len(shape), pipeline_mode=pl.Buffered(1))
    return pl.pallas_call(
        kernel,
        grid=(parts,),
        in_specs=[strip(a.shape[1]) for a in blocked] + [fixed(*a.shape) for a in whole],
        out_specs=[strip(cols) for cols, _ in outs] + [fixed(8, width)],
        out_shape=[jax.ShapeDtypeStruct((rows, cols), kind) for cols, kind in outs] + [jax.ShapeDtypeStruct((8, width), f32)],
        compiler_params=pltpu.CompilerParams(vmem_limit_bytes=VMEM, dimension_semantics=("arbitrary",)),
        cost_estimate=spent(us),
        name=name,
    )(*blocked, *whole)


def branch_gradient(grad, middle, cot, weight_out, vectors):
    width = middle.shape[1]
    outs = [(width, f32), (width, bf16), (width, bf16)]
    return row_blocks(branch_kernel, "branch_gradient", [grad, middle, cot], [weight_out, vectors], outs, 10, 4)


def input_gradient(one, two, tokens, middle_grad, weight, vectors):
    def kernel(one, two, tokens, middle_grad, weight, vectors, out, sums):
        input_kernel(one, two, weight, tokens, middle_grad, vectors, out, sums)

    return row_blocks(kernel, "input_gradient", [one, two, tokens, middle_grad], [weight, vectors], [(tokens.shape[1], bf16)], 12, 2)


def bit_orders(count):
    bits = [1 << i for i in range(count.bit_length() - 1)]
    return (bits[0], bits[2], bits[1], *bits[3:]), (bits[0], bits[1], bits[2], *bits[3:])


def exchange(x, bit, count):
    return lax.ppermute(x, "dev", [(i, i ^ bit) for i in range(count)])


def owners(order, me):
    table = []
    for place in range(PIECES):
        offset = 0
        for i, bit in enumerate(order):
            if (place >> (len(order) - 1 - i)) & 1:
                offset |= bit
        table.append(offset)
    return jnp.array(table, jnp.int32) ^ me


def places(order, me):
    offset = jnp.arange(PIECES, dtype=jnp.int32) ^ me
    return sum(jnp.where(offset & bit != 0, 1 << (len(order) - 1 - i), 0) for i, bit in enumerate(order)).astype(jnp.int32)


def gather_step(held, order, step, count):
    bit = order[len(order) - 1 - step]
    arrived = exchange(held, bit, count)
    return (held, arrived) if bit == order[0] else jnp.concatenate([held, arrived], axis=0)


def total(parts, kind=bf16):
    return functools.reduce(lambda a, b: a + b, [p.astype(f32) for p in parts]).astype(kind)


def straight(parts, bits, count):
    size = parts[0].shape[0] // (len(bits) + 1)
    return [exchange(total([p[(i + 1) * size : (i + 2) * size] for p in parts]), bit, count) for i, bit in enumerate(bits)]


def scatter_whole(near, far, count):
    whole = jnp.concatenate([near, far], axis=0).reshape(-1, near.shape[2])
    return lax.psum_scatter(whole.astype(f32), "dev", scatter_dimension=0, tiled=True)


def layer_norm(values, gain, bias):
    center = values - jnp.mean(values, axis=-1, keepdims=True)
    spread_of = jnp.mean(center * center, axis=-1, keepdims=True)
    return center * lax.rsqrt(spread_of + norm_epsilon) * gain + bias


def exact_gelu(values):
    return jax.nn.gelu(values, approximate=False)


def image_starts(segment_ids, me, rows):
    padded = jnp.pad(segment_ids, (REACH, REACH), constant_values=-2)
    window = lax.dynamic_slice_in_dim(padded, me * rows, rows + 2 * REACH, 0)
    own = window[REACH : REACH + rows]
    far = jnp.int32(1 << 20)
    first = jnp.min(jnp.where(own >= 0, own, far))
    places = jnp.arange(rows + 2 * REACH, dtype=jnp.int32)
    images = (rows - 2) // IMG + 2
    starts = []
    for i in range(images):
        start = jnp.min(jnp.where(window == first + i, places, far))
        starts.append(jnp.where(start == far, -far, start))
    return jnp.stack(starts)


def per_device(
    tokens,
    segment_ids,
    first_gain,
    first_bias,
    qkv_weight,
    query_bias,
    value_bias,
    out_weight,
    out_bias,
    second_gain,
    second_bias,
    hidden_weight,
    hidden_bias,
    final_weight,
    final_bias,
    cotangent,
):
    count = lax.axis_size("dev")
    me = lax.axis_index("dev")
    direct = count == PIECES
    rows, width = tokens.shape
    hidden_width = hidden_weight.shape[1]
    pairs = width // LANES
    part = width // count
    part_rows = width // PIECES
    half = PIECES // 2
    unit = hidden_width // PIECES
    orders = bit_orders(PIECES)
    tables = [owners(order, me) if direct else jnp.arange(PIECES, dtype=jnp.int32) for order in orders]
    home = places(orders[0], me) if direct else jnp.arange(PIECES, dtype=jnp.int32)
    sync = lax.optimization_barrier
    img = image_starts(segment_ids, me, rows)
    to_right = [(i, i + 1) for i in range(count - 1)]
    to_left = [(i + 1, i) for i in range(count - 1)]
    send = lambda left, right: (lax.ppermute(right, "dev", to_right), lax.ppermute(left, "dev", to_left))

    vectors = [first_gain, first_bias, query_bias, value_bias, out_bias, second_gain, second_bias, final_bias]
    small = sync(jnp.concatenate([jnp.stack(vectors), hidden_bias.reshape(-1, part)], axis=0)).T.astype(bf16)
    small = jnp.pad(small, ((0, 0), (0, LANES - small.shape[1])))
    cols = width // GROUPS
    qkv_low = qkv_weight.astype(bf16)
    qkv_low = jnp.concatenate(
        [qkv_low[:, i * width + g * cols : i * width + (g + 1) * cols] for g in range(GROUPS) for i in range(3)], axis=1
    )
    split = 2 * width
    early = jnp.concatenate([qkv_low, out_weight.astype(bf16), small], axis=1)
    hidden_low = hidden_weight.astype(bf16)
    final_low = final_weight.astype(bf16)
    if direct:
        feed = jnp.concatenate([hidden_low] + [final_low[32 * i : 32 * (i + 1)] for i in range(4)], axis=1)
        halo = send(tokens[:REACH], tokens[rows - REACH :])
        line = [exchange(early[None], bit, count) for bit in (orders[0][4], orders[0][3], orders[0][3] | orders[0][4])]
        line, halo, feed = sync((line, halo, feed)) if FEED_AFTER == 1 else (*sync((line, halo)), feed)
        held = [jnp.concatenate([p[..., cut] for p in (early[None], *line)], axis=0) for cut in (slice(0, split), slice(split, None))]
        held = [gather_step(h, o, 2, count) for h, o in zip(held, orders)]
        if FEED_AFTER == 2:
            held, feed = sync((held, feed))
        held = [gather_step(h, o, 3, count) for h, o in zip(held, orders)]
        if FEED_AFTER == 3:
            held, feed = sync((held, feed))
        held = [gather_step(h, o, 4, count) for h, o in zip(held, orders)]
        feed = lax.all_gather(feed, "dev", axis=0, tiled=True)
        one, two = held
    else:
        early = lax.all_gather(early, "dev", axis=0, tiled=True).reshape(PIECES, width // PIECES, -1)
        one, two = [jnp.split(p, 2) for p in (early[..., :split], early[..., split:])]
        hidden_low = lax.all_gather(hidden_low, "dev", axis=0, tiled=True)
        final_low = lax.all_gather(final_low, "dev", axis=0, tiled=True)
        final_low = final_low.reshape(PIECES, 4, 32, width).transpose(0, 2, 1, 3).reshape(width, 4 * width)
        feed = jnp.concatenate([hidden_low, final_low], axis=1)
        halo = send(tokens[:REACH], tokens[rows - REACH :])
    window = jnp.concatenate([halo[0], tokens, halo[1]], axis=0)
    inputs = tokens.astype(f32)
    queries, key_rows, value_rows, normed, weight_qkv, weight_out, vectors = project(window, one, two, tables)
    gain_one, bias_one, bias_query, bias_value, bias_out, gain_two, bias_two, bias_final = [vectors[i] for i in range(8)]
    bias_hidden = vectors[8 : 8 + hidden_width // width].reshape(-1, count, part).transpose(1, 0, 2).reshape(1, hidden_width)
    mixed_low, totals = attention_forward(img, queries, key_rows, value_rows, 0, pairs)
    middle = inputs + (jnp.dot(mixed_low, weight_out, preferred_element_type=f32) + bias_out)
    normed_two = layer_norm(middle, gain_two, bias_two).astype(bf16)
    result, grad_normed_two, hidden_bias_grad, *hidden_grads, active = feed_forward(
        normed_two, cotangent, middle, bias_final[None], feed, bias_hidden, tables[1]
    )
    step = pairs // GROUPS
    blocks = lambda pair: [g.reshape(g.shape[0], -1, part_rows, width) for g in pair]
    hidden_grads = blocks(hidden_grads)
    if direct:
        hidden_got = [hidden_grads[0], exchange(hidden_grads[1], orders[1][0], count)]
    final_grads = blocks(final_share(active, cotangent, home))
    if direct:
        hidden_got, final_grads, grad_normed_two = sync((hidden_got, final_grads, grad_normed_two))
        final_got = [final_grads[0], exchange(final_grads[1], orders[0][0], count)]
        away = total([p[8:] for p in hidden_got])
        away, grad_normed_two = sync((away, grad_normed_two))
        moving = [exchange(away, orders[1][1], count)]
    middle_grad, grad_branch, grad_mixed, sums_mid = branch_gradient(grad_normed_two, middle, cotangent, weight_out, vectors)
    if direct:
        final_got, grad_mixed = sync((final_got, grad_mixed))
        away = total([p[8:] for p in final_got])
        away, grad_mixed = sync((away, grad_mixed))
        moving.append(exchange(away, orders[0][1], count))
        got = [hidden_got, final_got]
        turns = orders[1], orders[0]
    else:
        grads = [hidden_grads, final_grads]
    first = attention_backward(img, queries, key_rows, value_rows, grad_mixed, totals, 0, step)
    if direct:
        grad_mixed, first = sync((grad_mixed, first))
    halo = send(*first[3:])
    second = attention_backward(img, queries, key_rows, value_rows, grad_mixed, totals, step, step)
    if direct:
        moving, first, second, halo, normed, grad_branch = sync((moving, first, second, halo, normed, grad_branch))
        got = [parts + [m] for parts, m in zip(got, moving)]
        away = [total([p[4:8] for p in parts]) for parts in got]
        away, first, second, halo, normed, grad_branch = sync((away, first, second, halo, normed, grad_branch))
        moving = [exchange(a, order[2], count) for a, order in zip(away, turns)]
    next_halo = send(*second[3:])
    packed_one, sums_one, *share_one, turned = weight_share(normed, *first[:3], *halo, tables[0], (mixed_low, grad_branch))
    if direct:
        moving, second, next_halo, turned, share_one = sync((moving, second, next_halo, turned, share_one))
        got = [parts + [m] for parts, m in zip(got, moving)]
        away = jnp.concatenate([total([p[2:4] for p in parts]) for parts in got], axis=0)
        away, second, next_halo, turned, share_one = sync((away, second, next_halo, turned, share_one))
        lined = exchange(away, orders[0][3], count)
        share_one = [share_one[0], exchange(share_one[1], orders[0][0], count)]
    packed_two, sums_two, *share_two = weight_share(turned, *second[:3], *next_halo, tables[0])
    plane = (orders[0][2], orders[0][1], orders[0][1] | orders[0][2])
    line = (orders[0][4], orders[0][3], orders[0][3] | orders[0][4])
    if direct:
        share_one, share_two, packed_one, packed_two = sync((share_one, share_two, packed_one, packed_two))
        plane_one = straight(share_one, plane, count)
        share_two = [share_two[0], exchange(share_two[1], orders[0][0], count)]
    input_grad, sums_first = input_gradient(packed_one, packed_two, tokens, middle_grad, weight_qkv, vectors)
    pick = lambda i: jnp.concatenate([s[:, i * cols : (i + 1) * cols] for s in (sums_one, sums_two)], axis=1)
    sums = jnp.concatenate([sums_first[:2], pick(0), pick(2), sums_one[:, 3 * cols :], sums_mid[:3]], axis=0)
    sums = jnp.concatenate(
        [sums.reshape(8, count, part).transpose(1, 0, 2).reshape(count, 8 * part), hidden_bias_grad.reshape(count, -1)], axis=1
    )
    if direct:
        sums = lax.all_to_all(sums, "dev", 0, 0, tiled=True)
        lined, plane_one, share_one, share_two, input_grad, sums = sync((lined, plane_one, share_one, share_two, input_grad, sums))
        got = [parts + [lined[2 * i : 2 * i + 2]] for i, parts in enumerate(got)]
        ended = exchange(jnp.concatenate([total([p[1:2] for p in parts]) for parts in got], axis=0), orders[0][4], count)
        plane_two = straight(share_two, plane, count)
        share_one = [p[:4] for p in share_one] + plane_one
        lined = exchange(total([p[2:4] for p in share_one]), orders[0][3], count)
        lined, plane_two, share_two, sums, ended, got = sync((lined, plane_two, share_two, sums, ended, got))
        share_one = [p[:2] for p in share_one] + [lined]
        share_two = [p[:4] for p in share_two] + plane_two
        away = [total([p[1:2] for p in share_one])] + [total([p[i : i + 1] for p in share_two]) for i in (1, 2, 3)]
        away, ended, got = sync((away, ended, got))
        last_one, *last_two = [exchange(a, bit, count) for a, bit in zip(away, (orders[0][4], *line))]
        finals = [total([p[0] for p in parts] + [ended[i]], f32) for i, parts in enumerate(got)]
        hidden_shard = finals[0].transpose(1, 0, 2).reshape(part, hidden_width)
        final_shard = finals[1].reshape(-1, width)
        shards_one = total([p[0] for p in share_one] + [last_one[0]], f32)
        shards_two = total([p[0] for p in share_two] + [p[0] for p in last_two], f32)
    else:
        sums = lax.all_to_all(sums, "dev", 0, 0, tiled=True)
        shards_one, shards_two = scatter_whole(*share_one, count), scatter_whole(*share_two, count)
        finals = [jnp.concatenate(g, axis=0) for g in grads]
        finals[0] = finals[0].transpose(0, 2, 1, 3).reshape(width, hidden_width)
        finals[1] = finals[1].reshape(hidden_width, width)
        hidden_shard, final_shard = [lax.psum_scatter(p.astype(f32), "dev", scatter_dimension=0, tiled=True) for p in finals]
    sums = jnp.sum(sums, axis=0)
    own = [sums[i * part : (i + 1) * part] for i in range(8)]
    own_hidden = sums[8 * part :]
    out_shard = shards_one[:, 3 * cols :]
    qkv_shard = jnp.concatenate([h[:, i * cols : (i + 1) * cols] for i in range(3) for h in (shards_one, shards_two)], axis=1)
    return (
        result,
        input_grad,
        own[0],
        own[1],
        qkv_shard,
        own[2],
        own[3],
        out_shard,
        own[4],
        own[5],
        own[6],
        hidden_shard,
        own_hidden,
        final_shard,
        own[7],
    )


def solution(mesh):
    split = P("dev", None)
    line = P("dev")
    return jax.shard_map(
        per_device,
        mesh=mesh,
        in_specs=(split, P(), line, line, split, line, line, split, line, line, line, split, line, split, line, split),
        out_specs=(split, split, line, line, split, line, line, split, line, line, line, split, line, split, line),
        check_vma=False,
    )
```
